512 devices in a mesh: gx: 32 (over y, x, core), gy: 16 (over z).
Axes of the slice: x: 4, y: 4, z: 16, core: 2. Of those that a mesh axis runs over, the one named last changes fastest.
Arguments:
- channel_activations: bfloat16 [512, 512, 128], P(('gx', 'gy')), may hold values from -6 to 6
- filled_flags: int32 [512, 512], P(('gx', 'gy')), may hold values 0 or 1
- cube_locations: int32 [3, 512], P(None, ('gx', 'gy')), may hold values from 0 to 63, as said below
- holder_flag: int32 [32, 16], P('gx', 'gy'), may hold values from 0 to 1, as said below
- first_kernel_matrices: bfloat16 [27, 128, 128], replicated, may hold values from -0.15625 to 0.15625
- first_offset_vector: float32 [128], replicated, may hold values from -3 to 3
- second_kernel_matrices: bfloat16 [27, 128, 128], replicated, may hold values from -0.15625 to 0.15625
- second_offset_vector: float32 [128], replicated, may hold values from -3 to 3
- reduction_kernel_matrices: bfloat16 [8, 128, 256], replicated, may hold values from -0.25 to 0.25
- reduction_offset_vector: float32 [256], replicated, may hold values from -3 to 3
Outputs:
- coarse: bfloat16 [8192, 64, 256], P(('gx', 'gy'))
The draws below stay inside these ranges and needn't reach their ends.
Inputs may be any that keep to these rules, and one draw needn't show every extreme that they name: `cube_locations`: the device with index i along gx and j along gy holds the single column d = i * 16 + j; its brick lies in that device's coarse brick: X is 2 i or 2 i + 1, Y is 2 j or 2 j + 1, Z is 0 or 1. `holder_flag`: in every index of gx, entry 0 along gy is 0 and entry 15 is 1.
All inputs are finite; a program needn't handle non-finite values. No bound on the sum of `filled_flags` on one device may be relied on, other than what follows from the above.
Results may differ from the reference program's by a relative error of at most 0.005.
Values may be sent and summed in bfloat16 or wider, within the bound.
A program may use at most 64 MiB of HBM per device.

```python
import jax
import jax.numpy as jnp
from jax import lax

CHANNEL_COUNT = 128
COARSE_CHANNEL2 = 256
BRICKS = 1
SXB = 2
SYB = 2
NZB = 2
TOTAL = 512
N_GX = 32
N_GY = 16


def draw_cube_locations(key, part):
    key = jax.random.fold_in(key, 101)

    def single(device_key):
        return jax.random.permutation(device_key, 8)[:BRICKS].astype(jnp.int32)
    octant = jax.vmap(single)(jax.random.split(key, N_GX * N_GY))
    device = jnp.arange(N_GX * N_GY, dtype=jnp.int32)[:, None]
    global_x = device // N_GY * SXB + octant // 4
    global_y = device % N_GY * SYB + octant // 2 % 2
    global_depth_index = octant % 2
    return jnp.stack([global_x, global_y, global_depth_index]).reshape(3, N_GX * N_GY * BRICKS).astype(jnp.int32)


def draw_holder_flag(key, part):
    key = jax.random.fold_in(key, 13)
    bits = jax.random.randint(key, (N_GX, N_GY), 0, 2).astype(jnp.int32)
    bits = bits.at[:, 0].set(0)
    bits = bits.at[:, N_GY - 1].set(1)
    return bits.astype(jnp.int32)


def set_ends(values, rng, smallest, top_value):
    longest = values.shape.index(max(values.shape))
    spots = []
    for shift in (0, 1):
        where = [jax.random.randint(jax.random.fold_in(rng, axis), (), 0, length) for axis, length in enumerate(values.shape)]
        where[longest] = (where[longest] + shift) % values.shape[longest]
        spots.append(tuple(where))
    return values.at[spots[0]].set(smallest).at[spots[1]].set(top_value)


def level_of(rng, shape, cuts, smallest, largest):
    def one(dim, shards_of):
        draws = jax.random.uniform(jax.random.fold_in(jax.random.fold_in(rng, 6), dim), (shards_of,), jnp.float32, smallest / len(cuts), largest / len(cuts))
        return jnp.repeat(jnp.exp(draws), shape[dim] // shards_of).reshape((-1,) + (1,) * (len(shape) - dim - 1))

    loudness = one(*cuts[0])
    for cut in cuts[1:]:
        loudness = loudness * one(*cut)
    return loudness


def gaussian(own_key, dims, width, limit, cuts=(), kind=jnp.bfloat16):
    result = jax.random.normal(own_key, dims, jnp.float32) * width
    if len(cuts) > 0:
        result = level_of(own_key, dims, cuts, -0.22, 0.18) * result
    return jnp.clip(result, min=-limit, max=limit).astype(kind)


def setup_inputs(seed: int = 0) -> dict:
    streams_of = jax.random.split(jax.random.key(seed), 11)
    channel_activations = gaussian(streams_of[0], (TOTAL, 512, CHANNEL_COUNT), 1.0, 6.0, ((0, 512),))
    filled_flags = set_ends((jax.random.randint(streams_of[1], (TOTAL, 512), 0, 2) < 1).astype(jnp.int32), jax.random.fold_in(streams_of[1], 1), 0, 1)
    cube_locations = draw_cube_locations(jax.random.fold_in(streams_of[10], 71), 0)
    holder_flag = draw_holder_flag(jax.random.fold_in(streams_of[10], 71), 0)
    first_kernel_matrices = gaussian(streams_of[4], (27, CHANNEL_COUNT, CHANNEL_COUNT), (27 * CHANNEL_COUNT // 2) ** -0.5, 0.15625)
    first_offset_vector = gaussian(streams_of[5], (CHANNEL_COUNT,), 0.5, 3.0, (), jnp.float32)
    second_kernel_matrices = gaussian(streams_of[6], (27, CHANNEL_COUNT, CHANNEL_COUNT), (27 * CHANNEL_COUNT // 2) ** -0.5, 0.15625)
    second_offset_vector = gaussian(streams_of[7], (CHANNEL_COUNT,), 0.5, 3.0, (), jnp.float32)
    reduction_kernel_matrices = gaussian(streams_of[8], (8, CHANNEL_COUNT, COARSE_CHANNEL2), (4 * CHANNEL_COUNT) ** -0.5, 0.25)
    reduction_offset_vector = gaussian(streams_of[9], (COARSE_CHANNEL2,), 0.5, 3.0, (), jnp.float32)
    return dict(channel_activations=channel_activations, filled_flags=filled_flags, cube_locations=cube_locations, holder_flag=holder_flag, first_kernel_matrices=first_kernel_matrices, first_offset_vector=first_offset_vector, second_kernel_matrices=second_kernel_matrices, second_offset_vector=second_offset_vector, reduction_kernel_matrices=reduction_kernel_matrices, reduction_offset_vector=reduction_offset_vector)


RANGES = ((7, 8, 0, 1), (0, 8, 1, 9), (0, 1, 9, 10))


def neighbour_table(brick_x, brick_y, brick_z, places, missing):
    extent = places.shape
    columns = []
    for p in range(3):
        for q in range(3):
            for r in range(3):
                near_x = brick_x + p - 1
                near_y = brick_y + q - 1
                near_z = brick_z + r - 1
                inside = (near_x >= 0) & (near_x < extent[0]) & (near_y >= 0) & (near_y < extent[1]) & (near_z >= 0) & (near_z < extent[2])
                found = places[jnp.clip(near_x, 0, extent[0] - 1), jnp.clip(near_y, 0, extent[1] - 1), jnp.clip(near_z, 0, extent[2] - 1)]
                columns.append(jnp.where(inside, found, missing))
    return jnp.stack(columns, axis=1).astype(jnp.int32)


def gather_pieces(pool, table):
    count = table.shape[0]
    padded = jnp.zeros((count, 10, 10, 10, pool.shape[-1]), pool.dtype)
    for p in range(3):
        for q in range(3):
            for r in range(3):
                first, second, third = RANGES[p], RANGES[q], RANGES[r]
                bricks = jnp.take(pool, table[:, (p * 3 + q) * 3 + r], axis=0)
                layer = bricks[:, first[0]:first[1], second[0]:second[1], third[0]:third[1]]
                padded = padded.at[:, first[2]:first[3], second[2]:second[3], third[2]:third[3]].set(layer)
    return padded


def convolve(padded, weight):
    count, lateral_extent = padded.shape[0], padded.shape[-1]
    total = jnp.zeros((count * 512, weight.shape[-1]), jnp.float32)
    for p in range(3):
        for q in range(3):
            for r in range(3):
                window = padded[:, p:p + 8, q:q + 8, r:r + 8].reshape(count * 512, lateral_extent)
                total = total + jnp.dot(window, weight[(p * 3 + q) * 3 + r], preferred_element_type=jnp.float32)
    return total


def halving_reduction(skip_connection_unit, filled_flags, reduction_kernel_matrices, reduction_offset_vector):
    count, lateral_extent = skip_connection_unit.shape[0], skip_connection_unit.shape[-1]
    voxel_values = skip_connection_unit.reshape(count, 4, 2, 4, 2, 4, 2, lateral_extent).transpose(0, 1, 3, 5, 2, 4, 6, 7).reshape(count * 64, 8 * lateral_extent)
    accumulated_result = jnp.dot(voxel_values, reduction_kernel_matrices.reshape(8 * lateral_extent, -1), preferred_element_type=jnp.float32) + reduction_offset_vector
    occupied = filled_flags.reshape(count, 4, 2, 4, 2, 4, 2).max(axis=(2, 4, 6)).reshape(count * 64, 1)
    return jnp.where(occupied > 0, accumulated_result, 0.0).astype(jnp.bfloat16).reshape(count, 64, -1)


def reference(channel_activations, filled_flags, cube_locations, holder_flag, first_kernel_matrices, first_offset_vector, second_kernel_matrices, second_offset_vector, reduction_kernel_matrices, reduction_offset_vector):
    total = channel_activations.shape[0]
    flat = cube_locations
    grid = jnp.full((SXB * N_GX, SYB * N_GY, NZB), total, jnp.int32)
    grid = grid.at[flat[0], flat[1], flat[2]].set(jnp.arange(total, dtype=jnp.int32))
    table = neighbour_table(flat[0], flat[1], flat[2], grid, total)
    live = filled_flags.astype(jnp.float32)[:, :, None]
    start = (channel_activations.astype(jnp.float32) * live).astype(jnp.bfloat16)

    def layer(values, weight):
        pool = jnp.concatenate([values.reshape(total, 8, 8, 8, CHANNEL_COUNT), jnp.zeros((1, 8, 8, 8, CHANNEL_COUNT), values.dtype)])

        def one_block(rows):
            return convolve(gather_pieces(pool, rows), weight)

        return lax.map(one_block, table.reshape(N_GX, total // N_GX, 27)).reshape(total, 512, -1)

    hidden = (live * jax.nn.silu(layer(start, first_kernel_matrices) + first_offset_vector)).astype(jnp.bfloat16)
    skip_connection_unit = (live * jax.nn.silu(start.astype(jnp.float32) + layer(hidden, second_kernel_matrices) + second_offset_vector)).astype(jnp.bfloat16)
    cube_sections = halving_reduction(skip_connection_unit, filled_flags, reduction_kernel_matrices, reduction_offset_vector)
    octant = (flat[0] % 2) * 4 + (flat[1] % 2) * 2 + flat[2] % 2
    device = jnp.arange(total, dtype=jnp.int32) // BRICKS
    row_index = device // N_GY
    col_index = device % N_GY
    gives = holder_flag.reshape(-1)[device]
    target_device = row_index * N_GY + (col_index + gives) % N_GY
    target = (target_device * 2 + gives) * 8 + octant
    return jnp.zeros((16 * N_GX * N_GY, 64, COARSE_CHANNEL2), jnp.bfloat16).at[target.astype(jnp.int32)].set(cube_sections)
```

```python
import functools

import jax
import jax.numpy as jnp
from jax import lax
from jax.experimental import pallas as pl
from jax.experimental.pallas import tpu as pltpu
from jax.sharding import PartitionSpec as P

MESH = pl.DeviceIdType.MESH
F32 = jnp.float32
BF16 = jnp.bfloat16
C = 128
DEEP = 16
SIDE_ROWS = 208
CORNER_ROWS = 48


def silu(s):
    return 0.5 * s * (1.0 + jnp.tanh(0.5 * s))


def number(condition):
    return jnp.where(condition, 1.0, 0.0).astype(F32)


def row_shift(value, by):
    return pltpu.roll(value, by % value.shape[0], 0)


def along_z(products):
    rows = products.shape[0]
    z = lax.broadcasted_iota(jnp.int32, (rows, C), 0) % DEEP
    low, mid, high = (products[:, k * C : (k + 1) * C] for k in range(3))
    return (
        mid
        + jnp.where(z == 0, 0.0, row_shift(low, 1))
        + jnp.where(z == DEEP - 1, 0.0, row_shift(high, -1))
    )


def convolve(field, x0, nx, y0, ny, weight):
    taps = [
        field[pl.ds(x0 + p, nx), pl.ds(y0 + q, ny)].reshape(nx * ny * DEEP, C)
        for p in range(3)
        for q in range(3)
    ]
    stacked = jnp.concatenate(taps, axis=1)
    products = jnp.dot(stacked, weight[...].reshape(9 * C, 3 * C), preferred_element_type=F32)
    return along_z(products)


def kernel(
    n_gx,
    n_gy,
    location,
    holder,
    flags,
    first_bias,
    second_bias,
    last_bias,
    features,
    first_weight,
    second_weight,
    last_weight,
    mine,
    arrived,
    code_out,
    cells,
    w1,
    w2,
    w3,
    s8,
    m8,
    field,
    full,
    hidden,
    block,
    occupied,
    side_out,
    side_in,
    corner_out,
    corner_in,
    local_sem,
    side_send,
    side_recv,
    corner_send,
    corner_recv,
    last_send,
    last_recv,
):
    i = lax.axis_index("gx")
    j = lax.axis_index("gy")
    left, right = lax.rem(i + n_gx - 1, n_gx), lax.rem(i + 1, n_gx)
    below, above = lax.rem(j + n_gy - 1, n_gy), lax.rem(j + 1, n_gy)
    sides = ((left, j), (right, j), (i, below), (i, above))
    corners = ((left, below), (left, above), (right, below), (right, above))

    barrier = pltpu.get_barrier_semaphore()
    for device in sides + corners:
        pl.semaphore_signal(barrier, inc=1, device_id=device, device_id_type=MESH)

    copies = [pltpu.make_async_copy(features.at[0], cells, local_sem.at[0])]
    for k in range(3):
        copies.append(
            pltpu.make_async_copy(
                first_weight.at[:, k], w1.at[:, :, pl.ds(k * C, C)], local_sem.at[1 + k]
            )
        )
    for k in range(3):
        copies.append(
            pltpu.make_async_copy(
                second_weight.at[:, k], w2.at[:, :, pl.ds(k * C, C)], local_sem.at[4 + k]
            )
        )
    for k in range(2):
        copies.append(
            pltpu.make_async_copy(
                last_weight.at[:, k], w3.at[:, :, pl.ds(k * 2 * C, 2 * C)], local_sem.at[7 + k]
            )
        )
    for copy in copies:
        copy.start()

    ox = lax.rem(location[0, 0], 2)
    oy = lax.rem(location[1, 0], 2)
    oz = lax.rem(location[2, 0], 2)
    oxf, oyf, ozf = (o.astype(F32) for o in (ox, oy, oz))
    code = (ox * 4 + oy * 2 + oz + 8 * holder[0, 0]).astype(F32)

    r = lax.broadcasted_iota(jnp.int32, (C, C), 0)
    c = lax.broadcasted_iota(jnp.int32, (C, C), 1)
    ones = jnp.ones((C, C), BF16)
    for k in range(4):
        line = jnp.broadcast_to(flags[:, k * C : (k + 1) * C].astype(F32), (C, C))
        diagonal = jnp.where(r == c, line, 0.0).astype(BF16)
        m8[pl.ds(2 * k, 2)] = jnp.dot(diagonal, ones, preferred_element_type=F32).reshape(
            2, 8, 8, C
        )

    copies[0].wait()
    s8[...] = cells[...].astype(F32).reshape(8, 8, 8, C) * m8[...]

    tag = jnp.full((16, C), code, F32).astype(BF16)
    for k, x in ((0, 0), (1, 6)):
        side_out[k, 0:128] = s8[x : x + 2].reshape(128, C).astype(BF16)
        side_out[k, 128:192] = m8[0 if k == 0 else 7].reshape(64, C).astype(BF16)
        side_out[k, 192:208] = tag
    for k, y in ((2, 0), (3, 6)):
        side_out[k, 0:128] = s8[:, y : y + 2].reshape(128, C).astype(BF16)
        side_out[k, 128:192] = m8[:, 0 if k == 2 else 7].reshape(64, C).astype(BF16)
        side_out[k, 192:208] = tag
    for a in range(2):
        for b in range(2):
            near = m8[7 * a, 7 * b]
            corner_out[2 * a + b, 0:32] = (
                s8[6 * a : 6 * a + 2, 6 * b : 6 * b + 2].reshape(32, C).astype(BF16)
            )
            corner_out[2 * a + b, 32:48] = jnp.concatenate(
                [near, jnp.full((8, C), code, F32)], axis=0
            ).astype(BF16)

    pl.semaphore_wait(barrier, 8)
    sent = []
    for k, device in enumerate(corners):
        sent.append(
            pltpu.make_async_remote_copy(
                src_ref=corner_out.at[k],
                dst_ref=corner_in.at[3 - k],
                send_sem=corner_send.at[k],
                recv_sem=corner_recv.at[3 - k],
                device_id=device,
                device_id_type=MESH,
            )
        )
    for k, device in enumerate(sides):
        sent.append(
            pltpu.make_async_remote_copy(
                src_ref=side_out.at[k],
                dst_ref=side_in.at[k ^ 1],
                send_sem=side_send.at[k],
                recv_sem=side_recv.at[k ^ 1],
                device_id=device,
                device_id_type=MESH,
            )
        )
    for copy in sent:
        copy.start()

    start16 = jnp.concatenate([s8[...] * (1.0 - ozf), s8[...] * ozf], axis=2).astype(BF16)
    flags16 = jnp.concatenate([m8[...] * (1.0 - ozf), m8[...] * ozf], axis=2).astype(BF16)
    field[2:10, 2:10] = start16
    full[1:9, 1:9] = flags16
    occupied[...] = flags16.reshape(4, 2, 4, 2, DEEP, C)

    bias1 = first_bias[...]
    bias2 = second_bias[...]

    def first(x0, nx, y0, ny):
        s = convolve(field, x0, nx, y0, ny, w1) + bias1
        flag = full[pl.ds(x0, nx), pl.ds(y0, ny)].reshape(nx * ny * DEEP, C).astype(F32)
        hidden[pl.ds(x0, nx), pl.ds(y0, ny)] = (
            (flag * silu(s)).astype(BF16).reshape(nx, ny, DEEP, C)
        )

    for copy in copies[1:4]:
        copy.wait()

    def inner(t, carry):
        first(2 + t, 1, 2, 6)
        return carry

    lax.fori_loop(0, 6, inner, 0)

    for copy in sent:
        copy.wait_recv()

    def decode(tag):
        nx = number(tag >= 4.0)
        rest = tag - 4.0 * nx
        ny = number(rest >= 2.0)
        nz = rest - 2.0 * ny
        return nx, ny, nz

    def placed(value, gate, nz):
        return jnp.concatenate([value * (gate * (1.0 - nz)), value * (gate * nz)], axis=-2)

    inside = (number(i > 0), number(i < n_gx - 1), number(j > 0), number(j < n_gy - 1))
    facing = (1.0 - oxf, oxf, 1.0 - oyf, oyf)
    lower = [None] * 4
    upper = [None] * 4
    for k in range(4):
        got = side_in[k, 192:208].astype(F32)[0:8]
        got = got - 8.0 * number(got >= 8.0)
        nx, ny, nz = decode(got)
        across, beside, own = (nx, ny, oyf) if k < 2 else (ny, nx, oxf)
        meets = across if k % 2 == 0 else 1.0 - across
        gate = meets * (inside[k] * facing[k])
        same = gate * (beside * own + (1.0 - beside) * (1.0 - own))
        minus = gate * ((1.0 - beside) * own)
        plus = gate * (beside * (1.0 - own))
        flag = side_in[k, 128:192].astype(F32).reshape(8, 8, C)
        if k < 2:
            value = side_in[k, 0:128].astype(F32).reshape(2, 8, 8, C)
            x = 0 if k == 0 else 10
            field[x : x + 2, 2:10] = placed(value, same, nz).astype(BF16)
            full[0 if k == 0 else 9, 1:9] = placed(flag, same, nz).astype(BF16)
            lower[k] = (placed(value[:, 6:8], minus, nz), placed(flag[7], minus, nz))
            upper[k] = (placed(value[:, 0:2], plus, nz), placed(flag[0], plus, nz))
        else:
            value = side_in[k, 0:128].astype(F32).reshape(8, 2, 8, C)
            y = 0 if k == 2 else 10
            field[2:10, y : y + 2] = placed(value, same, nz).astype(BF16)
            full[1:9, 0 if k == 2 else 9] = placed(flag, same, nz).astype(BF16)
            lower[k] = (placed(value[6:8], minus, nz), placed(flag[7], minus, nz))
            upper[k] = (placed(value[0:2], plus, nz), placed(flag[0], plus, nz))
    for a in range(2):
        for b in range(2):
            k = 2 * a + b
            tail = corner_in[k, 32:48].astype(F32)
            got = tail[8:16]
            got = got - 8.0 * number(got >= 8.0)
            nx, ny, nz = decode(got)
            gate = (nx if a == 0 else 1.0 - nx) * (ny if b == 0 else 1.0 - ny)
            gate = gate * (inside[a] * inside[2 + b] * facing[a] * facing[2 + b])
            value = corner_in[k, 0:32].astype(F32).reshape(2, 2, 8, C)
            from_x = (lower if b == 0 else upper)[a]
            from_y = (lower if a == 0 else upper)[2 + b]
            x, y = 10 * a, 10 * b
            field[x : x + 2, y : y + 2] = (
                placed(value, gate, nz) + from_x[0] + from_y[0]
            ).astype(BF16)
            full[9 * a, 9 * b] = (placed(tail[0:8], gate, nz) + from_x[1] + from_y[1]).astype(BF16)

    code_out[...] = side_in[2, 192:208].astype(F32)[0:8]

    def outer_x(t, carry):
        first(t // 2 * 8 + t % 2, 1, 0, 10)
        return carry

    def outer_y(t, carry):
        first(2, 6, t // 2 * 8 + t % 2, 1)
        return carry

    lax.fori_loop(0, 4, outer_x, 0)
    lax.fori_loop(0, 4, outer_y, 0)

    for copy in copies[4:]:
        copy.wait()

    def second(t, carry):
        s = convolve(hidden, t, 1, 0, 8, w2) + bias2
        s = s + field[pl.ds(t + 2, 1), 2:10].reshape(8 * DEEP, C).astype(F32)
        flag = full[pl.ds(t + 1, 1), 1:9].reshape(8 * DEEP, C).astype(F32)
        block[t // 2, t % 2] = (flag * silu(s)).astype(BF16).reshape(4, 2, DEEP, C)
        return carry

    lax.fori_loop(0, 8, second, 0)

    rows = 16 * DEEP
    stacked = jnp.concatenate(
        [block[:, a, :, b].reshape(rows, C) for a in range(2) for b in range(2)], axis=1
    )
    products = jnp.dot(stacked, w3[...].reshape(4 * C, 4 * C), preferred_element_type=F32)
    total = products[:, 0 : 2 * C] + row_shift(products[:, 2 * C :], -1) + last_bias[...]
    count = sum(
        occupied[:, a, :, b].reshape(rows, C).astype(F32) for a in range(2) for b in range(2)
    )
    count = count + row_shift(count, -1)
    total = jnp.where(jnp.concatenate([count, count], axis=1) > 0.5, total, 0.0).astype(BF16)
    pr = lax.broadcasted_iota(jnp.int32, (64, rows), 0)
    pc = lax.broadcasted_iota(jnp.int32, (64, rows), 1)
    pick = jnp.where(pc == pr // 4 * DEEP + pr % 4 * 2 + 8 * oz, 1.0, 0.0).astype(BF16)
    mine[...] = jnp.dot(pick, total, preferred_element_type=F32).astype(BF16)

    last = pltpu.make_async_remote_copy(
        src_ref=mine,
        dst_ref=arrived,
        send_sem=last_send,
        recv_sem=last_recv,
        device_id=(i, above),
        device_id_type=MESH,
    )
    last.start()
    for copy in sent:
        copy.wait_send()
    last.wait()


def per_device(
    n_gx,
    n_gy,
    channel_activations,
    filled_flags,
    cube_locations,
    holder_flag,
    first_kernel_matrices,
    first_offset_vector,
    second_kernel_matrices,
    second_offset_vector,
    reduction_kernel_matrices,
    reduction_offset_vector,
):
    vmem = pl.BlockSpec(memory_space=pltpu.VMEM)
    smem = pl.BlockSpec(memory_space=pltpu.SMEM)
    anywhere = pl.BlockSpec(memory_space=pl.ANY)
    dma = pltpu.SemaphoreType.DMA
    mine, arrived, code = pl.pallas_call(
        functools.partial(kernel, n_gx, n_gy),
        out_shape=(
            jax.ShapeDtypeStruct((64, 256), BF16),
            jax.ShapeDtypeStruct((64, 256), BF16),
            jax.ShapeDtypeStruct((8, C), F32),
        ),
        in_specs=[smem, smem, vmem, vmem, vmem, vmem, anywhere, anywhere, anywhere, anywhere],
        out_specs=(vmem, vmem, vmem),
        scratch_shapes=[
            pltpu.VMEM((512, C), BF16),
            pltpu.VMEM((9, C, 3 * C), BF16),
            pltpu.VMEM((9, C, 3 * C), BF16),
            pltpu.VMEM((4, C, 4 * C), BF16),
            pltpu.VMEM((8, 8, 8, C), F32),
            pltpu.VMEM((8, 8, 8, C), F32),
            pltpu.VMEM((12, 12, DEEP, C), BF16),
            pltpu.VMEM((10, 10, DEEP, C), BF16),
            pltpu.VMEM((10, 10, DEEP, C), BF16),
            pltpu.VMEM((4, 2, 4, 2, DEEP, C), BF16),
            pltpu.VMEM((4, 2, 4, 2, DEEP, C), BF16),
            pltpu.VMEM((4, SIDE_ROWS, C), BF16),
            pltpu.VMEM((4, SIDE_ROWS, C), BF16),
            pltpu.VMEM((4, CORNER_ROWS, C), BF16),
            pltpu.VMEM((4, CORNER_ROWS, C), BF16),
            dma((9,)),
            dma((4,)),
            dma((4,)),
            dma((4,)),
            dma((4,)),
            dma,
            dma,
        ],
        compiler_params=pltpu.CompilerParams(
            collective_id=0, has_side_effects=True, vmem_limit_bytes=48 * 1024 * 1024
        ),
    )(
        cube_locations,
        holder_flag,
        filled_flags,
        first_offset_vector.reshape(1, C),
        second_offset_vector.reshape(1, C),
        reduction_offset_vector.reshape(1, 2 * C),
        channel_activations,
        first_kernel_matrices.reshape(9, 3, C, C),
        second_kernel_matrices.reshape(9, 3, C, C),
        reduction_kernel_matrices.reshape(4, 2, C, 2 * C),
    )
    octant = cube_locations[0, 0] % 2 * 4 + cube_locations[1, 0] % 2 * 2 + cube_locations[2, 0] % 2
    there = code[0, 0].astype(jnp.int32)
    row = jnp.arange(16, dtype=jnp.int32)[:, None, None]
    own_row = jnp.where(holder_flag[0, 0] == 0, octant, -1)
    got_row = jnp.where(there >= 8, there, -1)
    return jnp.where(row == own_row, mine[None], jnp.where(row == got_row, arrived[None], 0)).astype(
        BF16
    )


def solution(mesh):
    return jax.shard_map(
        functools.partial(per_device, mesh.shape["gx"], mesh.shape["gy"]),
        mesh=mesh,
        in_specs=(
            P(("gx", "gy"), None, None),
            P(("gx", "gy"), None),
            P(None, ("gx", "gy")),
            P("gx", "gy"),
            P(),
            P(),
            P(),
            P(),
            P(),
            P(),
        ),
        out_specs=P(("gx", "gy"), None, None),
        check_vma=False,
    )
```

```python
import functools

import jax
import jax.numpy as jnp
from jax import lax
from jax.experimental import pallas as pl
from jax.experimental.pallas import tpu as pltpu
from jax.sharding import PartitionSpec as P

MESH = pl.DeviceIdType.MESH
F32 = jnp.float32
BF16 = jnp.bfloat16
C = 128
DEEP = 16
SIDE_ROWS = 208
CORNER_ROWS = 48


def silu(s):
    return 0.5 * s * (1.0 + jnp.tanh(0.5 * s))


def number(condition):
    return jnp.where(condition, 1.0, 0.0).astype(F32)


def along_z(products, deep):
    count = products.shape[0] // deep
    low, mid, high = (products[:, k * C : (k + 1) * C].reshape(count, deep, C) for k in range(3))
    z = lax.broadcasted_iota(jnp.int32, (count, deep, C), 1)
    low = jnp.where(z == 0, 0.0, pltpu.roll(low, 1, 1))
    high = jnp.where(z == deep - 1, 0.0, pltpu.roll(high, deep - 1, 1))
    return mid + low + high


def pack(target, value):
    zero = jnp.zeros((1, 8, 8, C), F32)
    upper = jnp.concatenate([zero, value[0:5]], axis=0)
    lower = jnp.concatenate([value[3:8], zero], axis=0)
    target[:, 1:9] = jnp.concatenate([upper, lower], axis=2).astype(BF16)


def own_conv(tiles, weight):
    taps = [tiles[p : p + 4, q : q + 8].reshape(512, C) for p in range(3) for q in range(3)]
    products = jnp.dot(
        jnp.concatenate(taps, axis=1),
        weight[...].reshape(9 * C, 3 * C),
        preferred_element_type=F32,
    )
    total = along_z(products, 8).reshape(4, 8, 2, 8, C)
    return jnp.concatenate([total[:, :, 0], total[:, :, 1]], axis=0)


def edge_conv(line, weight, ozf):
    taps = [line[k : k + 8].reshape(8 * DEEP, C) for k in range(3)]
    products = jnp.dot(jnp.concatenate(taps, axis=1), weight, preferred_element_type=F32)
    total = along_z(products, DEEP)
    return total[:, 0:8] * (1.0 - ozf) + total[:, 8:16] * ozf


def kernel(
    n_gx,
    n_gy,
    location_at,
    holder,
    flags_at,
    first_bias_at,
    second_bias_at,
    last_bias_at,
    features,
    first_weight,
    second_weight,
    last_weight,
    mine,
    arrived,
    codes,
    pieces,
    own_codes,
    location,
    flags,
    first_bias,
    second_bias,
    last_bias,
    cells,
    w1,
    w2,
    w3,
    s8,
    m8,
    total8,
    tiles,
    field,
    full,
    w1x,
    w1y,
    w2x,
    w2y,
    side_out,
    side_in,
    corner_out,
    corner_in,
    small_sem,
    local_sem,
    side_send,
    side_recv,
    corner_send,
    corner_recv,
    last_send,
    last_recv,
    result_sem,
):
    i = lax.axis_index("gx")
    j = lax.axis_index("gy")
    left, right = lax.rem(i + n_gx - 1, n_gx), lax.rem(i + 1, n_gx)
    below, above = lax.rem(j + n_gy - 1, n_gy), lax.rem(j + 1, n_gy)
    sides = ((left, j), (right, j), (i, below), (i, above))
    corners = ((left, below), (left, above), (right, below), (right, above))

    barrier = pltpu.get_barrier_semaphore()
    for device in sides + corners:
        pl.semaphore_signal(barrier, inc=1, device_id=device, device_id_type=MESH)

    copies = [pltpu.make_async_copy(features.at[0], cells, local_sem.at[0])]
    for k in range(3):
        copies.append(
            pltpu.make_async_copy(
                first_weight.at[:, k], w1.at[:, :, pl.ds(k * C, C)], local_sem.at[1 + k]
            )
        )
    for k in range(3):
        copies.append(
            pltpu.make_async_copy(
                second_weight.at[:, k], w2.at[:, :, pl.ds(k * C, C)], local_sem.at[4 + k]
            )
        )
    for k in range(2):
        copies.append(
            pltpu.make_async_copy(
                last_weight.at[:, k], w3.at[:, :, pl.ds(k * 2 * C, 2 * C)], local_sem.at[7 + k]
            )
        )
    small = [
        pltpu.make_async_copy(source, target, small_sem.at[k])
        for k, (source, target) in enumerate(
            (
                (location_at, location),
                (flags_at, flags),
                (first_bias_at, first_bias),
                (second_bias_at, second_bias),
                (last_bias_at, last_bias),
            )
        )
    ]
    for copy in small + copies:
        copy.start()
    for copy in small[0:2]:
        copy.wait()

    octant = (location[...] & 1).astype(F32)
    oxf, oyf, ozf = (jnp.broadcast_to(octant[:, k : k + 1], (8, C)) for k in range(3))
    code = oxf * 4.0 + oyf * 2.0 + ozf + 8.0 * holder[0, 0].astype(F32)
    own_codes[0:8] = code

    r = lax.broadcasted_iota(jnp.int32, (C, C), 0)
    c = lax.broadcasted_iota(jnp.int32, (C, C), 1)
    ones = jnp.ones((C, C), BF16)
    for k in range(4):
        line = jnp.broadcast_to(flags[:, k * C : (k + 1) * C].astype(F32), (C, C))
        diagonal = jnp.where(r == c, line, 0.0).astype(BF16)
        m8[pl.ds(2 * k, 2)] = jnp.dot(diagonal, ones, preferred_element_type=F32).reshape(
            2, 8, 8, C
        )

    copies[0].wait()
    s8[...] = cells[...].astype(F32).reshape(8, 8, 8, C) * m8[...]

    tag = jnp.concatenate([code, code], axis=0).astype(BF16)
    for k, x in ((0, 0), (1, 6)):
        side_out[k, 0:128] = s8[x : x + 2].reshape(128, C).astype(BF16)
        side_out[k, 128:192] = m8[0 if k == 0 else 7].reshape(64, C).astype(BF16)
        side_out[k, 192:208] = tag
    for k, y in ((2, 0), (3, 6)):
        side_out[k, 0:128] = s8[:, y : y + 2].reshape(128, C).astype(BF16)
        side_out[k, 128:192] = m8[:, 0 if k == 2 else 7].reshape(64, C).astype(BF16)
        side_out[k, 192:208] = tag
    for a in range(2):
        for b in range(2):
            near = m8[7 * a, 7 * b]
            corner_out[2 * a + b, 0:32] = (
                s8[6 * a : 6 * a + 2, 6 * b : 6 * b + 2].reshape(32, C).astype(BF16)
            )
            corner_out[2 * a + b, 32:48] = jnp.concatenate(
                [near, code], axis=0
            ).astype(BF16)

    pl.semaphore_wait(barrier, 8)
    sent = []
    for k, device in enumerate(corners):
        sent.append(
            pltpu.make_async_remote_copy(
                src_ref=corner_out.at[k],
                dst_ref=corner_in.at[3 - k],
                send_sem=corner_send.at[k],
                recv_sem=corner_recv.at[3 - k],
                device_id=device,
                device_id_type=MESH,
            )
        )
    for k, device in enumerate(sides):
        sent.append(
            pltpu.make_async_remote_copy(
                src_ref=side_out.at[k],
                dst_ref=side_in.at[k ^ 1],
                send_sem=side_send.at[k],
                recv_sem=side_recv.at[k ^ 1],
                device_id=device,
                device_id_type=MESH,
            )
        )
    for copy in sent:
        copy.start()

    ox2, oy2 = (jnp.concatenate([o, o], axis=0).astype(BF16) for o in (oxf, oyf))
    not_ox2, not_oy2 = (
        jnp.concatenate([1.0 - o, 1.0 - o], axis=0).astype(BF16) for o in (oxf, oyf)
    )
    field[2:10, 2:10] = jnp.concatenate([s8[...] * (1.0 - ozf), s8[...] * ozf], axis=2).astype(BF16)
    full[1:9, 1:9] = jnp.concatenate([m8[...] * (1.0 - ozf), m8[...] * ozf], axis=2).astype(BF16)
    tiles[:, 0] = jnp.zeros((6, DEEP, C), BF16)
    tiles[:, 9] = jnp.zeros((6, DEEP, C), BF16)
    pack(tiles, s8[...])

    def edge_weights(weight, along_x, along_y):
        for k in range(3):
            for r in range(3):
                rows, columns = slice(k * C, (k + 1) * C), slice(r * C, (r + 1) * C)
                for target, a, b, side, other in (
                    (along_x, k, 6 + k, not_ox2, ox2),
                    (along_y, 3 * k, 3 * k + 2, not_oy2, oy2),
                ):
                    first = weight[a, :, columns].reshape(8, DEEP, C) * side
                    second = weight[b, :, columns].reshape(8, DEEP, C) * other
                    target[rows, columns] = (first + second).reshape(C, C)

    for copy in small[2:]:
        copy.wait()
    bias1 = first_bias[...]
    bias2 = second_bias[...]
    for copy in copies[1:4]:
        copy.wait()
    total8[...] = own_conv(tiles, w1) + bias1
    edge_weights(w1, w1x, w1y)
    for copy in copies[4:]:
        copy.wait()
    edge_weights(w2, w2x, w2y)

    def corners_of(value):
        halves = value.reshape(4, 2, 4, 2, 8, C)
        return [halves[:, a, :, b].reshape(C, C) for a in range(2) for b in range(2)]

    def next_row(value):
        return pltpu.roll(value, C - 1, 0)

    count = sum(corners_of(m8[...]))
    count = count + next_row(count)
    count = jnp.concatenate([count, count], axis=1)

    for copy in sent:
        copy.wait_recv()

    def decode(tag):
        nx = number(tag >= 4.0)
        rest = tag - 4.0 * nx
        ny = number(rest >= 2.0)
        nz = rest - 2.0 * ny
        return nx, ny, nz

    def placed(value, gate, nz):
        return jnp.concatenate([value * (gate * (1.0 - nz)), value * (gate * nz)], axis=-2)

    inside = (number(i > 0), number(i < n_gx - 1), number(j > 0), number(j < n_gy - 1))
    facing = (1.0 - oxf, oxf, 1.0 - oyf, oyf)
    lower = [None] * 4
    upper = [None] * 4
    for k in range(4):
        got = side_in[k, 192:208].astype(F32)[0:8]
        got = got - 8.0 * number(got >= 8.0)
        nx, ny, nz = decode(got)
        across, beside, own = (nx, ny, oyf) if k < 2 else (ny, nx, oxf)
        meets = across if k % 2 == 0 else 1.0 - across
        gate = meets * (inside[k] * facing[k])
        same = gate * (beside * own + (1.0 - beside) * (1.0 - own))
        minus = gate * ((1.0 - beside) * own)
        plus = gate * (beside * (1.0 - own))
        flag = side_in[k, 128:192].astype(F32).reshape(8, 8, C)
        if k < 2:
            value = side_in[k, 0:128].astype(F32).reshape(2, 8, 8, C)
            x = 0 if k == 0 else 10
            field[x : x + 2, 2:10] = placed(value, same, nz).astype(BF16)
            full[0 if k == 0 else 9, 1:9] = placed(flag, same, nz).astype(BF16)
            lower[k] = (placed(value[:, 6:8], minus, nz), placed(flag[7], minus, nz))
            upper[k] = (placed(value[:, 0:2], plus, nz), placed(flag[0], plus, nz))
        else:
            value = side_in[k, 0:128].astype(F32).reshape(8, 2, 8, C)
            y = 0 if k == 2 else 10
            field[2:10, y : y + 2] = placed(value, same, nz).astype(BF16)
            full[1:9, 0 if k == 2 else 9] = placed(flag, same, nz).astype(BF16)
            lower[k] = (placed(value[6:8], minus, nz), placed(flag[7], minus, nz))
            upper[k] = (placed(value[0:2], plus, nz), placed(flag[0], plus, nz))
    for a in range(2):
        for b in range(2):
            k = 2 * a + b
            tail = corner_in[k, 32:48].astype(F32)
            got = tail[8:16]
            got = got - 8.0 * number(got >= 8.0)
            nx, ny, nz = decode(got)
            gate = (nx if a == 0 else 1.0 - nx) * (ny if b == 0 else 1.0 - ny)
            gate = gate * (inside[a] * inside[2 + b] * facing[a] * facing[2 + b])
            value = corner_in[k, 0:32].astype(F32).reshape(2, 2, 8, C)
            from_x = (lower if b == 0 else upper)[a]
            from_y = (lower if a == 0 else upper)[2 + b]
            x, y = 10 * a, 10 * b
            field[x : x + 2, y : y + 2] = (
                placed(value, gate, nz) + from_x[0] + from_y[0]
            ).astype(BF16)
            full[9 * a, 9 * b] = (placed(tail[0:8], gate, nz) + from_x[1] + from_y[1]).astype(BF16)

    own_codes[8:16] = side_in[2, 192:208].astype(F32)[0:8]

    beside_x = field[0:3] * not_ox2 + field[9:12] * ox2
    beside_y = field[:, 0:3] * not_oy2 + field[:, 9:12] * oy2
    stacked = jnp.concatenate(
        [
            jnp.concatenate(
                [
                    beside_x[p, q : q + 10].reshape(10 * DEEP, C),
                    beside_y[p : p + 10, q].reshape(10 * DEEP, C),
                ],
                axis=0,
            )
            for p in range(3)
            for q in range(3)
        ],
        axis=1,
    )
    products = jnp.dot(stacked, w1[...].reshape(9 * C, 3 * C), preferred_element_type=F32)
    flag = jnp.concatenate(
        [full[0] * not_ox2 + full[9] * ox2, full[:, 0] * not_oy2 + full[:, 9] * oy2], axis=0
    ).astype(F32)
    line = (flag * silu(along_z(products, DEEP) + bias1[None])).astype(BF16)

    def without_corner(line):
        return jnp.concatenate([line[0:1] * ox2, line[1:9], line[9:10] * not_ox2], axis=0)

    def add_edges(line_x, line_y, weight_x, weight_y):
        from_x = edge_conv(line_x, weight_x[...], ozf)
        from_y = edge_conv(without_corner(line_y), weight_y[...], ozf)
        total8[0] = total8[0] + from_x * (1.0 - oxf)
        total8[7] = total8[7] + from_x * oxf
        total8[:, 0] = total8[:, 0] + from_y * (1.0 - oyf)
        total8[:, 7] = total8[:, 7] + from_y * oyf

    add_edges(beside_x[1, 1:11], beside_y[1:11, 1], w1x, w1y)
    pack(tiles, m8[...] * silu(total8[...]))

    total8[...] = own_conv(tiles, w2) + bias2 + s8[...]
    add_edges(line[0:10], line[10:20], w2x, w2y)
    block = m8[...] * silu(total8[...])

    stacked = jnp.concatenate(corners_of(block), axis=1).astype(BF16)
    products = jnp.dot(stacked, w3[...].reshape(4 * C, 4 * C), preferred_element_type=F32)
    total = products[:, 0 : 2 * C] + next_row(products[:, 2 * C :]) + last_bias[...]
    total = jnp.where(count > 0.5, total, 0.0).astype(BF16)
    pr = lax.broadcasted_iota(jnp.int32, (64, C), 0)
    pc = lax.broadcasted_iota(jnp.int32, (64, C), 1)
    pick = jnp.where(pc == 2 * pr, 1.0, 0.0).astype(BF16)
    pieces[...] = jnp.dot(pick, total, preferred_element_type=F32).astype(BF16)

    last = pltpu.make_async_remote_copy(
        src_ref=pieces,
        dst_ref=arrived,
        send_sem=last_send,
        recv_sem=last_recv,
        device_id=(i, above),
        device_id_type=MESH,
    )
    last.start()
    results = [
        pltpu.make_async_copy(pieces, mine, result_sem.at[0]),
        pltpu.make_async_copy(own_codes, codes, result_sem.at[1]),
    ]
    for copy in results:
        copy.start()
    for copy in sent:
        copy.wait_send()
    for copy in results:
        copy.wait()
    last.wait()


def place(mine_at, arrived_at, codes_at, out, mine, arrived, codes, sem):
    pairs = ((codes_at, codes), (mine_at, mine), (arrived_at, arrived))
    copies = [pltpu.make_async_copy(a, b, sem.at[k]) for k, (a, b) in enumerate(pairs)]
    for copy in copies:
        copy.start()
    for copy in copies:
        copy.wait()
    for row in range(16):
        piece = mine if row < 8 else arrived
        here = codes[0:1, 0:1] if row < 8 else codes[8:9, 0:1]
        wanted = jnp.broadcast_to(number(here == float(row)), (64, 256))
        out[row] = (piece[...].astype(F32) * wanted).astype(BF16)


def per_device(
    n_gx,
    n_gy,
    channel_activations,
    filled_flags,
    cube_locations,
    holder_flag,
    first_kernel_matrices,
    first_offset_vector,
    second_kernel_matrices,
    second_offset_vector,
    reduction_kernel_matrices,
    reduction_offset_vector,
):
    vmem = pl.BlockSpec(memory_space=pltpu.VMEM)
    hbm = pl.BlockSpec(memory_space=pltpu.HBM)
    dma = pltpu.SemaphoreType.DMA
    limit = 56 * 1024 * 1024
    mine, arrived, codes = pl.pallas_call(
        functools.partial(kernel, n_gx, n_gy),
        out_shape=(
            jax.ShapeDtypeStruct((64, 256), BF16),
            jax.ShapeDtypeStruct((64, 256), BF16),
            jax.ShapeDtypeStruct((16, C), F32),
        ),
        in_specs=[hbm, pl.BlockSpec(memory_space=pltpu.SMEM)] + [hbm] * 8,
        out_specs=(hbm, hbm, hbm),
        scratch_shapes=[
            pltpu.VMEM((64, 2 * C), BF16),
            pltpu.VMEM((16, C), F32),
            pltpu.VMEM((1, 3), jnp.int32),
            pltpu.VMEM((1, 512), jnp.int32),
            pltpu.VMEM((1, C), F32),
            pltpu.VMEM((1, C), F32),
            pltpu.VMEM((1, 2 * C), F32),
            pltpu.VMEM((512, C), BF16),
            pltpu.VMEM((9, C, 3 * C), BF16),
            pltpu.VMEM((9, C, 3 * C), BF16),
            pltpu.VMEM((4, C, 4 * C), BF16),
            pltpu.VMEM((8, 8, 8, C), F32),
            pltpu.VMEM((8, 8, 8, C), F32),
            pltpu.VMEM((8, 8, 8, C), F32),
            pltpu.VMEM((6, 10, DEEP, C), BF16),
            pltpu.VMEM((12, 12, DEEP, C), BF16),
            pltpu.VMEM((10, 10, DEEP, C), BF16),
            pltpu.VMEM((3 * C, 3 * C), BF16),
            pltpu.VMEM((3 * C, 3 * C), BF16),
            pltpu.VMEM((3 * C, 3 * C), BF16),
            pltpu.VMEM((3 * C, 3 * C), BF16),
            pltpu.VMEM((4, SIDE_ROWS, C), BF16),
            pltpu.VMEM((4, SIDE_ROWS, C), BF16),
            pltpu.VMEM((4, CORNER_ROWS, C), BF16),
            pltpu.VMEM((4, CORNER_ROWS, C), BF16),
            dma((5,)),
            dma((9,)),
            dma((4,)),
            dma((4,)),
            dma((4,)),
            dma((4,)),
            dma,
            dma,
            dma((2,)),
        ],
        compiler_params=pltpu.CompilerParams(
            collective_id=0, has_side_effects=True, vmem_limit_bytes=limit
        ),
    )(
        cube_locations.reshape(1, 3),
        holder_flag,
        filled_flags,
        first_offset_vector.reshape(1, C),
        second_offset_vector.reshape(1, C),
        reduction_offset_vector.reshape(1, 2 * C),
        channel_activations,
        first_kernel_matrices.reshape(9, 3, C, C),
        second_kernel_matrices.reshape(9, 3, C, C),
        reduction_kernel_matrices.reshape(4, 2, C, 2 * C),
    )
    return pl.pallas_call(
        place,
        out_shape=jax.ShapeDtypeStruct((16, 64, 256), BF16),
        in_specs=[hbm] * 3,
        out_specs=vmem,
        scratch_shapes=[
            pltpu.VMEM((64, 2 * C), BF16),
            pltpu.VMEM((64, 2 * C), BF16),
            pltpu.VMEM((16, C), F32),
            dma((3,)),
        ],
        compiler_params=pltpu.CompilerParams(vmem_limit_bytes=limit),
    )(mine, arrived, codes)


def solution(mesh):
    return jax.shard_map(
        functools.partial(per_device, mesh.shape["gx"], mesh.shape["gy"]),
        mesh=mesh,
        in_specs=(
            P(("gx", "gy"), None, None),
            P(("gx", "gy"), None),
            P(None, ("gx", "gy")),
            P("gx", "gy"),
            P(),
            P(),
            P(),
            P(),
            P(),
            P(),
        ),
        out_specs=P(("gx", "gy"), None, None),
        check_vma=False,
    )
```

```python
import functools

import jax
import jax.numpy as jnp
from jax import lax
from jax.experimental import pallas as pl
from jax.experimental.pallas import tpu as pltpu
from jax.sharding import PartitionSpec as P

MESH = pl.DeviceIdType.MESH
F32 = jnp.float32
BF16 = jnp.bfloat16
C = 128
DEEP = 16
SIDE_ROWS = 144
CORNER_ROWS = 48
PIECE_ROWS = 80


def silu(s):
    return 0.5 * s * (1.0 + jnp.tanh(0.5 * s))


def number(condition):
    return jnp.where(condition, 1.0, 0.0).astype(F32)


def along_z(products, deep):
    count = products.shape[0] // deep
    low, mid, high = (products[:, k * C : (k + 1) * C].reshape(count, deep, C) for k in range(3))
    z = lax.broadcasted_iota(jnp.int32, (count, deep, C), 1)
    low = jnp.where(z == 0, 0.0, pltpu.roll(low, 1, 1))
    high = jnp.where(z == deep - 1, 0.0, pltpu.roll(high, deep - 1, 1))
    return mid + low + high


def pack(target, value):
    zero = jnp.zeros((1, 8, 8, C), F32)
    upper = jnp.concatenate([zero, value[0:5]], axis=0)
    lower = jnp.concatenate([value[3:8], zero], axis=0)
    target[:, 1:9] = jnp.concatenate([upper, lower], axis=2).astype(BF16)


def own_conv(tiles, weight):
    taps = [tiles[p : p + 4, q : q + 8].reshape(512, C) for p in range(3) for q in range(3)]
    products = jnp.dot(
        jnp.concatenate(taps, axis=1),
        weight[...].reshape(9 * C, 3 * C),
        preferred_element_type=F32,
    )
    total = along_z(products, 8).reshape(4, 8, 2, 8, C)
    return jnp.concatenate([total[:, :, 0], total[:, :, 1]], axis=0)


def edge_conv(line, weight, ozf):
    taps = [line[k : k + 8].reshape(8 * DEEP, C) for k in range(3)]
    products = jnp.dot(jnp.concatenate(taps, axis=1), weight, preferred_element_type=F32)
    total = along_z(products, DEEP)
    return total[:, 0:8] * (1.0 - ozf) + total[:, 8:16] * ozf


def kernel(
    n_gx,
    n_gy,
    location_at,
    holder,
    flags_at,
    first_bias_at,
    second_bias_at,
    last_bias_at,
    features,
    first_weight,
    second_weight,
    last_weight,
    mine,
    arrived,
    pieces,
    location,
    flags,
    first_bias,
    second_bias,
    last_bias,
    cells,
    w1,
    w2,
    w3,
    s8,
    m8,
    total8,
    tiles,
    field,
    full,
    w1x,
    w1y,
    w2x,
    w2y,
    side_out,
    side_in,
    corner_out,
    corner_in,
    small_sem,
    local_sem,
    side_send,
    side_recv,
    corner_send,
    corner_recv,
    last_send,
    last_recv,
    result_sem,
):
    i = lax.axis_index("gx")
    j = lax.axis_index("gy")
    above = lax.rem(j + 1, n_gy)
    sides = ((i - 1, j), (i + 1, j), (i, j - 1), (i, j + 1))
    corners = ((i - 1, j - 1), (i - 1, j + 1), (i + 1, j - 1), (i + 1, j + 1))
    there = (i > 0, i < n_gx - 1, j > 0, j < n_gy - 1)
    inside = tuple(number(t) for t in there)
    corner_there = tuple(there[a] & there[2 + b] for a in range(2) for b in range(2))

    barrier = pltpu.get_barrier_semaphore()

    def greet(device):
        pl.semaphore_signal(barrier, inc=1, device_id=device, device_id_type=MESH)

    for device, exists in zip(sides + corners, there + corner_there):
        pl.when(exists)(functools.partial(greet, device))
    pl.when(j == 0)(functools.partial(greet, (i, n_gy - 1)))

    copies = [pltpu.make_async_copy(features.at[0], cells, local_sem.at[0])]
    for k in range(3):
        copies.append(
            pltpu.make_async_copy(
                first_weight.at[:, k], w1.at[:, :, pl.ds(k * C, C)], local_sem.at[1 + k]
            )
        )
    for k in range(3):
        copies.append(
            pltpu.make_async_copy(
                second_weight.at[:, k], w2.at[:, :, pl.ds(k * C, C)], local_sem.at[4 + k]
            )
        )
    for k in range(2):
        copies.append(
            pltpu.make_async_copy(
                last_weight.at[:, k], w3.at[:, :, pl.ds(k * 2 * C, 2 * C)], local_sem.at[7 + k]
            )
        )
    small = [
        pltpu.make_async_copy(source, target, small_sem.at[k])
        for k, (source, target) in enumerate(
            (
                (location_at, location),
                (flags_at, flags),
                (first_bias_at, first_bias),
                (second_bias_at, second_bias),
                (last_bias_at, last_bias),
            )
        )
    ]
    for copy in small + copies:
        copy.start()
    for copy in small[0:2]:
        copy.wait()

    octant = (location[...] & 1).astype(F32)
    oxf, oyf, ozf = (jnp.broadcast_to(octant[:, k : k + 1], (8, C)) for k in range(3))
    code = oxf * 4.0 + oyf * 2.0 + ozf + 8.0 * holder[0, 0].astype(F32)

    r = lax.broadcasted_iota(jnp.int32, (C, C), 0)
    c = lax.broadcasted_iota(jnp.int32, (C, C), 1)
    ones = jnp.ones((C, C), BF16)
    for k in range(4):
        line = jnp.broadcast_to(flags[:, k * C : (k + 1) * C].astype(F32), (C, C))
        diagonal = jnp.where(r == c, line, 0.0).astype(BF16)
        m8[pl.ds(2 * k, 2)] = jnp.dot(diagonal, ones, preferred_element_type=F32).reshape(
            2, 8, 8, C
        )

    copies[0].wait()
    s8[...] = cells[...].astype(F32).reshape(8, 8, 8, C) * m8[...]

    lane = lax.broadcasted_iota(jnp.int32, (8, C), 1)

    def in_lanes(columns):
        return sum(jnp.where(lane == c, columns[c], 0.0) for c in range(8))

    tag = jnp.concatenate([code, code], axis=1)
    pieces[64:80] = jnp.concatenate([tag, tag], axis=0).astype(BF16)
    for k in range(4):
        n, f = (0, 0) if k % 2 == 0 else (7, 6)
        value = s8[f : f + 2] if k < 2 else s8[:, f : f + 2]
        near = m8[n] if k < 2 else m8[:, n]
        side_out[k, 0:128] = value.reshape(128, C).astype(BF16)
        side_out[k, 128:144] = jnp.concatenate([in_lanes(near), code], axis=0).astype(BF16)
    for a in range(2):
        for b in range(2):
            near = m8[7 * a, 7 * b]
            corner_out[2 * a + b, 0:32] = (
                s8[6 * a : 6 * a + 2, 6 * b : 6 * b + 2].reshape(32, C).astype(BF16)
            )
            corner_out[2 * a + b, 32:48] = jnp.concatenate(
                [near, code], axis=0
            ).astype(BF16)

    ways = [there[k].astype(jnp.int32) for k in range(4)]
    greeted = (1 + ways[0] + ways[1]) * (1 + ways[2] + ways[3]) - 1
    pl.semaphore_wait(barrier, greeted + (j == n_gy - 1).astype(jnp.int32))
    sent = []
    for k, device in enumerate(corners):
        copy = pltpu.make_async_remote_copy(
            src_ref=corner_out.at[k],
            dst_ref=corner_in.at[3 - k],
            send_sem=corner_send.at[k],
            recv_sem=corner_recv.at[3 - k],
            device_id=device,
            device_id_type=MESH,
        )
        sent.append((copy, corner_there[k], corner_there[3 - k]))
    for k, device in enumerate(sides):
        copy = pltpu.make_async_remote_copy(
            src_ref=side_out.at[k],
            dst_ref=side_in.at[k ^ 1],
            send_sem=side_send.at[k],
            recv_sem=side_recv.at[k ^ 1],
            device_id=device,
            device_id_type=MESH,
        )
        sent.append((copy, there[k], there[k ^ 1]))
    for copy, exists, _ in sent:
        pl.when(exists)(copy.start)

    def clear(ref, k):
        ref[k] = jnp.zeros(ref.shape[1:], BF16)

    for k in range(4):
        pl.when(jnp.logical_not(there[k]))(functools.partial(clear, side_in, k))
        pl.when(jnp.logical_not(corner_there[k]))(functools.partial(clear, corner_in, k))

    ox2, oy2 = (jnp.concatenate([o, o], axis=0).astype(BF16) for o in (oxf, oyf))
    not_ox2, not_oy2 = (
        jnp.concatenate([1.0 - o, 1.0 - o], axis=0).astype(BF16) for o in (oxf, oyf)
    )
    field[2:10, 2:10] = jnp.concatenate([s8[...] * (1.0 - ozf), s8[...] * ozf], axis=2).astype(BF16)
    full[1:9, 1:9] = jnp.concatenate([m8[...] * (1.0 - ozf), m8[...] * ozf], axis=2).astype(BF16)
    tiles[:, 0] = jnp.zeros((6, DEEP, C), BF16)
    tiles[:, 9] = jnp.zeros((6, DEEP, C), BF16)
    pack(tiles, s8[...])

    def edge_weights(weight, along_x, along_y):
        for k in range(3):
            for r in range(3):
                rows, columns = slice(k * C, (k + 1) * C), slice(r * C, (r + 1) * C)
                for target, a, b, side, other in (
                    (along_x, k, 6 + k, not_ox2, ox2),
                    (along_y, 3 * k, 3 * k + 2, not_oy2, oy2),
                ):
                    first = weight[a, :, columns].reshape(8, DEEP, C) * side
                    second = weight[b, :, columns].reshape(8, DEEP, C) * other
                    target[rows, columns] = (first + second).reshape(C, C)

    for copy in small[2:]:
        copy.wait()
    bias1 = first_bias[...]
    bias2 = second_bias[...]
    for copy in copies[1:4]:
        copy.wait()
    total8[...] = own_conv(tiles, w1) + bias1
    edge_weights(w1, w1x, w1y)
    for copy in copies[4:]:
        copy.wait()
    edge_weights(w2, w2x, w2y)

    def corners_of(value):
        halves = value.reshape(4, 2, 4, 2, 8, C)
        return [halves[:, a, :, b].reshape(C, C) for a in range(2) for b in range(2)]

    def next_row(value):
        return pltpu.roll(value, C - 1, 0)

    count = sum(corners_of(m8[...]))
    count = count + next_row(count)
    count = jnp.concatenate([count, count], axis=1)

    for copy, _, exists in sent:
        pl.when(exists)(copy.wait_recv)

    def decode(tag):
        nx = number(tag >= 4.0)
        rest = tag - 4.0 * nx
        ny = number(rest >= 2.0)
        nz = rest - 2.0 * ny
        return nx, ny, nz

    def placed(value, gate, nz):
        return jnp.concatenate([value * (gate * (1.0 - nz)), value * (gate * nz)], axis=-2)

    facing = (1.0 - oxf, oxf, 1.0 - oyf, oyf)
    lower = [None] * 4
    upper = [None] * 4
    for k in range(4):
        tail = side_in[k, 128:144].astype(F32)
        got = tail[8:16]
        got = got - 8.0 * number(got >= 8.0)
        nx, ny, nz = decode(got)
        across, beside, own = (nx, ny, oyf) if k < 2 else (ny, nx, oxf)
        meets = across if k % 2 == 0 else 1.0 - across
        gate = meets * (inside[k] * facing[k])
        same = gate * (beside * own + (1.0 - beside) * (1.0 - own))
        minus = gate * ((1.0 - beside) * own)
        plus = gate * (beside * (1.0 - own))
        flag = jnp.stack([jnp.broadcast_to(tail[0:8, c : c + 1], (8, C)) for c in range(8)])
        if k < 2:
            value = side_in[k, 0:128].astype(F32).reshape(2, 8, 8, C)
            x = 0 if k == 0 else 10
            field[x : x + 2, 2:10] = placed(value, same, nz).astype(BF16)
            full[0 if k == 0 else 9, 1:9] = placed(flag, same, nz).astype(BF16)
            lower[k] = (placed(value[:, 6:8], minus, nz), placed(flag[7], minus, nz))
            upper[k] = (placed(value[:, 0:2], plus, nz), placed(flag[0], plus, nz))
        else:
            value = side_in[k, 0:128].astype(F32).reshape(8, 2, 8, C)
            y = 0 if k == 2 else 10
            field[2:10, y : y + 2] = placed(value, same, nz).astype(BF16)
            full[1:9, 0 if k == 2 else 9] = placed(flag, same, nz).astype(BF16)
            lower[k] = (placed(value[6:8], minus, nz), placed(flag[7], minus, nz))
            upper[k] = (placed(value[0:2], plus, nz), placed(flag[0], plus, nz))
    for a in range(2):
        for b in range(2):
            k = 2 * a + b
            tail = corner_in[k, 32:48].astype(F32)
            got = tail[8:16]
            got = got - 8.0 * number(got >= 8.0)
            nx, ny, nz = decode(got)
            gate = (nx if a == 0 else 1.0 - nx) * (ny if b == 0 else 1.0 - ny)
            gate = gate * (inside[a] * inside[2 + b] * facing[a] * facing[2 + b])
            value = corner_in[k, 0:32].astype(F32).reshape(2, 2, 8, C)
            from_x = (lower if b == 0 else upper)[a]
            from_y = (lower if a == 0 else upper)[2 + b]
            x, y = 10 * a, 10 * b
            field[x : x + 2, y : y + 2] = (
                placed(value, gate, nz) + from_x[0] + from_y[0]
            ).astype(BF16)
            full[9 * a, 9 * b] = (placed(tail[0:8], gate, nz) + from_x[1] + from_y[1]).astype(BF16)

    beside_x = field[0:3] * not_ox2 + field[9:12] * ox2
    beside_y = field[:, 0:3] * not_oy2 + field[:, 9:12] * oy2
    stacked = jnp.concatenate(
        [
            jnp.concatenate(
                [
                    beside_x[p, q : q + 10].reshape(10 * DEEP, C),
                    beside_y[p : p + 10, q].reshape(10 * DEEP, C),
                ],
                axis=0,
            )
            for p in range(3)
            for q in range(3)
        ],
        axis=1,
    )
    products = jnp.dot(stacked, w1[...].reshape(9 * C, 3 * C), preferred_element_type=F32)
    flag = jnp.concatenate(
        [full[0] * not_ox2 + full[9] * ox2, full[:, 0] * not_oy2 + full[:, 9] * oy2], axis=0
    ).astype(F32)
    line = (flag * silu(along_z(products, DEEP) + bias1[None])).astype(BF16)

    def without_corner(line):
        return jnp.concatenate([line[0:1] * ox2, line[1:9], line[9:10] * not_ox2], axis=0)

    def add_edges(line_x, line_y, weight_x, weight_y):
        from_x = edge_conv(line_x, weight_x[...], ozf)
        from_y = edge_conv(without_corner(line_y), weight_y[...], ozf)
        total8[0] = total8[0] + from_x * (1.0 - oxf)
        total8[7] = total8[7] + from_x * oxf
        total8[:, 0] = total8[:, 0] + from_y * (1.0 - oyf)
        total8[:, 7] = total8[:, 7] + from_y * oyf

    add_edges(beside_x[1, 1:11], beside_y[1:11, 1], w1x, w1y)
    pack(tiles, m8[...] * silu(total8[...]))

    total8[...] = own_conv(tiles, w2) + bias2 + s8[...]
    add_edges(line[0:10], line[10:20], w2x, w2y)
    block = m8[...] * silu(total8[...])

    stacked = jnp.concatenate(corners_of(block), axis=1).astype(BF16)
    products = jnp.dot(stacked, w3[...].reshape(4 * C, 4 * C), preferred_element_type=F32)
    total = products[:, 0 : 2 * C] + next_row(products[:, 2 * C :]) + last_bias[...]
    total = jnp.where(count > 0.5, total, 0.0).astype(BF16)
    pr = lax.broadcasted_iota(jnp.int32, (64, C), 0)
    pc = lax.broadcasted_iota(jnp.int32, (64, C), 1)
    pick = jnp.where(pc == 2 * pr, 1.0, 0.0).astype(BF16)
    pieces[0:64] = jnp.dot(pick, total, preferred_element_type=F32).astype(BF16)

    last = pltpu.make_async_remote_copy(
        src_ref=pieces,
        dst_ref=arrived,
        send_sem=last_send,
        recv_sem=last_recv,
        device_id=(i, above),
        device_id_type=MESH,
    )
    last.start()
    result = pltpu.make_async_copy(pieces, mine, result_sem)
    result.start()
    for copy, exists, _ in sent:
        pl.when(exists)(copy.wait_send)
    result.wait()
    last.wait()


def place(mine_at, arrived_at, out, mine, arrived, sem):
    pairs = ((mine_at, mine), (arrived_at, arrived))
    copies = [pltpu.make_async_copy(a, b, sem.at[k]) for k, (a, b) in enumerate(pairs)]
    for copy in copies:
        copy.start()
    for copy in copies:
        copy.wait()
    for row in range(16):
        held = mine if row < 8 else arrived
        here = held[64:80].astype(F32)[0:1, 0:1]
        wanted = jnp.broadcast_to(number(here == float(row)), (64, 256))
        out[row] = (held[0:64].astype(F32) * wanted).astype(BF16)


def per_device(
    n_gx,
    n_gy,
    channel_activations,
    filled_flags,
    cube_locations,
    holder_flag,
    first_kernel_matrices,
    first_offset_vector,
    second_kernel_matrices,
    second_offset_vector,
    reduction_kernel_matrices,
    reduction_offset_vector,
):
    vmem = pl.BlockSpec(memory_space=pltpu.VMEM)
    hbm = pl.BlockSpec(memory_space=pltpu.HBM)
    dma = pltpu.SemaphoreType.DMA
    limit = 56 * 1024 * 1024
    mine, arrived = pl.pallas_call(
        functools.partial(kernel, n_gx, n_gy),
        out_shape=(
            jax.ShapeDtypeStruct((PIECE_ROWS, 256), BF16),
            jax.ShapeDtypeStruct((PIECE_ROWS, 256), BF16),
        ),
        in_specs=[hbm, pl.BlockSpec(memory_space=pltpu.SMEM)] + [hbm] * 8,
        out_specs=(hbm, hbm),
        scratch_shapes=[
            pltpu.VMEM((PIECE_ROWS, 2 * C), BF16),
            pltpu.VMEM((1, 3), jnp.int32),
            pltpu.VMEM((1, 512), jnp.int32),
            pltpu.VMEM((1, C), F32),
            pltpu.VMEM((1, C), F32),
            pltpu.VMEM((1, 2 * C), F32),
            pltpu.VMEM((512, C), BF16),
            pltpu.VMEM((9, C, 3 * C), BF16),
            pltpu.VMEM((9, C, 3 * C), BF16),
            pltpu.VMEM((4, C, 4 * C), BF16),
            pltpu.VMEM((8, 8, 8, C), F32),
            pltpu.VMEM((8, 8, 8, C), F32),
            pltpu.VMEM((8, 8, 8, C), F32),
            pltpu.VMEM((6, 10, DEEP, C), BF16),
            pltpu.VMEM((12, 12, DEEP, C), BF16),
            pltpu.VMEM((10, 10, DEEP, C), BF16),
            pltpu.VMEM((3 * C, 3 * C), BF16),
            pltpu.VMEM((3 * C, 3 * C), BF16),
            pltpu.VMEM((3 * C, 3 * C), BF16),
            pltpu.VMEM((3 * C, 3 * C), BF16),
            pltpu.VMEM((4, SIDE_ROWS, C), BF16),
            pltpu.VMEM((4, SIDE_ROWS, C), BF16),
            pltpu.VMEM((4, CORNER_ROWS, C), BF16),
            pltpu.VMEM((4, CORNER_ROWS, C), BF16),
            dma((5,)),
            dma((9,)),
            dma((4,)),
            dma((4,)),
            dma((4,)),
            dma((4,)),
            dma,
            dma,
            dma,
        ],
        compiler_params=pltpu.CompilerParams(
            collective_id=0, has_side_effects=True, vmem_limit_bytes=limit
        ),
    )(
        cube_locations.reshape(1, 3),
        holder_flag,
        filled_flags,
        first_offset_vector.reshape(1, C),
        second_offset_vector.reshape(1, C),
        reduction_offset_vector.reshape(1, 2 * C),
        channel_activations,
        first_kernel_matrices.reshape(9, 3, C, C),
        second_kernel_matrices.reshape(9, 3, C, C),
        reduction_kernel_matrices.reshape(4, 2, C, 2 * C),
    )
    return pl.pallas_call(
        place,
        out_shape=jax.ShapeDtypeStruct((16, 64, 256), BF16),
        in_specs=[hbm] * 2,
        out_specs=vmem,
        scratch_shapes=[
            pltpu.VMEM((PIECE_ROWS, 2 * C), BF16),
            pltpu.VMEM((PIECE_ROWS, 2 * C), BF16),
            dma((2,)),
        ],
        compiler_params=pltpu.CompilerParams(vmem_limit_bytes=limit),
    )(mine, arrived)


def solution(mesh):
    return jax.shard_map(
        functools.partial(per_device, mesh.shape["gx"], mesh.shape["gy"]),
        mesh=mesh,
        in_specs=(
            P(("gx", "gy"), None, None),
            P(("gx", "gy"), None),
            P(None, ("gx", "gy")),
            P("gx", "gy"),
            P(),
            P(),
            P(),
            P(),
            P(),
            P(),
        ),
        out_specs=P(("gx", "gy"), None, None),
        check_vma=False,
    )
```

```python
import functools

import jax
import jax.numpy as jnp
from jax import lax
from jax.experimental import pallas as pl
from jax.experimental.pallas import tpu as pltpu
from jax.sharding import PartitionSpec as P

MESH = pl.DeviceIdType.MESH
F32 = jnp.float32
BF16 = jnp.bfloat16
C = 128
DEEP = 16
SIDE_ROWS = 144
CORNER_ROWS = 48
PIECE_ROWS = 80


def silu(s):
    return 0.5 * s * (1.0 + jnp.tanh(0.5 * s))


def number(condition):
    return jnp.where(condition, 1.0, 0.0).astype(F32)


def along_z(products, deep):
    count = products.shape[0] // deep
    low, mid, high = (products[:, k * C : (k + 1) * C].reshape(count, deep, C) for k in range(3))
    z = lax.broadcasted_iota(jnp.int32, (count, deep, C), 1)
    low = jnp.where(z == 0, 0.0, pltpu.roll(low, 1, 1))
    high = jnp.where(z == deep - 1, 0.0, pltpu.roll(high, deep - 1, 1))
    return mid + low + high


def pack(target, value):
    zero = jnp.zeros((1, 8, 8, C), F32)
    upper = jnp.concatenate([zero, value[0:5]], axis=0)
    lower = jnp.concatenate([value[3:8], zero], axis=0)
    target[:, 1:9] = jnp.concatenate([upper, lower], axis=2).astype(BF16)


def own_conv(tiles, weight):
    taps = [tiles[p : p + 4, q : q + 8].reshape(512, C) for p in range(3) for q in range(3)]
    products = jnp.dot(
        jnp.concatenate(taps, axis=1),
        weight[...].reshape(9 * C, 3 * C),
        preferred_element_type=F32,
    )
    total = along_z(products, 8).reshape(4, 8, 2, 8, C)
    return jnp.concatenate([total[:, :, 0], total[:, :, 1]], axis=0)


def line_taps(line):
    return jnp.concatenate([line[k : k + 8].reshape(8 * DEEP, C) for k in range(3)], axis=1)


def own_half(products, ozf):
    total = along_z(products, DEEP)
    return total[:, 0:8] * (1.0 - ozf) + total[:, 8:16] * ozf


def dot(a, b):
    return jnp.dot(a, b, preferred_element_type=F32)


def split_rows(target, value):
    value = value.reshape(8, 4, 2, 8, C)
    for b in range(2):
        target[:, b] = value[:, :, b].reshape(8, 32, C)


def corner_rows(source, a, b, k):
    return jnp.concatenate(
        [source[2 * u + a, b, pl.ds(k, 16, stride=2), :] for u in range(4)], axis=0
    )


def kernel(
    n_gx,
    n_gy,
    location_at,
    holder,
    flags_at,
    first_bias_at,
    second_bias_at,
    last_bias_at,
    features,
    first_weight,
    second_weight,
    last_weight,
    mine,
    arrived,
    location,
    flags,
    first_bias,
    second_bias,
    last_bias,
    cells,
    w1,
    w2,
    w3,
    s8,
    m8,
    total8,
    block8,
    halves,
    tiles,
    field,
    full,
    w1x,
    w1y,
    w2x,
    w2y,
    w2m,
    side_out,
    side_in,
    corner_out,
    corner_in,
    small_sem,
    local_sem,
    side_send,
    side_recv,
    corner_send,
    corner_recv,
    last_send,
    last_recv,
):
    i = lax.axis_index("gx")
    j = lax.axis_index("gy")
    above = lax.rem(j + 1, n_gy)
    sides = ((i - 1, j), (i + 1, j), (i, j - 1), (i, j + 1))
    corners = ((i - 1, j - 1), (i - 1, j + 1), (i + 1, j - 1), (i + 1, j + 1))
    there = (i > 0, i < n_gx - 1, j > 0, j < n_gy - 1)
    inside = tuple(number(t) for t in there)
    corner_there = tuple(there[a] & there[2 + b] for a in range(2) for b in range(2))

    barrier = pltpu.get_barrier_semaphore()

    def greet(device):
        pl.semaphore_signal(barrier, inc=1, device_id=device, device_id_type=MESH)

    for device, exists in zip(sides + corners, there + corner_there):
        pl.when(exists)(functools.partial(greet, device))
    pl.when(j == 0)(functools.partial(greet, (i, n_gy - 1)))

    copies = [pltpu.make_async_copy(features.at[0], cells, local_sem.at[0])]
    for k in range(3):
        copies.append(
            pltpu.make_async_copy(
                first_weight.at[:, k], w1.at[:, :, pl.ds(k * C, C)], local_sem.at[1 + k]
            )
        )
    for k in range(3):
        copies.append(
            pltpu.make_async_copy(
                second_weight.at[:, k], w2.at[:, :, pl.ds(k * C, C)], local_sem.at[4 + k]
            )
        )
    copies.append(pltpu.make_async_copy(last_weight, w3, local_sem.at[7]))
    small = [
        pltpu.make_async_copy(source, target, small_sem.at[k])
        for k, (source, target) in enumerate(
            (
                (location_at, location),
                (flags_at, flags),
                (first_bias_at, first_bias),
                (second_bias_at, second_bias),
                (last_bias_at, last_bias),
            )
        )
    ]
    for copy in small + copies:
        copy.start()
    for copy in small[0:2]:
        copy.wait()

    octant = (location[...] & 1).astype(F32)
    oxf, oyf, ozf = (jnp.broadcast_to(octant[:, k : k + 1], (8, C)) for k in range(3))
    code = oxf * 4.0 + oyf * 2.0 + ozf + 8.0 * holder[0, 0].astype(F32)

    r = lax.broadcasted_iota(jnp.int32, (C, C), 0)
    c = lax.broadcasted_iota(jnp.int32, (C, C), 1)
    ones = jnp.ones((C, C), BF16)
    for k in range(4):
        line = jnp.broadcast_to(flags[:, k * C : (k + 1) * C].astype(F32), (C, C))
        diagonal = jnp.where(r == c, line, 0.0).astype(BF16)
        m8[pl.ds(2 * k, 2)] = jnp.dot(diagonal, ones, preferred_element_type=F32).reshape(
            2, 8, 8, C
        )

    copies[0].wait()
    s8[...] = cells[...].astype(F32).reshape(8, 8, 8, C) * m8[...]

    lane = lax.broadcasted_iota(jnp.int32, (8, C), 1)

    def in_lanes(columns):
        return sum(jnp.where(lane == c, columns[c], 0.0) for c in range(8))

    tag = jnp.concatenate([code, code], axis=1)
    mine[64:80] = jnp.concatenate([tag, tag], axis=0).astype(BF16)
    for k in range(4):
        n, f = (0, 0) if k % 2 == 0 else (7, 6)
        value = s8[f : f + 2] if k < 2 else s8[:, f : f + 2]
        near = m8[n] if k < 2 else m8[:, n]
        side_out[k, 0:128] = value.reshape(128, C).astype(BF16)
        side_out[k, 128:144] = jnp.concatenate([in_lanes(near), code], axis=0).astype(BF16)
    for a in range(2):
        for b in range(2):
            near = m8[7 * a, 7 * b]
            corner_out[2 * a + b, 0:32] = (
                s8[6 * a : 6 * a + 2, 6 * b : 6 * b + 2].reshape(32, C).astype(BF16)
            )
            corner_out[2 * a + b, 32:48] = jnp.concatenate(
                [near, code], axis=0
            ).astype(BF16)

    ways = [there[k].astype(jnp.int32) for k in range(4)]
    greeted = (1 + ways[0] + ways[1]) * (1 + ways[2] + ways[3]) - 1
    pl.semaphore_wait(barrier, greeted + (j == n_gy - 1).astype(jnp.int32))
    sent = []
    for k, device in enumerate(corners):
        copy = pltpu.make_async_remote_copy(
            src_ref=corner_out.at[k],
            dst_ref=corner_in.at[3 - k],
            send_sem=corner_send.at[k],
            recv_sem=corner_recv.at[3 - k],
            device_id=device,
            device_id_type=MESH,
        )
        sent.append((copy, corner_there[k], corner_there[3 - k]))
    for k, device in enumerate(sides):
        copy = pltpu.make_async_remote_copy(
            src_ref=side_out.at[k],
            dst_ref=side_in.at[k ^ 1],
            send_sem=side_send.at[k],
            recv_sem=side_recv.at[k ^ 1],
            device_id=device,
            device_id_type=MESH,
        )
        sent.append((copy, there[k], there[k ^ 1]))
    for copy, exists, _ in sent:
        pl.when(exists)(copy.start)

    def clear(ref, k):
        ref[k] = jnp.zeros(ref.shape[1:], BF16)

    for k in range(4):
        pl.when(jnp.logical_not(there[k]))(functools.partial(clear, side_in, k))
        pl.when(jnp.logical_not(corner_there[k]))(functools.partial(clear, corner_in, k))

    ox2, oy2 = (jnp.concatenate([o, o], axis=0).astype(BF16) for o in (oxf, oyf))
    not_ox2, not_oy2 = (
        jnp.concatenate([1.0 - o, 1.0 - o], axis=0).astype(BF16) for o in (oxf, oyf)
    )
    field[2:10, 2:10] = jnp.concatenate([s8[...] * (1.0 - ozf), s8[...] * ozf], axis=2).astype(BF16)
    full[1:9, 1:9] = jnp.concatenate([m8[...] * (1.0 - ozf), m8[...] * ozf], axis=2).astype(BF16)
    tiles[:, 0] = jnp.zeros((6, DEEP, C), BF16)
    tiles[:, 9] = jnp.zeros((6, DEEP, C), BF16)
    pack(tiles, s8[...])

    def edge_weights(weight, along_x, along_y):
        for k in range(3):
            for r in range(3):
                rows, columns = slice(k * C, (k + 1) * C), slice(r * C, (r + 1) * C)
                for target, a, b, side, other in (
                    (along_x, k, 6 + k, not_ox2, ox2),
                    (along_y, 3 * k, 3 * k + 2, not_oy2, oy2),
                ):
                    first = weight[a, :, columns].reshape(8, DEEP, C) * side
                    second = weight[b, :, columns].reshape(8, DEEP, C) * other
                    target[rows, columns] = (first + second).reshape(C, C)

    for copy in small[2:]:
        copy.wait()
    bias1 = first_bias[...]
    bias2 = second_bias[...]
    for copy in copies[1:4]:
        copy.wait()
    total8[...] = own_conv(tiles, w1) + bias1
    edge_weights(w1, w1x, w1y)
    for copy in copies[4:]:
        copy.wait()
    edge_weights(w2, w2x, w2y)
    for k in range(3):
        w2m[k * C : (k + 1) * C] = w2[3 * k + 1]

    x = lax.broadcasted_iota(jnp.int32, (8, 8, 8, C), 0)
    y = lax.broadcasted_iota(jnp.int32, (8, 8, 8, C), 1)
    inner_x = jnp.where(x == 0, oxf, jnp.where(x == 7, 1.0 - oxf, 1.0))
    inner_y = jnp.where(y == 0, oyf, jnp.where(y == 7, 1.0 - oyf, 1.0))
    pack(tiles, m8[...] * inner_x * inner_y * silu(total8[...]))
    block8[...] = own_conv(tiles, w2) + bias2 + s8[...]

    groups = [(a, b, k) for a in range(2) for b in range(2) for k in range(2)]
    split_rows(halves, m8[...])
    count = sum(corner_rows(halves, *group) for group in groups)
    count = jnp.concatenate([count, count], axis=1)

    for copy, _, exists in sent:
        pl.when(exists)(copy.wait_recv)

    def decode(tag):
        nx = number(tag >= 4.0)
        rest = tag - 4.0 * nx
        ny = number(rest >= 2.0)
        nz = rest - 2.0 * ny
        return nx, ny, nz

    def placed(value, gate, nz):
        return jnp.concatenate([value * (gate * (1.0 - nz)), value * (gate * nz)], axis=-2)

    facing = (1.0 - oxf, oxf, 1.0 - oyf, oyf)
    lower = [None] * 4
    upper = [None] * 4
    for k in range(4):
        tail = side_in[k, 128:144].astype(F32)
        got = tail[8:16]
        got = got - 8.0 * number(got >= 8.0)
        nx, ny, nz = decode(got)
        across, beside, own = (nx, ny, oyf) if k < 2 else (ny, nx, oxf)
        meets = across if k % 2 == 0 else 1.0 - across
        gate = meets * (inside[k] * facing[k])
        same = gate * (beside * own + (1.0 - beside) * (1.0 - own))
        minus = gate * ((1.0 - beside) * own)
        plus = gate * (beside * (1.0 - own))
        flag = jnp.stack([jnp.broadcast_to(tail[0:8, c : c + 1], (8, C)) for c in range(8)])
        if k < 2:
            value = side_in[k, 0:128].astype(F32).reshape(2, 8, 8, C)
            x = 0 if k == 0 else 10
            field[x : x + 2, 2:10] = placed(value, same, nz).astype(BF16)
            full[0 if k == 0 else 9, 1:9] = placed(flag, same, nz).astype(BF16)
            lower[k] = (placed(value[:, 6:8], minus, nz), placed(flag[7], minus, nz))
            upper[k] = (placed(value[:, 0:2], plus, nz), placed(flag[0], plus, nz))
        else:
            value = side_in[k, 0:128].astype(F32).reshape(8, 2, 8, C)
            y = 0 if k == 2 else 10
            field[2:10, y : y + 2] = placed(value, same, nz).astype(BF16)
            full[1:9, 0 if k == 2 else 9] = placed(flag, same, nz).astype(BF16)
            lower[k] = (placed(value[6:8], minus, nz), placed(flag[7], minus, nz))
            upper[k] = (placed(value[0:2], plus, nz), placed(flag[0], plus, nz))
    for a in range(2):
        for b in range(2):
            k = 2 * a + b
            tail = corner_in[k, 32:48].astype(F32)
            got = tail[8:16]
            got = got - 8.0 * number(got >= 8.0)
            nx, ny, nz = decode(got)
            gate = (nx if a == 0 else 1.0 - nx) * (ny if b == 0 else 1.0 - ny)
            gate = gate * (inside[a] * inside[2 + b] * facing[a] * facing[2 + b])
            value = corner_in[k, 0:32].astype(F32).reshape(2, 2, 8, C)
            from_x = (lower if b == 0 else upper)[a]
            from_y = (lower if a == 0 else upper)[2 + b]
            x, y = 10 * a, 10 * b
            field[x : x + 2, y : y + 2] = (
                placed(value, gate, nz) + from_x[0] + from_y[0]
            ).astype(BF16)
            full[9 * a, 9 * b] = (placed(tail[0:8], gate, nz) + from_x[1] + from_y[1]).astype(BF16)

    beside_x = field[0:3] * not_ox2 + field[9:12] * ox2
    beside_y = field[:, 0:3] * not_oy2 + field[:, 9:12] * oy2
    stacked = jnp.concatenate(
        [
            jnp.concatenate(
                [
                    beside_x[p, q : q + 10].reshape(10 * DEEP, C),
                    beside_y[p : p + 10, q].reshape(10 * DEEP, C),
                ],
                axis=0,
            )
            for p in range(3)
            for q in range(3)
        ],
        axis=1,
    )
    products = jnp.dot(stacked, w1[...].reshape(9 * C, 3 * C), preferred_element_type=F32)
    flag = jnp.concatenate(
        [full[0] * not_ox2 + full[9] * ox2, full[:, 0] * not_oy2 + full[:, 9] * oy2], axis=0
    ).astype(F32)
    line = (flag * silu(along_z(products, DEEP) + bias1[None])).astype(BF16)

    def without_corner(line):
        return jnp.concatenate([line[0:1] * ox2, line[1:9], line[9:10] * not_ox2], axis=0)

    def add(target, from_x, from_y, near):
        target[near] = target[near] + from_x * (1.0 - oxf)
        target[7 - near] = target[7 - near] + from_x * oxf
        target[:, near] = target[:, near] + from_y * (1.0 - oyf)
        target[:, 7 - near] = target[:, 7 - near] + from_y * oyf

    from_x = own_half(dot(line_taps(beside_x[1, 1:11]), w1x[...]), ozf)
    from_y = own_half(dot(line_taps(without_corner(beside_y[1:11, 1])), w1y[...]), ozf)
    add(total8, from_x, from_y, 0)

    def edge_line(total, flag):
        value = flag * silu(total)
        value = jnp.concatenate([value * (1.0 - ozf), value * ozf], axis=1).astype(BF16)
        zero = jnp.zeros((1, DEEP, C), BF16)
        return jnp.concatenate([zero, value, zero], axis=0)

    plane_x = edge_line(
        total8[0] * (1.0 - oxf) + total8[7] * oxf, m8[0] * (1.0 - oxf) + m8[7] * oxf
    )
    plane_y = edge_line(
        total8[:, 0] * (1.0 - oyf) + total8[:, 7] * oyf, m8[:, 0] * (1.0 - oyf) + m8[:, 7] * oyf
    )
    plane_y = jnp.concatenate(
        [plane_y[0:1], plane_y[1:2] * ox2, plane_y[2:8], plane_y[8:9] * not_ox2, plane_y[9:10]],
        axis=0,
    )

    def edges(outside, plane, side, middle):
        inward = line_taps(plane)
        crossing = dot(jnp.concatenate([line_taps(outside), inward], axis=0), side)
        near = crossing[0 : 8 * DEEP] + dot(inward, middle)
        return own_half(near, ozf), own_half(crossing[8 * DEEP :], ozf)

    near_x, next_x = edges(line[0:10], plane_x, w2x[...], w2[3:6].reshape(3 * C, 3 * C))
    near_y, next_y = edges(without_corner(line[10:20]), plane_y, w2y[...], w2m[...])
    add(block8, near_x, near_y, 0)
    add(block8, next_x, next_y, 1)
    split_rows(halves, m8[...] * silu(block8[...]))

    stacked = jnp.concatenate([corner_rows(halves, *group) for group in groups], axis=1)
    total = dot(stacked.astype(BF16), w3[...].reshape(8 * C, 2 * C)) + last_bias[...]
    mine[0:64] = jnp.where(count > 0.5, total, 0.0).astype(BF16)

    last = pltpu.make_async_remote_copy(
        src_ref=mine,
        dst_ref=arrived,
        send_sem=last_send,
        recv_sem=last_recv,
        device_id=(i, above),
        device_id_type=MESH,
    )
    last.start()
    for copy, exists, _ in sent:
        pl.when(exists)(copy.wait_send)
    last.wait()


def place(mine, arrived, out, zero, row_sem):
    zero[...] = jnp.zeros_like(zero)
    heres = [held[64:80].astype(F32)[0, 0] for held in (mine, arrived)]
    rows = []
    for row in range(16):
        here = heres[row // 8] == float(row)
        held = (mine, arrived)[row // 8]
        piece = pltpu.make_async_copy(held.at[0:64], out.at[row], row_sem.at[row])
        blank = pltpu.make_async_copy(zero, out.at[row], row_sem.at[row])
        pl.when(here)(piece.start)
        pl.when(jnp.logical_not(here))(blank.start)
        rows.append(blank)
    for copy in rows:
        copy.wait()


def per_device(
    n_gx,
    n_gy,
    channel_activations,
    filled_flags,
    cube_locations,
    holder_flag,
    first_kernel_matrices,
    first_offset_vector,
    second_kernel_matrices,
    second_offset_vector,
    reduction_kernel_matrices,
    reduction_offset_vector,
):
    vmem = pl.BlockSpec(memory_space=pltpu.VMEM)
    hbm = pl.BlockSpec(memory_space=pltpu.HBM)
    dma = pltpu.SemaphoreType.DMA
    limit = 56 * 1024 * 1024
    mine, arrived = pl.pallas_call(
        functools.partial(kernel, n_gx, n_gy),
        out_shape=(
            pltpu.VMEM((PIECE_ROWS, 256), BF16),
            pltpu.VMEM((PIECE_ROWS, 256), BF16),
        ),
        in_specs=[hbm, pl.BlockSpec(memory_space=pltpu.SMEM)] + [hbm] * 8,
        out_specs=(vmem, vmem),
        scratch_shapes=[
            pltpu.VMEM((1, 3), jnp.int32),
            pltpu.VMEM((1, 512), jnp.int32),
            pltpu.VMEM((1, C), F32),
            pltpu.VMEM((1, C), F32),
            pltpu.VMEM((1, 2 * C), F32),
            pltpu.VMEM((512, C), BF16),
            pltpu.VMEM((9, C, 3 * C), BF16),
            pltpu.VMEM((9, C, 3 * C), BF16),
            pltpu.VMEM((8, C, 2 * C), BF16),
            pltpu.VMEM((8, 8, 8, C), F32),
            pltpu.VMEM((8, 8, 8, C), F32),
            pltpu.VMEM((8, 8, 8, C), F32),
            pltpu.VMEM((8, 8, 8, C), F32),
            pltpu.VMEM((8, 2, 32, C), F32),
            pltpu.VMEM((6, 10, DEEP, C), BF16),
            pltpu.VMEM((12, 12, DEEP, C), BF16),
            pltpu.VMEM((10, 10, DEEP, C), BF16),
            pltpu.VMEM((3 * C, 3 * C), BF16),
            pltpu.VMEM((3 * C, 3 * C), BF16),
            pltpu.VMEM((3 * C, 3 * C), BF16),
            pltpu.VMEM((3 * C, 3 * C), BF16),
            pltpu.VMEM((3 * C, 3 * C), BF16),
            pltpu.VMEM((4, SIDE_ROWS, C), BF16),
            pltpu.VMEM((4, SIDE_ROWS, C), BF16),
            pltpu.VMEM((4, CORNER_ROWS, C), BF16),
            pltpu.VMEM((4, CORNER_ROWS, C), BF16),
            dma((5,)),
            dma((8,)),
            dma((4,)),
            dma((4,)),
            dma((4,)),
            dma((4,)),
            dma,
            dma,
        ],
        compiler_params=pltpu.CompilerParams(
            collective_id=0, has_side_effects=True, vmem_limit_bytes=limit
        ),
    )(
        cube_locations.reshape(1, 3),
        holder_flag,
        filled_flags,
        first_offset_vector.reshape(1, C),
        second_offset_vector.reshape(1, C),
        reduction_offset_vector.reshape(1, 2 * C),
        channel_activations,
        first_kernel_matrices.reshape(9, 3, C, C),
        second_kernel_matrices.reshape(9, 3, C, C),
        reduction_kernel_matrices,
    )
    return pl.pallas_call(
        place,
        out_shape=jax.ShapeDtypeStruct((16, 64, 256), BF16),
        in_specs=[vmem] * 2,
        out_specs=hbm,
        scratch_shapes=[
            pltpu.VMEM((64, 2 * C), BF16),
            dma((16,)),
        ],
        compiler_params=pltpu.CompilerParams(vmem_limit_bytes=4 * 1024 * 1024),
    )(mine, arrived)


def solution(mesh):
    return jax.shard_map(
        functools.partial(per_device, mesh.shape["gx"], mesh.shape["gy"]),
        mesh=mesh,
        in_specs=(
            P(("gx", "gy"), None, None),
            P(("gx", "gy"), None),
            P(None, ("gx", "gy")),
            P("gx", "gy"),
            P(),
            P(),
            P(),
            P(),
            P(),
            P(),
        ),
        out_specs=P(("gx", "gy"), None, None),
        check_vma=False,
    )
```

```python
import functools

import jax
import jax.numpy as jnp
from jax import lax
from jax.experimental import pallas as pl
from jax.experimental.pallas import tpu as pltpu
from jax.sharding import PartitionSpec as P

MESH = pl.DeviceIdType.MESH
F32 = jnp.float32
BF16 = jnp.bfloat16
C = 128
DEEP = 16
SIDE_ROWS = 144
CORNER_ROWS = 48


def silu(s):
    return 0.5 * s * (1.0 + jnp.tanh(0.5 * s))


def number(condition):
    return jnp.where(condition, 1.0, 0.0).astype(F32)


def along_z(products, deep):
    count = products.shape[0] // deep
    low, mid, high = (products[:, k * C : (k + 1) * C].reshape(count, deep, C) for k in range(3))
    z = lax.broadcasted_iota(jnp.int32, (count, deep, C), 1)
    low = jnp.where(z == 0, 0.0, pltpu.roll(low, 1, 1))
    high = jnp.where(z == deep - 1, 0.0, pltpu.roll(high, deep - 1, 1))
    return mid + low + high


def pack(target, value):
    zero = jnp.zeros((1, 8, 8, C), F32)
    upper = jnp.concatenate([zero, value[0:5]], axis=0)
    lower = jnp.concatenate([value[3:8], zero], axis=0)
    target[:, 1:9] = jnp.concatenate([upper, lower], axis=2).astype(BF16)


def own_conv(tiles, weight):
    taps = [tiles[p : p + 4, q : q + 8].reshape(512, C) for p in range(3) for q in range(3)]
    products = jnp.dot(
        jnp.concatenate(taps, axis=1),
        weight[...].reshape(9 * C, 3 * C),
        preferred_element_type=F32,
    )
    total = along_z(products, 8).reshape(4, 8, 2, 8, C)
    return jnp.concatenate([total[:, :, 0], total[:, :, 1]], axis=0)


def line_taps(line):
    return jnp.concatenate([line[k : k + 8].reshape(8 * DEEP, C) for k in range(3)], axis=1)


def own_half(products, ozf):
    total = along_z(products, DEEP)
    return total[:, 0:8] * (1.0 - ozf) + total[:, 8:16] * ozf


def dot(a, b):
    return jnp.dot(a, b, preferred_element_type=F32)


def split_rows(target, value):
    value = value.reshape(8, 4, 2, 8, C)
    for b in range(2):
        target[:, b] = value[:, :, b].reshape(8, 32, C)


def corner_rows(source, a, b, k):
    return jnp.concatenate(
        [source[2 * u + a, b, pl.ds(k, 16, stride=2), :] for u in range(4)], axis=0
    )


def kernel(
    n_gx,
    n_gy,
    location_at,
    holder,
    flags_at,
    first_bias_at,
    second_bias_at,
    last_bias_at,
    features,
    first_weight,
    second_weight,
    last_weight,
    coarse,
    mine,
    arrived,
    code_out,
    code_in,
    location,
    flags,
    first_bias,
    second_bias,
    last_bias,
    cells,
    w1,
    w2,
    w3,
    s8,
    m8,
    total8,
    block8,
    halves,
    tiles,
    field,
    full,
    w1x,
    w1y,
    w2x,
    w2y,
    w2m,
    side_out,
    side_in,
    corner_out,
    corner_in,
    small_sem,
    local_sem,
    side_send,
    side_recv,
    corner_send,
    corner_recv,
    code_send,
    code_recv,
    last_send,
    last_recv,
):
    i = lax.axis_index("gx")
    j = lax.axis_index("gy")
    above = lax.rem(j + 1, n_gy)
    sides = ((i - 1, j), (i + 1, j), (i, j - 1), (i, j + 1))
    corners = ((i - 1, j - 1), (i - 1, j + 1), (i + 1, j - 1), (i + 1, j + 1))
    there = (i > 0, i < n_gx - 1, j > 0, j < n_gy - 1)
    inside = tuple(number(t) for t in there)
    corner_there = tuple(there[a] & there[2 + b] for a in range(2) for b in range(2))

    barrier = pltpu.get_barrier_semaphore()

    def greet(device):
        pl.semaphore_signal(barrier, inc=1, device_id=device, device_id_type=MESH)

    for device, exists in zip(corners + sides, corner_there + there):
        pl.when(exists)(functools.partial(greet, device))
    pl.when(j == 0)(functools.partial(greet, (i, n_gy - 1)))

    copies = [pltpu.make_async_copy(features.at[0], cells, local_sem.at[0])]
    for k in range(3):
        copies.append(
            pltpu.make_async_copy(
                first_weight.at[:, k], w1.at[:, :, pl.ds(k * C, C)], local_sem.at[1 + k]
            )
        )
    for k in range(3):
        copies.append(
            pltpu.make_async_copy(
                second_weight.at[:, k], w2.at[:, :, pl.ds(k * C, C)], local_sem.at[4 + k]
            )
        )
    copies.append(pltpu.make_async_copy(last_weight, w3, local_sem.at[7]))
    small = [
        pltpu.make_async_copy(source, target, small_sem.at[k])
        for k, (source, target) in enumerate(
            (
                (location_at, location),
                (flags_at, flags),
                (first_bias_at, first_bias),
                (second_bias_at, second_bias),
                (last_bias_at, last_bias),
            )
        )
    ]
    for copy in small + copies:
        copy.start()
    for copy in small[0:2]:
        copy.wait()

    octant = (location[...] & 1).astype(F32)
    oxf, oyf, ozf = (jnp.broadcast_to(octant[:, k : k + 1], (8, C)) for k in range(3))
    code = oxf * 4.0 + oyf * 2.0 + ozf + 8.0 * holder[0, 0].astype(F32)

    r = lax.broadcasted_iota(jnp.int32, (C, C), 0)
    c = lax.broadcasted_iota(jnp.int32, (C, C), 1)
    ones = jnp.ones((C, C), BF16)
    for k in range(4):
        line = jnp.broadcast_to(flags[:, k * C : (k + 1) * C].astype(F32), (C, C))
        diagonal = jnp.where(r == c, line, 0.0).astype(BF16)
        m8[pl.ds(2 * k, 2)] = jnp.dot(diagonal, ones, preferred_element_type=F32).reshape(
            2, 8, 8, C
        )

    copies[0].wait()
    s8[...] = cells[...].astype(F32).reshape(8, 8, 8, C) * m8[...]

    lane = lax.broadcasted_iota(jnp.int32, (8, C), 1)

    def in_lanes(columns):
        return sum(jnp.where(lane == c, columns[c], 0.0) for c in range(8))

    code_out[...] = jnp.concatenate([code, code], axis=0).astype(BF16)
    for k in range(4):
        n, f = (0, 0) if k % 2 == 0 else (7, 6)
        value = s8[f : f + 2] if k < 2 else s8[:, f : f + 2]
        near = m8[n] if k < 2 else m8[:, n]
        side_out[k, 0:128] = value.reshape(128, C).astype(BF16)
        side_out[k, 128:144] = jnp.concatenate([in_lanes(near), code], axis=0).astype(BF16)
    for a in range(2):
        for b in range(2):
            near = m8[7 * a, 7 * b]
            corner_out[2 * a + b, 0:32] = (
                s8[6 * a : 6 * a + 2, 6 * b : 6 * b + 2].reshape(32, C).astype(BF16)
            )
            corner_out[2 * a + b, 32:48] = jnp.concatenate(
                [near, code], axis=0
            ).astype(BF16)

    ways = [there[k].astype(jnp.int32) for k in range(4)]
    greeted = (1 + ways[0] + ways[1]) * (1 + ways[2] + ways[3]) - 1
    pl.semaphore_wait(barrier, greeted + (j == n_gy - 1).astype(jnp.int32))
    sent = []
    for k, device in enumerate(corners):
        copy = pltpu.make_async_remote_copy(
            src_ref=corner_out.at[k],
            dst_ref=corner_in.at[3 - k],
            send_sem=corner_send.at[k],
            recv_sem=corner_recv.at[3 - k],
            device_id=device,
            device_id_type=MESH,
        )
        sent.append((copy, corner_there[k], corner_there[3 - k]))
    for k, device in enumerate(sides):
        copy = pltpu.make_async_remote_copy(
            src_ref=side_out.at[k],
            dst_ref=side_in.at[k ^ 1],
            send_sem=side_send.at[k],
            recv_sem=side_recv.at[k ^ 1],
            device_id=device,
            device_id_type=MESH,
        )
        sent.append((copy, there[k], there[k ^ 1]))
    for k in (3, 1, 5, 4, 7, 2, 0, 6):
        copy, exists, _ = sent[k]
        pl.when(exists)(copy.start)
    tell = pltpu.make_async_remote_copy(
        src_ref=code_out,
        dst_ref=code_in,
        send_sem=code_send,
        recv_sem=code_recv,
        device_id=(i, above),
        device_id_type=MESH,
    )
    tell.start()

    def clear(ref, k):
        ref[k] = jnp.zeros(ref.shape[1:], BF16)

    for k in range(4):
        pl.when(jnp.logical_not(there[k]))(functools.partial(clear, side_in, k))
        pl.when(jnp.logical_not(corner_there[k]))(functools.partial(clear, corner_in, k))

    ox2, oy2 = (jnp.concatenate([o, o], axis=0).astype(BF16) for o in (oxf, oyf))
    not_ox2, not_oy2 = (
        jnp.concatenate([1.0 - o, 1.0 - o], axis=0).astype(BF16) for o in (oxf, oyf)
    )
    field[2:10, 2:10] = jnp.concatenate([s8[...] * (1.0 - ozf), s8[...] * ozf], axis=2).astype(BF16)
    full[1:9, 1:9] = jnp.concatenate([m8[...] * (1.0 - ozf), m8[...] * ozf], axis=2).astype(BF16)
    tiles[:, 0] = jnp.zeros((6, DEEP, C), BF16)
    tiles[:, 9] = jnp.zeros((6, DEEP, C), BF16)
    pack(tiles, s8[...])

    def edge_weights(weight, along_x, along_y):
        for k in range(3):
            for r in range(3):
                rows, columns = slice(k * C, (k + 1) * C), slice(r * C, (r + 1) * C)
                for target, a, b, side, other in (
                    (along_x, k, 6 + k, not_ox2, ox2),
                    (along_y, 3 * k, 3 * k + 2, not_oy2, oy2),
                ):
                    first = weight[a, :, columns].reshape(8, DEEP, C) * side
                    second = weight[b, :, columns].reshape(8, DEEP, C) * other
                    target[rows, columns] = (first + second).reshape(C, C)

    for copy in small[2:]:
        copy.wait()
    bias1 = first_bias[...]
    bias2 = second_bias[...]
    for copy in copies[1:4]:
        copy.wait()
    total8[...] = own_conv(tiles, w1) + bias1
    edge_weights(w1, w1x, w1y)
    for copy in copies[4:]:
        copy.wait()
    edge_weights(w2, w2x, w2y)
    for k in range(3):
        w2m[k * C : (k + 1) * C] = w2[3 * k + 1]

    x = lax.broadcasted_iota(jnp.int32, (8, 8, 8, C), 0)
    y = lax.broadcasted_iota(jnp.int32, (8, 8, 8, C), 1)
    inner_x = jnp.where(x == 0, oxf, jnp.where(x == 7, 1.0 - oxf, 1.0))
    inner_y = jnp.where(y == 0, oyf, jnp.where(y == 7, 1.0 - oyf, 1.0))
    pack(tiles, m8[...] * inner_x * inner_y * silu(total8[...]))
    block8[...] = own_conv(tiles, w2) + bias2 + s8[...]

    groups = [(a, b, k) for a in range(2) for b in range(2) for k in range(2)]
    split_rows(halves, m8[...])
    count = sum(corner_rows(halves, *group) for group in groups)
    count = jnp.concatenate([count, count], axis=1)

    for copy, _, exists in sent[4:]:
        pl.when(exists)(copy.wait_recv)

    def decode(tag):
        nx = number(tag >= 4.0)
        rest = tag - 4.0 * nx
        ny = number(rest >= 2.0)
        nz = rest - 2.0 * ny
        return nx, ny, nz

    def placed(value, gate, nz):
        return jnp.concatenate([value * (gate * (1.0 - nz)), value * (gate * nz)], axis=-2)

    facing = (1.0 - oxf, oxf, 1.0 - oyf, oyf)
    lower = [None] * 4
    upper = [None] * 4
    for k in range(4):
        tail = side_in[k, 128:144].astype(F32)
        got = tail[8:16]
        got = got - 8.0 * number(got >= 8.0)
        nx, ny, nz = decode(got)
        across, beside, own = (nx, ny, oyf) if k < 2 else (ny, nx, oxf)
        meets = across if k % 2 == 0 else 1.0 - across
        gate = meets * (inside[k] * facing[k])
        same = gate * (beside * own + (1.0 - beside) * (1.0 - own))
        minus = gate * ((1.0 - beside) * own)
        plus = gate * (beside * (1.0 - own))
        flag = jnp.stack([jnp.broadcast_to(tail[0:8, c : c + 1], (8, C)) for c in range(8)])
        if k < 2:
            value = side_in[k, 0:128].astype(F32).reshape(2, 8, 8, C)
            x = 0 if k == 0 else 10
            field[x : x + 2, 2:10] = placed(value, same, nz).astype(BF16)
            full[0 if k == 0 else 9, 1:9] = placed(flag, same, nz).astype(BF16)
            lower[k] = (placed(value[:, 6:8], minus, nz), placed(flag[7], minus, nz))
            upper[k] = (placed(value[:, 0:2], plus, nz), placed(flag[0], plus, nz))
        else:
            value = side_in[k, 0:128].astype(F32).reshape(8, 2, 8, C)
            y = 0 if k == 2 else 10
            field[2:10, y : y + 2] = placed(value, same, nz).astype(BF16)
            full[1:9, 0 if k == 2 else 9] = placed(flag, same, nz).astype(BF16)
            lower[k] = (placed(value[6:8], minus, nz), placed(flag[7], minus, nz))
            upper[k] = (placed(value[0:2], plus, nz), placed(flag[0], plus, nz))
    for copy, _, exists in sent[:4]:
        pl.when(exists)(copy.wait_recv)
    for a in range(2):
        for b in range(2):
            k = 2 * a + b
            tail = corner_in[k, 32:48].astype(F32)
            got = tail[8:16]
            got = got - 8.0 * number(got >= 8.0)
            nx, ny, nz = decode(got)
            gate = (nx if a == 0 else 1.0 - nx) * (ny if b == 0 else 1.0 - ny)
            gate = gate * (inside[a] * inside[2 + b] * facing[a] * facing[2 + b])
            value = corner_in[k, 0:32].astype(F32).reshape(2, 2, 8, C)
            from_x = (lower if b == 0 else upper)[a]
            from_y = (lower if a == 0 else upper)[2 + b]
            x, y = 10 * a, 10 * b
            field[x : x + 2, y : y + 2] = (
                placed(value, gate, nz) + from_x[0] + from_y[0]
            ).astype(BF16)
            full[9 * a, 9 * b] = (placed(tail[0:8], gate, nz) + from_x[1] + from_y[1]).astype(BF16)

    beside_x = field[0:3] * not_ox2 + field[9:12] * ox2
    beside_y = field[:, 0:3] * not_oy2 + field[:, 9:12] * oy2
    stacked = jnp.concatenate(
        [
            jnp.concatenate(
                [
                    beside_x[p, q : q + 10].reshape(10 * DEEP, C),
                    beside_y[p : p + 10, q].reshape(10 * DEEP, C),
                ],
                axis=0,
            )
            for p in range(3)
            for q in range(3)
        ],
        axis=1,
    )
    products = jnp.dot(stacked, w1[...].reshape(9 * C, 3 * C), preferred_element_type=F32)
    flag = jnp.concatenate(
        [full[0] * not_ox2 + full[9] * ox2, full[:, 0] * not_oy2 + full[:, 9] * oy2], axis=0
    ).astype(F32)
    line = (flag * silu(along_z(products, DEEP) + bias1[None])).astype(BF16)

    def without_corner(line):
        return jnp.concatenate([line[0:1] * ox2, line[1:9], line[9:10] * not_ox2], axis=0)

    def add(target, from_x, from_y, near):
        target[near] = target[near] + from_x * (1.0 - oxf)
        target[7 - near] = target[7 - near] + from_x * oxf
        target[:, near] = target[:, near] + from_y * (1.0 - oyf)
        target[:, 7 - near] = target[:, 7 - near] + from_y * oyf

    from_x = own_half(dot(line_taps(beside_x[1, 1:11]), w1x[...]), ozf)
    from_y = own_half(dot(line_taps(without_corner(beside_y[1:11, 1])), w1y[...]), ozf)
    add(total8, from_x, from_y, 0)

    def edge_line(total, flag):
        value = flag * silu(total)
        value = jnp.concatenate([value * (1.0 - ozf), value * ozf], axis=1).astype(BF16)
        zero = jnp.zeros((1, DEEP, C), BF16)
        return jnp.concatenate([zero, value, zero], axis=0)

    plane_x = edge_line(
        total8[0] * (1.0 - oxf) + total8[7] * oxf, m8[0] * (1.0 - oxf) + m8[7] * oxf
    )
    plane_y = edge_line(
        total8[:, 0] * (1.0 - oyf) + total8[:, 7] * oyf, m8[:, 0] * (1.0 - oyf) + m8[:, 7] * oyf
    )
    plane_y = jnp.concatenate(
        [plane_y[0:1], plane_y[1:2] * ox2, plane_y[2:8], plane_y[8:9] * not_ox2, plane_y[9:10]],
        axis=0,
    )

    def edges(outside, plane, side, middle):
        inward = line_taps(plane)
        crossing = dot(jnp.concatenate([line_taps(outside), inward], axis=0), side)
        near = crossing[0 : 8 * DEEP] + dot(inward, middle)
        return own_half(near, ozf), own_half(crossing[8 * DEEP :], ozf)

    near_x, next_x = edges(line[0:10], plane_x, w2x[...], w2[3:6].reshape(3 * C, 3 * C))
    near_y, next_y = edges(without_corner(line[10:20]), plane_y, w2y[...], w2m[...])
    add(block8, near_x, near_y, 0)
    add(block8, next_x, next_y, 1)
    split_rows(halves, m8[...] * silu(block8[...]))

    stacked = jnp.concatenate([corner_rows(halves, *group) for group in groups], axis=1)
    total = dot(stacked.astype(BF16), w3[...].reshape(8 * C, 2 * C)) + last_bias[...]
    mine[...] = jnp.where(count > 0.5, total, 0.0).astype(BF16)

    last = pltpu.make_async_remote_copy(
        src_ref=mine,
        dst_ref=arrived,
        send_sem=last_send,
        recv_sem=last_recv,
        device_id=(i, above),
        device_id_type=MESH,
    )
    last.start()

    def put(held, code, first):
        here = jnp.concatenate([jnp.concatenate([code] * 4, axis=0)] * 2, axis=1)
        for row in range(first, first + 8):
            coarse[row] = jnp.where(here == row, held[...], 0.0).astype(BF16)

    put(mine, code_out[...], 0)
    for copy, exists, _ in sent:
        pl.when(exists)(copy.wait_send)
    tell.wait()
    last.wait_send()
    last.wait_recv()
    put(arrived, code_in[...], 8)


def per_device(
    n_gx,
    n_gy,
    channel_activations,
    filled_flags,
    cube_locations,
    holder_flag,
    first_kernel_matrices,
    first_offset_vector,
    second_kernel_matrices,
    second_offset_vector,
    reduction_kernel_matrices,
    reduction_offset_vector,
):
    vmem = pl.BlockSpec(memory_space=pltpu.VMEM)
    hbm = pl.BlockSpec(memory_space=pltpu.HBM)
    dma = pltpu.SemaphoreType.DMA
    limit = 56 * 1024 * 1024
    (coarse,) = pl.pallas_call(
        functools.partial(kernel, n_gx, n_gy),
        out_shape=(
            pltpu.VMEM((16, 64, 256), BF16),
        ),
        in_specs=[hbm, pl.BlockSpec(memory_space=pltpu.SMEM)] + [hbm] * 8,
        out_specs=(vmem,),
        scratch_shapes=[
            pltpu.VMEM((64, 2 * C), BF16),
            pltpu.VMEM((64, 2 * C), BF16),
            pltpu.VMEM((DEEP, C), BF16),
            pltpu.VMEM((DEEP, C), BF16),
            pltpu.VMEM((1, 3), jnp.int32),
            pltpu.VMEM((1, 512), jnp.int32),
            pltpu.VMEM((1, C), F32),
            pltpu.VMEM((1, C), F32),
            pltpu.VMEM((1, 2 * C), F32),
            pltpu.VMEM((512, C), BF16),
            pltpu.VMEM((9, C, 3 * C), BF16),
            pltpu.VMEM((9, C, 3 * C), BF16),
            pltpu.VMEM((8, C, 2 * C), BF16),
            pltpu.VMEM((8, 8, 8, C), F32),
            pltpu.VMEM((8, 8, 8, C), F32),
            pltpu.VMEM((8, 8, 8, C), F32),
            pltpu.VMEM((8, 8, 8, C), F32),
            pltpu.VMEM((8, 2, 32, C), F32),
            pltpu.VMEM((6, 10, DEEP, C), BF16),
            pltpu.VMEM((12, 12, DEEP, C), BF16),
            pltpu.VMEM((10, 10, DEEP, C), BF16),
            pltpu.VMEM((3 * C, 3 * C), BF16),
            pltpu.VMEM((3 * C, 3 * C), BF16),
            pltpu.VMEM((3 * C, 3 * C), BF16),
            pltpu.VMEM((3 * C, 3 * C), BF16),
            pltpu.VMEM((3 * C, 3 * C), BF16),
            pltpu.VMEM((4, SIDE_ROWS, C), BF16),
            pltpu.VMEM((4, SIDE_ROWS, C), BF16),
            pltpu.VMEM((4, CORNER_ROWS, C), BF16),
            pltpu.VMEM((4, CORNER_ROWS, C), BF16),
            dma((5,)),
            dma((8,)),
            dma((4,)),
            dma((4,)),
            dma((4,)),
            dma((4,)),
            dma,
            dma,
            dma,
            dma,
        ],
        compiler_params=pltpu.CompilerParams(
            collective_id=0, has_side_effects=True, vmem_limit_bytes=limit
        ),
    )(
        cube_locations.reshape(1, 3),
        holder_flag,
        filled_flags,
        first_offset_vector.reshape(1, C),
        second_offset_vector.reshape(1, C),
        reduction_offset_vector.reshape(1, 2 * C),
        channel_activations,
        first_kernel_matrices.reshape(9, 3, C, C),
        second_kernel_matrices.reshape(9, 3, C, C),
        reduction_kernel_matrices,
    )
    return coarse


def solution(mesh):
    return jax.shard_map(
        functools.partial(per_device, mesh.shape["gx"], mesh.shape["gy"]),
        mesh=mesh,
        in_specs=(
            P(("gx", "gy"), None, None),
            P(("gx", "gy"), None),
            P(None, ("gx", "gy")),
            P("gx", "gy"),
            P(),
            P(),
            P(),
            P(),
            P(),
            P(),
        ),
        out_specs=P(("gx", "gy"), None, None),
        check_vma=False,
    )
```

```python
import functools

import jax
import jax.numpy as jnp
from jax import lax
from jax.experimental import pallas as pl
from jax.experimental.pallas import tpu as pltpu
from jax.sharding import PartitionSpec as P

MESH = pl.DeviceIdType.MESH
F32 = jnp.float32
BF16 = jnp.bfloat16
C = 128
DEEP = 16
SIDE_ROWS = 144
CORNER_ROWS = 48


def silu(s):
    return 0.5 * s * (1.0 + jnp.tanh(0.5 * s))


def number(condition):
    return jnp.where(condition, 1.0, 0.0).astype(F32)


def along_z(products, deep):
    count = products.shape[0] // deep
    low, mid, high = (products[:, k * C : (k + 1) * C].reshape(count, deep, C) for k in range(3))
    z = lax.broadcasted_iota(jnp.int32, (count, deep, C), 1)
    low = jnp.where(z == 0, 0.0, pltpu.roll(low, 1, 1))
    high = jnp.where(z == deep - 1, 0.0, pltpu.roll(high, deep - 1, 1))
    return mid + low + high


def pack(target, value):
    zero = jnp.zeros((1, 8, 8, C), F32)
    upper = jnp.concatenate([zero, value[0:5]], axis=0)
    lower = jnp.concatenate([value[3:8], zero], axis=0)
    target[:, 1:9] = jnp.concatenate([upper, lower], axis=2).astype(BF16)


def own_conv(tiles, weight):
    taps = [tiles[p : p + 4, q : q + 8].reshape(512, C) for p in range(3) for q in range(3)]
    products = jnp.dot(
        jnp.concatenate(taps, axis=1),
        weight[...].reshape(9 * C, 3 * C),
        preferred_element_type=F32,
    )
    total = along_z(products, 8).reshape(4, 8, 2, 8, C)
    return jnp.concatenate([total[:, :, 0], total[:, :, 1]], axis=0)


def line_taps(line):
    return jnp.concatenate([line[k : k + 8].reshape(8 * DEEP, C) for k in range(3)], axis=1)


def own_half(products, ozf):
    total = along_z(products, DEEP)
    return total[:, 0:8] * (1.0 - ozf) + total[:, 8:16] * ozf


def dot(a, b):
    return jnp.dot(a, b, preferred_element_type=F32)


def split_rows(target, value):
    value = value.reshape(8, 4, 2, 8, C)
    for b in range(2):
        target[:, b] = value[:, :, b].reshape(8, 32, C)


def corner_rows(source, a, b, k):
    return jnp.concatenate(
        [source[2 * u + a, b, pl.ds(k, 16, stride=2), :] for u in range(4)], axis=0
    )


def faces(cells, oxf, oyf):
    return [cells[a] * (1.0 - oxf) + cells[6 + a] * oxf for a in range(2)] + [
        cells[:, b] * (1.0 - oyf) + cells[:, 6 + b] * oyf for b in range(2)
    ]


def split_faces(target, planes):
    for k, plane in enumerate(planes):
        plane = plane.reshape(4, 2, 8, C)
        for b in range(2):
            target[k, b] = plane[:, b].reshape(32, C)


def face_rows(source, a, b, k):
    return jnp.concatenate(
        [
            source[a, b, pl.ds(k, 16, stride=2), :],
            source[2 + b, a, pl.ds(k, 16, stride=2), :],
        ],
        axis=0,
    )


def merged(inner, outer, code):
    code = code.astype(F32)
    code = code - 8.0 * number(code >= 8.0)
    ox = number(code >= 4.0)
    oy = number(code - 4.0 * ox >= 2.0)
    ox, oy = (jnp.concatenate([o, o], axis=1) for o in (ox, oy))
    v = (lax.broadcasted_iota(jnp.int32, (16, 2 * C), 0) // 4).astype(F32)
    face_x = outer[0:16].astype(F32)
    face_y = outer[16:32].astype(F32)
    blocks = []
    for u in range(4):
        across = jnp.concatenate([face_y[4 * u : 4 * u + 4]] * 4, axis=0)
        block = jnp.where(v == 3.0 * oy, across, inner[16 * u : 16 * u + 16].astype(F32))
        if u in (0, 3):
            block = jnp.where(ox == float(u == 3), face_x, block)
        blocks.append(block)
    return jnp.concatenate(blocks, axis=0)


def kernel(
    n_gx,
    n_gy,
    location_at,
    holder,
    flags_at,
    first_bias_at,
    second_bias_at,
    last_bias_at,
    features,
    first_weight,
    second_weight,
    last_weight,
    coarse,
    mine,
    arrived,
    mine_faces,
    arrived_faces,
    code_out,
    code_in,
    location,
    flags,
    first_bias,
    second_bias,
    last_bias,
    cells,
    w1,
    w2,
    w3,
    s8,
    m8,
    total8,
    block8,
    halves,
    faced,
    tiles,
    field,
    full,
    w1x,
    w1y,
    w2x,
    w2y,
    side_out,
    side_in,
    corner_out,
    corner_in,
    small_sem,
    local_sem,
    side_send,
    side_recv,
    corner_send,
    corner_recv,
    code_send,
    code_recv,
    ahead_send,
    ahead_recv,
    last_send,
    last_recv,
):
    i = lax.axis_index("gx")
    j = lax.axis_index("gy")
    above = lax.rem(j + 1, n_gy)
    sides = ((i - 1, j), (i + 1, j), (i, j - 1), (i, j + 1))
    corners = ((i - 1, j - 1), (i - 1, j + 1), (i + 1, j - 1), (i + 1, j + 1))
    there = (i > 0, i < n_gx - 1, j > 0, j < n_gy - 1)
    inside = tuple(number(t) for t in there)
    corner_there = tuple(there[a] & there[2 + b] for a in range(2) for b in range(2))

    barrier = pltpu.get_barrier_semaphore()

    def greet(device):
        pl.semaphore_signal(barrier, inc=1, device_id=device, device_id_type=MESH)

    for device, exists in zip(corners + sides, corner_there + there):
        pl.when(exists)(functools.partial(greet, device))
    pl.when(j == 0)(functools.partial(greet, (i, n_gy - 1)))

    copies = [pltpu.make_async_copy(features.at[0], cells, local_sem.at[0])]
    for k in range(3):
        copies.append(
            pltpu.make_async_copy(
                first_weight.at[:, k], w1.at[:, :, pl.ds(k * C, C)], local_sem.at[1 + k]
            )
        )
    for k in range(3):
        copies.append(
            pltpu.make_async_copy(
                second_weight.at[:, k], w2.at[:, :, pl.ds(k * C, C)], local_sem.at[4 + k]
            )
        )
    copies.append(pltpu.make_async_copy(last_weight, w3, local_sem.at[7]))
    small = [
        pltpu.make_async_copy(source, target, small_sem.at[k])
        for k, (source, target) in enumerate(
            (
                (location_at, location),
                (flags_at, flags),
                (first_bias_at, first_bias),
                (second_bias_at, second_bias),
                (last_bias_at, last_bias),
            )
        )
    ]
    for copy in small + copies:
        copy.start()
    for copy in small[0:2]:
        copy.wait()

    octant = (location[...] & 1).astype(F32)
    oxf, oyf, ozf = (jnp.broadcast_to(octant[:, k : k + 1], (8, C)) for k in range(3))
    code = oxf * 4.0 + oyf * 2.0 + ozf + 8.0 * holder[0, 0].astype(F32)

    r = lax.broadcasted_iota(jnp.int32, (C, C), 0)
    c = lax.broadcasted_iota(jnp.int32, (C, C), 1)
    ones = jnp.ones((C, C), BF16)
    for k in range(4):
        line = jnp.broadcast_to(flags[:, k * C : (k + 1) * C].astype(F32), (C, C))
        diagonal = jnp.where(r == c, line, 0.0).astype(BF16)
        m8[pl.ds(2 * k, 2)] = jnp.dot(diagonal, ones, preferred_element_type=F32).reshape(
            2, 8, 8, C
        )

    copies[0].wait()
    s8[...] = cells[...].astype(F32).reshape(8, 8, 8, C) * m8[...]

    lane = lax.broadcasted_iota(jnp.int32, (8, C), 1)

    def in_lanes(columns):
        return sum(jnp.where(lane == c, columns[c], 0.0) for c in range(8))

    code_out[...] = jnp.concatenate([code, code], axis=0).astype(BF16)
    for k in range(4):
        n, f = (0, 0) if k % 2 == 0 else (7, 6)
        value = s8[f : f + 2] if k < 2 else s8[:, f : f + 2]
        near = m8[n] if k < 2 else m8[:, n]
        side_out[k, 0:128] = value.reshape(128, C).astype(BF16)
        side_out[k, 128:144] = jnp.concatenate([in_lanes(near), code], axis=0).astype(BF16)
    for a in range(2):
        for b in range(2):
            near = m8[7 * a, 7 * b]
            corner_out[2 * a + b, 0:32] = (
                s8[6 * a : 6 * a + 2, 6 * b : 6 * b + 2].reshape(32, C).astype(BF16)
            )
            corner_out[2 * a + b, 32:48] = jnp.concatenate(
                [near, code], axis=0
            ).astype(BF16)

    ways = [there[k].astype(jnp.int32) for k in range(4)]
    greeted = (1 + ways[0] + ways[1]) * (1 + ways[2] + ways[3]) - 1
    pl.semaphore_wait(barrier, greeted + (j == n_gy - 1).astype(jnp.int32))
    sent = []
    for k, device in enumerate(corners):
        copy = pltpu.make_async_remote_copy(
            src_ref=corner_out.at[k],
            dst_ref=corner_in.at[3 - k],
            send_sem=corner_send.at[k],
            recv_sem=corner_recv.at[3 - k],
            device_id=device,
            device_id_type=MESH,
        )
        sent.append((copy, corner_there[k], corner_there[3 - k]))
    for k, device in enumerate(sides):
        copy = pltpu.make_async_remote_copy(
            src_ref=side_out.at[k],
            dst_ref=side_in.at[k ^ 1],
            send_sem=side_send.at[k],
            recv_sem=side_recv.at[k ^ 1],
            device_id=device,
            device_id_type=MESH,
        )
        sent.append((copy, there[k], there[k ^ 1]))
    for k in (3, 1, 5, 4, 7, 2, 0, 6):
        copy, exists, _ = sent[k]
        pl.when(exists)(copy.start)
    tell = pltpu.make_async_remote_copy(
        src_ref=code_out,
        dst_ref=code_in,
        send_sem=code_send,
        recv_sem=code_recv,
        device_id=(i, above),
        device_id_type=MESH,
    )
    tell.start()

    def clear(ref, k):
        ref[k] = jnp.zeros(ref.shape[1:], BF16)

    for k in range(4):
        pl.when(jnp.logical_not(there[k]))(functools.partial(clear, side_in, k))
        pl.when(jnp.logical_not(corner_there[k]))(functools.partial(clear, corner_in, k))

    ox2, oy2 = (jnp.concatenate([o, o], axis=0).astype(BF16) for o in (oxf, oyf))
    not_ox2, not_oy2 = (
        jnp.concatenate([1.0 - o, 1.0 - o], axis=0).astype(BF16) for o in (oxf, oyf)
    )
    field[2:10, 2:10] = jnp.concatenate([s8[...] * (1.0 - ozf), s8[...] * ozf], axis=2).astype(BF16)
    full[1:9, 1:9] = jnp.concatenate([m8[...] * (1.0 - ozf), m8[...] * ozf], axis=2).astype(BF16)
    tiles[:, 0] = jnp.zeros((6, DEEP, C), BF16)
    tiles[:, 9] = jnp.zeros((6, DEEP, C), BF16)
    pack(tiles, s8[...])

    def edge_weights(weight, along_x, along_y):
        for k in range(3):
            for r in range(3):
                rows, columns = slice(k * C, (k + 1) * C), slice(r * C, (r + 1) * C)
                for target, a, b, side, other in (
                    (along_x, k, 6 + k, not_ox2, ox2),
                    (along_y, 3 * k, 3 * k + 2, not_oy2, oy2),
                ):
                    first = weight[a, :, columns].reshape(8, DEEP, C) * side
                    second = weight[b, :, columns].reshape(8, DEEP, C) * other
                    target[rows, columns] = (first + second).reshape(C, C)

    for copy in small[2:]:
        copy.wait()
    bias1 = first_bias[...]
    bias2 = second_bias[...]
    for copy in copies[1:4]:
        copy.wait()
    total8[...] = own_conv(tiles, w1) + bias1
    edge_weights(w1, w1x, w1y)
    for copy in copies[4:]:
        copy.wait()
    edge_weights(w2, w2x, w2y)
    for k in range(3):
        w2x[k * C : (k + 1) * C, 3 * C :] = w2[3 + k]
        w2y[k * C : (k + 1) * C, 3 * C :] = w2[3 * k + 1]

    x = lax.broadcasted_iota(jnp.int32, (8, 8, 8, C), 0)
    y = lax.broadcasted_iota(jnp.int32, (8, 8, 8, C), 1)
    inner_x = jnp.where(x == 0, oxf, jnp.where(x == 7, 1.0 - oxf, 1.0))
    inner_y = jnp.where(y == 0, oyf, jnp.where(y == 7, 1.0 - oyf, 1.0))
    pack(tiles, m8[...] * inner_x * inner_y * silu(total8[...]))
    block8[...] = own_conv(tiles, w2) + bias2 + s8[...]

    groups = [(a, b, k) for a in range(2) for b in range(2) for k in range(2)]
    split_rows(halves, m8[...])
    count = sum(corner_rows(halves, *group) for group in groups)
    count = jnp.concatenate([count, count], axis=1)
    flags_faces = faces(m8, oxf, oyf)
    split_faces(faced, flags_faces)
    face_count = sum(face_rows(faced, *group) for group in groups)
    face_count = jnp.concatenate([face_count, face_count], axis=1)

    def reduced(rows, counted):
        stacked = jnp.concatenate([rows(*group) for group in groups], axis=1).astype(BF16)
        total = dot(stacked, w3[...].reshape(8 * C, 2 * C)) + last_bias[...]
        return jnp.where(counted > 0.5, total, 0.0).astype(BF16)

    split_rows(halves, m8[...] * silu(block8[...]))
    mine[...] = reduced(functools.partial(corner_rows, halves), count)

    for copy, _, exists in sent[4:]:
        pl.when(exists)(copy.wait_recv)

    def decode(tag):
        nx = number(tag >= 4.0)
        rest = tag - 4.0 * nx
        ny = number(rest >= 2.0)
        nz = rest - 2.0 * ny
        return nx, ny, nz

    def placed(value, gate, nz):
        return jnp.concatenate([value * (gate * (1.0 - nz)), value * (gate * nz)], axis=-2)

    facing = (1.0 - oxf, oxf, 1.0 - oyf, oyf)
    lower = [None] * 4
    upper = [None] * 4
    for k in range(4):
        tail = side_in[k, 128:144].astype(F32)
        got = tail[8:16]
        got = got - 8.0 * number(got >= 8.0)
        nx, ny, nz = decode(got)
        across, beside, own = (nx, ny, oyf) if k < 2 else (ny, nx, oxf)
        meets = across if k % 2 == 0 else 1.0 - across
        gate = meets * (inside[k] * facing[k])
        same = gate * (beside * own + (1.0 - beside) * (1.0 - own))
        minus = gate * ((1.0 - beside) * own)
        plus = gate * (beside * (1.0 - own))
        flag = jnp.stack([jnp.broadcast_to(tail[0:8, c : c + 1], (8, C)) for c in range(8)])
        if k < 2:
            value = side_in[k, 0:128].astype(F32).reshape(2, 8, 8, C)
            x = 0 if k == 0 else 10
            field[x : x + 2, 2:10] = placed(value, same, nz).astype(BF16)
            full[0 if k == 0 else 9, 1:9] = placed(flag, same, nz).astype(BF16)
            lower[k] = (placed(value[:, 6:8], minus, nz), placed(flag[7], minus, nz))
            upper[k] = (placed(value[:, 0:2], plus, nz), placed(flag[0], plus, nz))
        else:
            value = side_in[k, 0:128].astype(F32).reshape(8, 2, 8, C)
            y = 0 if k == 2 else 10
            field[2:10, y : y + 2] = placed(value, same, nz).astype(BF16)
            full[1:9, 0 if k == 2 else 9] = placed(flag, same, nz).astype(BF16)
            lower[k] = (placed(value[6:8], minus, nz), placed(flag[7], minus, nz))
            upper[k] = (placed(value[0:2], plus, nz), placed(flag[0], plus, nz))
    def to_owner(source, target, send_sem, recv_sem):
        copy = pltpu.make_async_remote_copy(
            src_ref=source,
            dst_ref=target,
            send_sem=send_sem,
            recv_sem=recv_sem,
            device_id=(i, above),
            device_id_type=MESH,
        )
        copy.start()
        return copy

    for copy, _, exists in sent[:4]:
        pl.when(exists)(copy.wait_recv)
    ahead = to_owner(mine, arrived, ahead_send, ahead_recv)
    for a in range(2):
        for b in range(2):
            k = 2 * a + b
            tail = corner_in[k, 32:48].astype(F32)
            got = tail[8:16]
            got = got - 8.0 * number(got >= 8.0)
            nx, ny, nz = decode(got)
            gate = (nx if a == 0 else 1.0 - nx) * (ny if b == 0 else 1.0 - ny)
            gate = gate * (inside[a] * inside[2 + b] * facing[a] * facing[2 + b])
            value = corner_in[k, 0:32].astype(F32).reshape(2, 2, 8, C)
            from_x = (lower if b == 0 else upper)[a]
            from_y = (lower if a == 0 else upper)[2 + b]
            x, y = 10 * a, 10 * b
            field[x : x + 2, y : y + 2] = (
                placed(value, gate, nz) + from_x[0] + from_y[0]
            ).astype(BF16)
            full[9 * a, 9 * b] = (placed(tail[0:8], gate, nz) + from_x[1] + from_y[1]).astype(BF16)

    beside_x = field[0:3] * not_ox2 + field[9:12] * ox2
    beside_y = field[:, 0:3] * not_oy2 + field[:, 9:12] * oy2
    stacked = jnp.concatenate(
        [
            jnp.concatenate(
                [
                    beside_x[p, q : q + 10].reshape(10 * DEEP, C),
                    beside_y[p : p + 10, q].reshape(10 * DEEP, C),
                ],
                axis=0,
            )
            for p in range(3)
            for q in range(3)
        ],
        axis=1,
    )
    products = jnp.dot(stacked, w1[...].reshape(9 * C, 3 * C), preferred_element_type=F32)
    flag = jnp.concatenate(
        [full[0] * not_ox2 + full[9] * ox2, full[:, 0] * not_oy2 + full[:, 9] * oy2], axis=0
    ).astype(F32)
    line = (flag * silu(along_z(products, DEEP) + bias1[None])).astype(BF16)

    def without_corner(line):
        return jnp.concatenate([line[0:1] * ox2, line[1:9], line[9:10] * not_ox2], axis=0)

    def add(target, from_x, from_y, near):
        target[near] = target[near] + from_x * (1.0 - oxf)
        target[7 - near] = target[7 - near] + from_x * oxf
        target[:, near] = target[:, near] + from_y * (1.0 - oyf)
        target[:, 7 - near] = target[:, 7 - near] + from_y * oyf

    from_x = own_half(dot(line_taps(beside_x[1, 1:11]), w1x[...]), ozf)
    from_y = own_half(dot(line_taps(without_corner(beside_y[1:11, 1])), w1y[...]), ozf)
    add(total8, from_x, from_y, 0)

    def edge_plane(total, flag):
        zero = jnp.zeros((1, 8, C), F32)
        return jnp.concatenate([zero, flag * silu(total), zero], axis=0)

    plane_x = edge_plane(
        total8[0] * (1.0 - oxf) + total8[7] * oxf, m8[0] * (1.0 - oxf) + m8[7] * oxf
    )
    plane_y = edge_plane(
        total8[:, 0] * (1.0 - oyf) + total8[:, 7] * oyf, m8[:, 0] * (1.0 - oyf) + m8[:, 7] * oyf
    )
    plane_y = jnp.concatenate(
        [
            plane_y[0:1],
            plane_y[1:2] * oxf,
            plane_y[2:8],
            plane_y[8:9] * (1.0 - oxf),
            plane_y[9:10],
        ],
        axis=0,
    )

    def edges(outside, plane, weight):
        inward = jnp.concatenate(
            [plane[k : k + 8].reshape(8 * 8, C).astype(BF16) for k in range(3)], axis=1
        )
        inward = dot(inward, weight[...])
        near = own_half(dot(line_taps(outside), weight[:, 0 : 3 * C]), ozf)
        return near + along_z(inward[:, 3 * C :], 8), along_z(inward[:, 0 : 3 * C], 8)

    near_x, next_x = edges(line[0:10], plane_x, w2x)
    near_y, next_y = edges(without_corner(line[10:20]), plane_y, w2y)
    add(block8, near_x, near_y, 0)
    add(block8, next_x, next_y, 1)
    blocks = faces(block8, oxf, oyf)
    split_faces(faced, [flag * silu(block) for flag, block in zip(flags_faces, blocks)])
    mine_faces[...] = reduced(functools.partial(face_rows, faced), face_count)
    last = to_owner(mine_faces, arrived_faces, last_send, last_recv)

    def put(inner, outer, code, first):
        piece = merged(inner, outer, code)
        here = jnp.concatenate([jnp.concatenate([code] * 4, axis=0)] * 2, axis=1).astype(F32)
        for row in range(first, first + 8):
            coarse[row] = jnp.where(here == float(row), piece, 0.0).astype(BF16)

    put(mine, mine_faces, code_out[...], 0)
    for copy, exists, _ in sent:
        pl.when(exists)(copy.wait_send)
    tell.wait()
    ahead.wait()
    last.wait()
    put(arrived, arrived_faces, code_in[...], 8)


def per_device(
    n_gx,
    n_gy,
    channel_activations,
    filled_flags,
    cube_locations,
    holder_flag,
    first_kernel_matrices,
    first_offset_vector,
    second_kernel_matrices,
    second_offset_vector,
    reduction_kernel_matrices,
    reduction_offset_vector,
):
    vmem = pl.BlockSpec(memory_space=pltpu.VMEM)
    hbm = pl.BlockSpec(memory_space=pltpu.HBM)
    dma = pltpu.SemaphoreType.DMA
    limit = 56 * 1024 * 1024
    (coarse,) = pl.pallas_call(
        functools.partial(kernel, n_gx, n_gy),
        out_shape=(
            pltpu.VMEM((16, 64, 256), BF16),
        ),
        in_specs=[hbm, pl.BlockSpec(memory_space=pltpu.SMEM)] + [hbm] * 8,
        out_specs=(vmem,),
        scratch_shapes=[
            pltpu.VMEM((64, 2 * C), BF16),
            pltpu.VMEM((64, 2 * C), BF16),
            pltpu.VMEM((32, 2 * C), BF16),
            pltpu.VMEM((32, 2 * C), BF16),
            pltpu.VMEM((DEEP, C), BF16),
            pltpu.VMEM((DEEP, C), BF16),
            pltpu.VMEM((1, 3), jnp.int32),
            pltpu.VMEM((1, 512), jnp.int32),
            pltpu.VMEM((1, C), F32),
            pltpu.VMEM((1, C), F32),
            pltpu.VMEM((1, 2 * C), F32),
            pltpu.VMEM((512, C), BF16),
            pltpu.VMEM((9, C, 3 * C), BF16),
            pltpu.VMEM((9, C, 3 * C), BF16),
            pltpu.VMEM((8, C, 2 * C), BF16),
            pltpu.VMEM((8, 8, 8, C), F32),
            pltpu.VMEM((8, 8, 8, C), F32),
            pltpu.VMEM((8, 8, 8, C), F32),
            pltpu.VMEM((8, 8, 8, C), F32),
            pltpu.VMEM((8, 2, 32, C), F32),
            pltpu.VMEM((4, 2, 32, C), F32),
            pltpu.VMEM((6, 10, DEEP, C), BF16),
            pltpu.VMEM((12, 12, DEEP, C), BF16),
            pltpu.VMEM((10, 10, DEEP, C), BF16),
            pltpu.VMEM((3 * C, 3 * C), BF16),
            pltpu.VMEM((3 * C, 3 * C), BF16),
            pltpu.VMEM((3 * C, 6 * C), BF16),
            pltpu.VMEM((3 * C, 6 * C), BF16),
            pltpu.VMEM((4, SIDE_ROWS, C), BF16),
            pltpu.VMEM((4, SIDE_ROWS, C), BF16),
            pltpu.VMEM((4, CORNER_ROWS, C), BF16),
            pltpu.VMEM((4, CORNER_ROWS, C), BF16),
            dma((5,)),
            dma((8,)),
            dma((4,)),
            dma((4,)),
            dma((4,)),
            dma((4,)),
            dma,
            dma,
            dma,
            dma,
            dma,
            dma,
        ],
        compiler_params=pltpu.CompilerParams(
            collective_id=0, has_side_effects=True, vmem_limit_bytes=limit
        ),
    )(
        cube_locations.reshape(1, 3),
        holder_flag,
        filled_flags,
        first_offset_vector.reshape(1, C),
        second_offset_vector.reshape(1, C),
        reduction_offset_vector.reshape(1, 2 * C),
        channel_activations,
        first_kernel_matrices.reshape(9, 3, C, C),
        second_kernel_matrices.reshape(9, 3, C, C),
        reduction_kernel_matrices,
    )
    return coarse


def solution(mesh):
    return jax.shard_map(
        functools.partial(per_device, mesh.shape["gx"], mesh.shape["gy"]),
        mesh=mesh,
        in_specs=(
            P(("gx", "gy"), None, None),
            P(("gx", "gy"), None),
            P(None, ("gx", "gy")),
            P("gx", "gy"),
            P(),
            P(),
            P(),
            P(),
            P(),
            P(),
        ),
        out_specs=P(("gx", "gy"), None, None),
        check_vma=False,
    )
```

```python
import functools

import jax
import jax.numpy as jnp
from jax import lax
from jax.experimental import pallas as pl
from jax.experimental.pallas import tpu as pltpu
from jax.sharding import PartitionSpec as P

MESH = pl.DeviceIdType.MESH
F32 = jnp.float32
BF16 = jnp.bfloat16
C = 128
DEEP = 16
SIDE_ROWS = 144
CORNER_ROWS = 48


def silu(s):
    return 0.5 * s * (1.0 + jnp.tanh(0.5 * s))


def number(condition):
    return jnp.where(condition, 1.0, 0.0).astype(F32)


def along_z(products, deep):
    count = products.shape[0] // deep
    low, mid, high = (products[:, k * C : (k + 1) * C].reshape(count, deep, C) for k in range(3))
    z = lax.broadcasted_iota(jnp.int32, (count, deep, C), 1)
    low = jnp.where(z == 0, 0.0, pltpu.roll(low, 1, 1))
    high = jnp.where(z == deep - 1, 0.0, pltpu.roll(high, deep - 1, 1))
    return mid + low + high


def pack(target, value):
    zero = jnp.zeros((1, 8, 8, C), F32)
    upper = jnp.concatenate([zero, value[0:5]], axis=0)
    lower = jnp.concatenate([value[3:8], zero], axis=0)
    target[:, 1:9] = jnp.concatenate([upper, lower], axis=2).astype(BF16)


def own_conv(tiles, weight):
    taps = [tiles[p : p + 4, q : q + 8].reshape(512, C) for p in range(3) for q in range(3)]
    products = jnp.dot(
        jnp.concatenate(taps, axis=1),
        weight[...].reshape(9 * C, 3 * C),
        preferred_element_type=F32,
    )
    total = along_z(products, 8).reshape(4, 8, 2, 8, C)
    return jnp.concatenate([total[:, :, 0], total[:, :, 1]], axis=0)


def line_taps(line):
    return jnp.concatenate([line[k : k + 8].reshape(8 * DEEP, C) for k in range(3)], axis=1)


def own_half(products, ozf):
    total = along_z(products, DEEP)
    return total[:, 0:8] * (1.0 - ozf) + total[:, 8:16] * ozf


def dot(a, b):
    return jnp.dot(a, b, preferred_element_type=F32)


def split_rows(target, value):
    value = value.reshape(8, 4, 2, 8, C)
    for b in range(2):
        target[:, b] = value[:, :, b].reshape(8, 32, C)


def corner_rows(source, a, b, k):
    return jnp.concatenate(
        [source[2 * u + a, b, pl.ds(k, 16, stride=2), :] for u in range(4)], axis=0
    )


def faces(cells, oxf, oyf):
    return [cells[a] * (1.0 - oxf) + cells[6 + a] * oxf for a in range(2)] + [
        cells[:, b] * (1.0 - oyf) + cells[:, 6 + b] * oyf for b in range(2)
    ]


def split_faces(target, planes):
    for k, plane in enumerate(planes):
        plane = plane.reshape(4, 2, 8, C)
        for b in range(2):
            target[k, b] = plane[:, b].reshape(32, C)


def face_rows(source, a, b, k):
    return jnp.concatenate(
        [
            source[a, b, pl.ds(k, 16, stride=2), :],
            source[2 + b, a, pl.ds(k, 16, stride=2), :],
        ],
        axis=0,
    )


def merged(inner, outer, code):
    code = code.astype(F32)
    code = code - 8.0 * number(code >= 8.0)
    ox = number(code >= 4.0)
    oy = number(code - 4.0 * ox >= 2.0)
    ox, oy = (jnp.concatenate([o, o], axis=1) for o in (ox, oy))
    v = (lax.broadcasted_iota(jnp.int32, (16, 2 * C), 0) // 4).astype(F32)
    face_x = outer[0:16].astype(F32)
    face_y = outer[16:32].astype(F32)
    blocks = []
    for u in range(4):
        across = jnp.concatenate([face_y[4 * u : 4 * u + 4]] * 4, axis=0)
        block = jnp.where(v == 3.0 * oy, across, inner[16 * u : 16 * u + 16].astype(F32))
        if u in (0, 3):
            block = jnp.where(ox == float(u == 3), face_x, block)
        blocks.append(block)
    return jnp.concatenate(blocks, axis=0)


def kernel(
    n_gx,
    n_gy,
    location_at,
    holder,
    flags_at,
    first_bias_at,
    second_bias_at,
    last_bias_at,
    features,
    first_weight,
    second_weight,
    last_weight,
    coarse,
    mine,
    arrived,
    mine_faces,
    arrived_faces,
    code_out,
    code_in,
    location,
    flags,
    first_bias,
    second_bias,
    last_bias,
    cells,
    w1,
    w2,
    w3,
    s8,
    m8,
    total8,
    block8,
    halves,
    faced,
    tiles,
    field,
    full,
    w1x,
    w1y,
    w2x,
    w2y,
    side_out,
    side_in,
    corner_out,
    corner_in,
    small_sem,
    local_sem,
    side_send,
    side_recv,
    corner_send,
    corner_recv,
    code_send,
    code_recv,
    ahead_send,
    ahead_recv,
    last_send,
    last_recv,
):
    i = lax.axis_index("gx")
    j = lax.axis_index("gy")
    above = lax.rem(j + 1, n_gy)
    sides = ((i - 1, j), (i + 1, j), (i, j - 1), (i, j + 1))
    corners = ((i - 1, j - 1), (i - 1, j + 1), (i + 1, j - 1), (i + 1, j + 1))
    there = (i > 0, i < n_gx - 1, j > 0, j < n_gy - 1)
    inside = tuple(number(t) for t in there)
    corner_there = tuple(there[a] & there[2 + b] for a in range(2) for b in range(2))

    barrier = pltpu.get_barrier_semaphore()

    def greet(device):
        pl.semaphore_signal(barrier, inc=1, device_id=device, device_id_type=MESH)

    for device, exists in zip(corners + sides, corner_there + there):
        pl.when(exists)(functools.partial(greet, device))
    pl.when(j == 0)(functools.partial(greet, (i, n_gy - 1)))

    copies = [pltpu.make_async_copy(features.at[0], cells, local_sem.at[0])]
    for k in range(3):
        copies.append(
            pltpu.make_async_copy(
                first_weight.at[:, k], w1.at[:, :, pl.ds(k * C, C)], local_sem.at[1 + k]
            )
        )
    for k in range(3):
        copies.append(
            pltpu.make_async_copy(
                second_weight.at[:, k], w2.at[:, :, pl.ds(k * C, C)], local_sem.at[4 + k]
            )
        )
    copies.append(pltpu.make_async_copy(last_weight, w3, local_sem.at[7]))
    small = [
        pltpu.make_async_copy(source, target, small_sem.at[k])
        for k, (source, target) in enumerate(
            (
                (location_at, location),
                (flags_at, flags),
                (first_bias_at, first_bias),
                (second_bias_at, second_bias),
                (last_bias_at, last_bias),
            )
        )
    ]
    for copy in small + copies:
        copy.start()
    for copy in small[0:2]:
        copy.wait()

    octant = (location[...] & 1).astype(F32)
    oxf, oyf, ozf = (jnp.broadcast_to(octant[:, k : k + 1], (8, C)) for k in range(3))
    code = oxf * 4.0 + oyf * 2.0 + ozf + 8.0 * holder[0, 0].astype(F32)

    r = lax.broadcasted_iota(jnp.int32, (C, C), 0)
    c = lax.broadcasted_iota(jnp.int32, (C, C), 1)
    ones = jnp.ones((C, C), BF16)
    for k in range(4):
        line = jnp.broadcast_to(flags[:, k * C : (k + 1) * C].astype(F32), (C, C))
        diagonal = jnp.where(r == c, line, 0.0).astype(BF16)
        m8[pl.ds(2 * k, 2)] = jnp.dot(diagonal, ones, preferred_element_type=F32).reshape(
            2, 8, 8, C
        )

    copies[0].wait()
    s8[...] = cells[...].astype(F32).reshape(8, 8, 8, C) * m8[...]

    lane = lax.broadcasted_iota(jnp.int32, (8, C), 1)

    def in_lanes(columns):
        return sum(jnp.where(lane == c, columns[c], 0.0) for c in range(8))

    code_out[...] = jnp.concatenate([code, code], axis=0).astype(BF16)
    for k in range(4):
        n, f = (0, 0) if k % 2 == 0 else (7, 6)
        value = s8[f : f + 2] if k < 2 else s8[:, f : f + 2]
        near = m8[n] if k < 2 else m8[:, n]
        side_out[k, 0:128] = value.reshape(128, C).astype(BF16)
        side_out[k, 128:144] = jnp.concatenate([in_lanes(near), code], axis=0).astype(BF16)
    for a in range(2):
        for b in range(2):
            near = m8[7 * a, 7 * b]
            corner_out[2 * a + b, 0:32] = (
                s8[6 * a : 6 * a + 2, 6 * b : 6 * b + 2].reshape(32, C).astype(BF16)
            )
            corner_out[2 * a + b, 32:48] = jnp.concatenate(
                [near, code], axis=0
            ).astype(BF16)

    ways = [there[k].astype(jnp.int32) for k in range(4)]
    greeted = (1 + ways[0] + ways[1]) * (1 + ways[2] + ways[3]) - 1
    pl.semaphore_wait(barrier, greeted + (j == n_gy - 1).astype(jnp.int32))
    sent = []
    for k, device in enumerate(corners):
        copy = pltpu.make_async_remote_copy(
            src_ref=corner_out.at[k],
            dst_ref=corner_in.at[3 - k],
            send_sem=corner_send.at[k],
            recv_sem=corner_recv.at[3 - k],
            device_id=device,
            device_id_type=MESH,
        )
        sent.append((copy, corner_there[k], corner_there[3 - k]))
    for k, device in enumerate(sides):
        copy = pltpu.make_async_remote_copy(
            src_ref=side_out.at[k],
            dst_ref=side_in.at[k ^ 1],
            send_sem=side_send.at[k],
            recv_sem=side_recv.at[k ^ 1],
            device_id=device,
            device_id_type=MESH,
        )
        sent.append((copy, there[k], there[k ^ 1]))
    for k in (3, 1, 5, 4, 7, 2, 0, 6):
        copy, exists, _ = sent[k]
        pl.when(exists)(copy.start)
    tell = pltpu.make_async_remote_copy(
        src_ref=code_out,
        dst_ref=code_in,
        send_sem=code_send,
        recv_sem=code_recv,
        device_id=(i, above),
        device_id_type=MESH,
    )
    tell.start()

    def clear(ref, k):
        ref[k] = jnp.zeros(ref.shape[1:], BF16)

    for k in range(4):
        pl.when(jnp.logical_not(there[k]))(functools.partial(clear, side_in, k))
        pl.when(jnp.logical_not(corner_there[k]))(functools.partial(clear, corner_in, k))

    ox2, oy2 = (jnp.concatenate([o, o], axis=0).astype(BF16) for o in (oxf, oyf))
    not_ox2, not_oy2 = (
        jnp.concatenate([1.0 - o, 1.0 - o], axis=0).astype(BF16) for o in (oxf, oyf)
    )
    field[2:10, 2:10] = jnp.concatenate([s8[...] * (1.0 - ozf), s8[...] * ozf], axis=2).astype(BF16)
    full[1:9, 1:9] = jnp.concatenate([m8[...] * (1.0 - ozf), m8[...] * ozf], axis=2).astype(BF16)
    tiles[:, 0] = jnp.zeros((6, DEEP, C), BF16)
    tiles[:, 9] = jnp.zeros((6, DEEP, C), BF16)
    pack(tiles, s8[...])

    def edge_weights(weight, along_x, along_y):
        for k in range(3):
            for r in range(3):
                rows, columns = slice(k * C, (k + 1) * C), slice(r * C, (r + 1) * C)
                for target, a, b, side, other in (
                    (along_x, k, 6 + k, not_ox2, ox2),
                    (along_y, 3 * k, 3 * k + 2, not_oy2, oy2),
                ):
                    first = weight[a, :, columns].reshape(8, DEEP, C) * side
                    second = weight[b, :, columns].reshape(8, DEEP, C) * other
                    target[rows, columns] = (first + second).reshape(C, C)

    for copy in small[2:]:
        copy.wait()
    bias1 = first_bias[...]
    bias2 = second_bias[...]
    for copy in copies[1:4]:
        copy.wait()
    total8[...] = own_conv(tiles, w1) + bias1
    edge_weights(w1, w1x, w1y)
    for copy in copies[4:]:
        copy.wait()
    edge_weights(w2, w2x, w2y)
    for k in range(3):
        w2x[k * C : (k + 1) * C, 3 * C :] = w2[3 + k]
        w2y[k * C : (k + 1) * C, 3 * C :] = w2[3 * k + 1]

    x = lax.broadcasted_iota(jnp.int32, (8, 8, 8, C), 0)
    y = lax.broadcasted_iota(jnp.int32, (8, 8, 8, C), 1)
    inner_x = jnp.where(x == 0, oxf, jnp.where(x == 7, 1.0 - oxf, 1.0))
    inner_y = jnp.where(y == 0, oyf, jnp.where(y == 7, 1.0 - oyf, 1.0))
    pack(tiles, m8[...] * inner_x * inner_y * silu(total8[...]))
    block8[...] = own_conv(tiles, w2) + bias2 + s8[...]

    groups = [(a, b, k) for a in range(2) for b in range(2) for k in range(2)]
    split_rows(halves, m8[...])
    count = sum(corner_rows(halves, *group) for group in groups)
    count = jnp.concatenate([count, count], axis=1)
    flags_faces = faces(m8, oxf, oyf)
    split_faces(faced, flags_faces)
    face_count = sum(face_rows(faced, *group) for group in groups)
    face_count = jnp.concatenate([face_count, face_count], axis=1)

    def reduced(rows, counted):
        stacked = jnp.concatenate([rows(*group) for group in groups], axis=1).astype(BF16)
        total = dot(stacked, w3[...].reshape(8 * C, 2 * C)) + last_bias[...]
        return jnp.where(counted > 0.5, total, 0.0).astype(BF16)

    split_rows(halves, m8[...] * silu(block8[...]))
    mine[...] = reduced(functools.partial(corner_rows, halves), count)

    for copy, _, exists in sent[4:]:
        pl.when(exists)(copy.wait_recv)

    def decode(tag):
        nx = number(tag >= 4.0)
        rest = tag - 4.0 * nx
        ny = number(rest >= 2.0)
        nz = rest - 2.0 * ny
        return nx, ny, nz

    def placed(value, gate, nz):
        return jnp.concatenate([value * (gate * (1.0 - nz)), value * (gate * nz)], axis=-2)

    facing = (1.0 - oxf, oxf, 1.0 - oyf, oyf)
    lower = [None] * 4
    upper = [None] * 4
    for k in range(4):
        tail = side_in[k, 128:144].astype(F32)
        got = tail[8:16]
        got = got - 8.0 * number(got >= 8.0)
        nx, ny, nz = decode(got)
        across, beside, own = (nx, ny, oyf) if k < 2 else (ny, nx, oxf)
        meets = across if k % 2 == 0 else 1.0 - across
        gate = meets * (inside[k] * facing[k])
        same = gate * (beside * own + (1.0 - beside) * (1.0 - own))
        minus = gate * ((1.0 - beside) * own)
        plus = gate * (beside * (1.0 - own))
        flag = jnp.stack([jnp.broadcast_to(tail[0:8, c : c + 1], (8, C)) for c in range(8)])
        if k < 2:
            value = side_in[k, 0:128].astype(F32).reshape(2, 8, 8, C)
            x = 0 if k == 0 else 10
            field[x : x + 2, 2:10] = placed(value, same, nz).astype(BF16)
            full[0 if k == 0 else 9, 1:9] = placed(flag, same, nz).astype(BF16)
            lower[k] = (placed(value[:, 6:8], minus, nz), placed(flag[7], minus, nz))
            upper[k] = (placed(value[:, 0:2], plus, nz), placed(flag[0], plus, nz))
        else:
            value = side_in[k, 0:128].astype(F32).reshape(8, 2, 8, C)
            y = 0 if k == 2 else 10
            field[2:10, y : y + 2] = placed(value, same, nz).astype(BF16)
            full[1:9, 0 if k == 2 else 9] = placed(flag, same, nz).astype(BF16)
            lower[k] = (placed(value[6:8], minus, nz), placed(flag[7], minus, nz))
            upper[k] = (placed(value[0:2], plus, nz), placed(flag[0], plus, nz))
    def to_owner(source, target, send_sem, recv_sem):
        copy = pltpu.make_async_remote_copy(
            src_ref=source,
            dst_ref=target,
            send_sem=send_sem,
            recv_sem=recv_sem,
            device_id=(i, above),
            device_id_type=MESH,
        )
        copy.start()
        return copy

    for copy, _, exists in sent[:4]:
        pl.when(exists)(copy.wait_recv)
    ahead = to_owner(mine, arrived, ahead_send, ahead_recv)
    for a in range(2):
        for b in range(2):
            k = 2 * a + b
            tail = corner_in[k, 32:48].astype(F32)
            got = tail[8:16]
            got = got - 8.0 * number(got >= 8.0)
            nx, ny, nz = decode(got)
            gate = (nx if a == 0 else 1.0 - nx) * (ny if b == 0 else 1.0 - ny)
            gate = gate * (inside[a] * inside[2 + b] * facing[a] * facing[2 + b])
            value = corner_in[k, 0:32].astype(F32).reshape(2, 2, 8, C)
            from_x = (lower if b == 0 else upper)[a]
            from_y = (lower if a == 0 else upper)[2 + b]
            x, y = 10 * a, 10 * b
            field[x : x + 2, y : y + 2] = (
                placed(value, gate, nz) + from_x[0] + from_y[0]
            ).astype(BF16)
            full[9 * a, 9 * b] = (placed(tail[0:8], gate, nz) + from_x[1] + from_y[1]).astype(BF16)

    beside_x = field[0:3] * not_ox2 + field[9:12] * ox2
    beside_y = field[:, 0:3] * not_oy2 + field[:, 9:12] * oy2
    def without_corner(line):
        return jnp.concatenate([line[0:1] * ox2, line[1:9], line[9:10] * not_ox2], axis=0)

    def add(target, from_x, from_y, near):
        target[near] = target[near] + from_x * (1.0 - oxf)
        target[7 - near] = target[7 - near] + from_x * oxf
        target[:, near] = target[:, near] + from_y * (1.0 - oyf)
        target[:, 7 - near] = target[:, 7 - near] + from_y * oyf

    from_x = own_half(dot(line_taps(beside_x[1, 1:11]), w1x[...]), ozf)
    from_y = own_half(dot(line_taps(without_corner(beside_y[1:11, 1])), w1y[...]), ozf)
    add(total8, from_x, from_y, 0)

    def edge_plane(total, flag):
        zero = jnp.zeros((1, 8, C), F32)
        return jnp.concatenate([zero, flag * silu(total), zero], axis=0)

    plane_x = edge_plane(
        total8[0] * (1.0 - oxf) + total8[7] * oxf, m8[0] * (1.0 - oxf) + m8[7] * oxf
    )
    plane_y = edge_plane(
        total8[:, 0] * (1.0 - oyf) + total8[:, 7] * oyf, m8[:, 0] * (1.0 - oyf) + m8[:, 7] * oyf
    )
    plane_y = jnp.concatenate(
        [
            plane_y[0:1],
            plane_y[1:2] * oxf,
            plane_y[2:8],
            plane_y[8:9] * (1.0 - oxf),
            plane_y[9:10],
        ],
        axis=0,
    )

    stacked = jnp.concatenate(
        [
            jnp.concatenate(
                [
                    beside_x[p, q : q + 10].reshape(10 * DEEP, C),
                    beside_y[p : p + 10, q].reshape(10 * DEEP, C),
                ],
                axis=0,
            )
            for p in range(3)
            for q in range(3)
        ],
        axis=1,
    )
    products = jnp.dot(stacked, w1[...].reshape(9 * C, 3 * C), preferred_element_type=F32)
    flag = jnp.concatenate(
        [full[0] * not_ox2 + full[9] * ox2, full[:, 0] * not_oy2 + full[:, 9] * oy2], axis=0
    ).astype(F32)
    line = (flag * silu(along_z(products, DEEP) + bias1[None])).astype(BF16)

    def edges(outside, plane, weight):
        inward = jnp.concatenate(
            [plane[k : k + 8].reshape(8 * 8, C).astype(BF16) for k in range(3)], axis=1
        )
        inward = dot(inward, weight[...])
        near = own_half(dot(line_taps(outside), weight[:, 0 : 3 * C]), ozf)
        return near + along_z(inward[:, 3 * C :], 8), along_z(inward[:, 0 : 3 * C], 8)

    near_x, next_x = edges(line[0:10], plane_x, w2x)
    near_y, next_y = edges(without_corner(line[10:20]), plane_y, w2y)
    add(block8, near_x, near_y, 0)
    add(block8, next_x, next_y, 1)
    blocks = faces(block8, oxf, oyf)
    split_faces(faced, [flag * silu(block) for flag, block in zip(flags_faces, blocks)])
    mine_faces[...] = reduced(functools.partial(face_rows, faced), face_count)
    last = to_owner(mine_faces, arrived_faces, last_send, last_recv)

    def put(inner, outer, code, first):
        piece = merged(inner, outer, code)
        here = jnp.concatenate([jnp.concatenate([code] * 4, axis=0)] * 2, axis=1).astype(F32)
        for row in range(first, first + 8):
            coarse[row] = jnp.where(here == float(row), piece, 0.0).astype(BF16)

    put(mine, mine_faces, code_out[...], 0)
    for copy, exists, _ in sent:
        pl.when(exists)(copy.wait_send)
    tell.wait()
    ahead.wait()
    last.wait()
    put(arrived, arrived_faces, code_in[...], 8)


def per_device(
    n_gx,
    n_gy,
    channel_activations,
    filled_flags,
    cube_locations,
    holder_flag,
    first_kernel_matrices,
    first_offset_vector,
    second_kernel_matrices,
    second_offset_vector,
    reduction_kernel_matrices,
    reduction_offset_vector,
):
    vmem = pl.BlockSpec(memory_space=pltpu.VMEM)
    hbm = pl.BlockSpec(memory_space=pltpu.HBM)
    dma = pltpu.SemaphoreType.DMA
    limit = 56 * 1024 * 1024
    (coarse,) = pl.pallas_call(
        functools.partial(kernel, n_gx, n_gy),
        out_shape=(
            pltpu.VMEM((16, 64, 256), BF16),
        ),
        in_specs=[hbm, pl.BlockSpec(memory_space=pltpu.SMEM)] + [hbm] * 8,
        out_specs=(vmem,),
        scratch_shapes=[
            pltpu.VMEM((64, 2 * C), BF16),
            pltpu.VMEM((64, 2 * C), BF16),
            pltpu.VMEM((32, 2 * C), BF16),
            pltpu.VMEM((32, 2 * C), BF16),
            pltpu.VMEM((DEEP, C), BF16),
            pltpu.VMEM((DEEP, C), BF16),
            pltpu.VMEM((1, 3), jnp.int32),
            pltpu.VMEM((1, 512), jnp.int32),
            pltpu.VMEM((1, C), F32),
            pltpu.VMEM((1, C), F32),
            pltpu.VMEM((1, 2 * C), F32),
            pltpu.VMEM((512, C), BF16),
            pltpu.VMEM((9, C, 3 * C), BF16),
            pltpu.VMEM((9, C, 3 * C), BF16),
            pltpu.VMEM((8, C, 2 * C), BF16),
            pltpu.VMEM((8, 8, 8, C), F32),
            pltpu.VMEM((8, 8, 8, C), F32),
            pltpu.VMEM((8, 8, 8, C), F32),
            pltpu.VMEM((8, 8, 8, C), F32),
            pltpu.VMEM((8, 2, 32, C), F32),
            pltpu.VMEM((4, 2, 32, C), F32),
            pltpu.VMEM((6, 10, DEEP, C), BF16),
            pltpu.VMEM((12, 12, DEEP, C), BF16),
            pltpu.VMEM((10, 10, DEEP, C), BF16),
            pltpu.VMEM((3 * C, 3 * C), BF16),
            pltpu.VMEM((3 * C, 3 * C), BF16),
            pltpu.VMEM((3 * C, 6 * C), BF16),
            pltpu.VMEM((3 * C, 6 * C), BF16),
            pltpu.VMEM((4, SIDE_ROWS, C), BF16),
            pltpu.VMEM((4, SIDE_ROWS, C), BF16),
            pltpu.VMEM((4, CORNER_ROWS, C), BF16),
            pltpu.VMEM((4, CORNER_ROWS, C), BF16),
            dma((5,)),
            dma((8,)),
            dma((4,)),
            dma((4,)),
            dma((4,)),
            dma((4,)),
            dma,
            dma,
            dma,
            dma,
            dma,
            dma,
        ],
        compiler_params=pltpu.CompilerParams(
            collective_id=0, has_side_effects=True, vmem_limit_bytes=limit
        ),
    )(
        cube_locations.reshape(1, 3),
        holder_flag,
        filled_flags,
        first_offset_vector.reshape(1, C),
        second_offset_vector.reshape(1, C),
        reduction_offset_vector.reshape(1, 2 * C),
        channel_activations,
        first_kernel_matrices.reshape(9, 3, C, C),
        second_kernel_matrices.reshape(9, 3, C, C),
        reduction_kernel_matrices,
    )
    return coarse


def solution(mesh):
    return jax.shard_map(
        functools.partial(per_device, mesh.shape["gx"], mesh.shape["gy"]),
        mesh=mesh,
        in_specs=(
            P(("gx", "gy"), None, None),
            P(("gx", "gy"), None),
            P(None, ("gx", "gy")),
            P("gx", "gy"),
            P(),
            P(),
            P(),
            P(),
            P(),
            P(),
        ),
        out_specs=P(("gx", "gy"), None, None),
        check_vma=False,
    )
```

```python
import functools

import jax
import jax.numpy as jnp
from jax import lax
from jax.experimental import pallas as pl
from jax.experimental.pallas import tpu as pltpu
from jax.sharding import PartitionSpec as P

MESH = pl.DeviceIdType.MESH
F32 = jnp.float32
BF16 = jnp.bfloat16
C = 128
DEEP = 16
SIDE_ROWS = 144
CORNER_ROWS = 48


def silu(s):
    return 0.5 * s * (1.0 + jnp.tanh(0.5 * s))


def number(condition):
    return jnp.where(condition, 1.0, 0.0).astype(F32)


def along_z(products, deep):
    count = products.shape[0] // deep
    low, mid, high = (products[:, k * C : (k + 1) * C].reshape(count, deep, C) for k in range(3))
    z = lax.broadcasted_iota(jnp.int32, (count, deep, C), 1)
    low = jnp.where(z == 0, 0.0, pltpu.roll(low, 1, 1))
    high = jnp.where(z == deep - 1, 0.0, pltpu.roll(high, deep - 1, 1))
    return mid + low + high


def pack(target, value):
    zero = jnp.zeros((1, 8, 8, C), F32)
    upper = jnp.concatenate([zero, value[0:5]], axis=0)
    lower = jnp.concatenate([value[3:8], zero], axis=0)
    target[:, 1:9] = jnp.concatenate([upper, lower], axis=2).astype(BF16)


def own_conv(tiles, weight):
    taps = [tiles[p : p + 4, q : q + 8].reshape(512, C) for p in range(3) for q in range(3)]
    products = jnp.dot(
        jnp.concatenate(taps, axis=1),
        weight[...].reshape(9 * C, 3 * C),
        preferred_element_type=F32,
    )
    total = along_z(products, 8).reshape(4, 8, 2, 8, C)
    return jnp.concatenate([total[:, :, 0], total[:, :, 1]], axis=0)


def line_taps(line):
    return jnp.concatenate([line[k : k + 8].reshape(8 * DEEP, C) for k in range(3)], axis=1)


def own_half(products, ozf):
    total = along_z(products, DEEP)
    return total[:, 0:8] * (1.0 - ozf) + total[:, 8:16] * ozf


def dot(a, b):
    return jnp.dot(a, b, preferred_element_type=F32)


def split_rows(target, value):
    value = value.reshape(8, 4, 2, 8, C)
    for b in range(2):
        target[:, b] = value[:, :, b].reshape(8, 32, C)


def corner_rows(source, a, b, k):
    return jnp.concatenate(
        [source[2 * u + a, b, pl.ds(k, 16, stride=2), :] for u in range(4)], axis=0
    )


def faces(cells, oxf, oyf):
    return [cells[a] * (1.0 - oxf) + cells[6 + a] * oxf for a in range(2)] + [
        cells[:, b] * (1.0 - oyf) + cells[:, 6 + b] * oyf for b in range(2)
    ]


def split_faces(target, planes):
    for k, plane in enumerate(planes):
        plane = plane.reshape(4, 2, 8, C)
        for b in range(2):
            target[k, b] = plane[:, b].reshape(32, C)


def face_rows(source, a, b, k):
    return jnp.concatenate(
        [
            source[a, b, pl.ds(k, 16, stride=2), :],
            source[2 + b, a, pl.ds(k, 16, stride=2), :],
        ],
        axis=0,
    )


def own_masks(code):
    code = code.astype(F32)
    code = jnp.concatenate([code, code], axis=1)
    octant = code - 8.0 * number(code >= 8.0)
    ox = number(octant >= 4.0)
    oy = number(octant - 4.0 * ox >= 2.0)
    v = (lax.broadcasted_iota(jnp.int32, (16, 2 * C), 0) // 4).astype(F32)
    return ox, v == 3.0 * oy, code


def merged(inner, outer, masks):
    ox, on_face_y, _ = masks
    face_x = outer[0:16].astype(F32)
    face_y = outer[16:32].astype(F32)
    blocks = []
    for u in range(4):
        across = jnp.concatenate([face_y[4 * u : 4 * u + 4]] * 4, axis=0)
        block = jnp.where(on_face_y, across, inner[u])
        if u in (0, 3):
            block = jnp.where(ox == float(u == 3), face_x, block)
        blocks.append(block)
    return blocks


def kernel(
    n_gx,
    n_gy,
    location_at,
    holder,
    flags_at,
    first_bias_at,
    second_bias_at,
    last_bias_at,
    features,
    first_weight,
    second_weight,
    last_weight,
    coarse,
    mine,
    arrived,
    mine_faces,
    arrived_faces,
    code_out,
    code_in,
    location,
    flags,
    first_bias,
    second_bias,
    last_bias,
    cells,
    w1,
    w2,
    w3,
    s8,
    m8,
    total8,
    block8,
    halves,
    faced,
    tiles,
    field,
    full,
    w1x,
    w1y,
    w2x,
    w2y,
    side_out,
    side_in,
    corner_out,
    corner_in,
    small_sem,
    local_sem,
    side_send,
    side_recv,
    corner_send,
    corner_recv,
    code_send,
    code_recv,
    ahead_send,
    ahead_recv,
    last_send,
    last_recv,
):
    i = lax.axis_index("gx")
    j = lax.axis_index("gy")
    above = lax.rem(j + 1, n_gy)
    sides = ((i - 1, j), (i + 1, j), (i, j - 1), (i, j + 1))
    corners = ((i - 1, j - 1), (i - 1, j + 1), (i + 1, j - 1), (i + 1, j + 1))
    there = (i > 0, i < n_gx - 1, j > 0, j < n_gy - 1)
    inside = tuple(number(t) for t in there)
    corner_there = tuple(there[a] & there[2 + b] for a in range(2) for b in range(2))

    barrier = pltpu.get_barrier_semaphore()

    def greet(device):
        pl.semaphore_signal(barrier, inc=1, device_id=device, device_id_type=MESH)

    for device, exists in zip(corners + sides, corner_there + there):
        pl.when(exists)(functools.partial(greet, device))
    pl.when(j == 0)(functools.partial(greet, (i, n_gy - 1)))

    copies = [pltpu.make_async_copy(features.at[0], cells, local_sem.at[0])]
    for k in range(3):
        copies.append(
            pltpu.make_async_copy(
                first_weight.at[:, k], w1.at[:, :, pl.ds(k * C, C)], local_sem.at[1 + k]
            )
        )
    for k in range(3):
        copies.append(
            pltpu.make_async_copy(
                second_weight.at[:, k], w2.at[:, :, pl.ds(k * C, C)], local_sem.at[4 + k]
            )
        )
    copies.append(pltpu.make_async_copy(last_weight, w3, local_sem.at[7]))
    small = [
        pltpu.make_async_copy(source, target, small_sem.at[k])
        for k, (source, target) in enumerate(
            (
                (location_at, location),
                (flags_at, flags),
                (first_bias_at, first_bias),
                (second_bias_at, second_bias),
                (last_bias_at, last_bias),
            )
        )
    ]
    for copy in small + copies:
        copy.start()
    for copy in small[0:2]:
        copy.wait()

    octant = (location[...] & 1).astype(F32)
    oxf, oyf, ozf = (jnp.broadcast_to(octant[:, k : k + 1], (8, C)) for k in range(3))
    code = oxf * 4.0 + oyf * 2.0 + ozf + 8.0 * holder[0, 0].astype(F32)

    r = lax.broadcasted_iota(jnp.int32, (C, C), 0)
    c = lax.broadcasted_iota(jnp.int32, (C, C), 1)
    ones = jnp.ones((C, C), BF16)
    for k in range(4):
        line = jnp.broadcast_to(flags[:, k * C : (k + 1) * C].astype(F32), (C, C))
        diagonal = jnp.where(r == c, line, 0.0).astype(BF16)
        m8[pl.ds(2 * k, 2)] = jnp.dot(diagonal, ones, preferred_element_type=F32).reshape(
            2, 8, 8, C
        )

    copies[0].wait()
    s8[...] = cells[...].astype(F32).reshape(8, 8, 8, C) * m8[...]

    lane = lax.broadcasted_iota(jnp.int32, (8, C), 1)

    def in_lanes(columns):
        return sum(jnp.where(lane == c, columns[c], 0.0) for c in range(8))

    code_out[...] = jnp.concatenate([code, code], axis=0).astype(BF16)
    for k in range(4):
        n, f = (0, 0) if k % 2 == 0 else (7, 6)
        value = s8[f : f + 2] if k < 2 else s8[:, f : f + 2]
        near = m8[n] if k < 2 else m8[:, n]
        side_out[k, 0:128] = value.reshape(128, C).astype(BF16)
        side_out[k, 128:144] = jnp.concatenate([in_lanes(near), code], axis=0).astype(BF16)
    for a in range(2):
        for b in range(2):
            near = m8[7 * a, 7 * b]
            corner_out[2 * a + b, 0:32] = (
                s8[6 * a : 6 * a + 2, 6 * b : 6 * b + 2].reshape(32, C).astype(BF16)
            )
            corner_out[2 * a + b, 32:48] = jnp.concatenate(
                [near, code], axis=0
            ).astype(BF16)

    ways = [there[k].astype(jnp.int32) for k in range(4)]
    greeted = (1 + ways[0] + ways[1]) * (1 + ways[2] + ways[3]) - 1
    pl.semaphore_wait(barrier, greeted + (j == n_gy - 1).astype(jnp.int32))
    sent = []
    for k, device in enumerate(corners):
        copy = pltpu.make_async_remote_copy(
            src_ref=corner_out.at[k],
            dst_ref=corner_in.at[3 - k],
            send_sem=corner_send.at[k],
            recv_sem=corner_recv.at[3 - k],
            device_id=device,
            device_id_type=MESH,
        )
        sent.append((copy, corner_there[k], corner_there[3 - k]))
    for k, device in enumerate(sides):
        copy = pltpu.make_async_remote_copy(
            src_ref=side_out.at[k],
            dst_ref=side_in.at[k ^ 1],
            send_sem=side_send.at[k],
            recv_sem=side_recv.at[k ^ 1],
            device_id=device,
            device_id_type=MESH,
        )
        sent.append((copy, there[k], there[k ^ 1]))
    for k in (3, 1, 5, 4, 7, 2, 0, 6):
        copy, exists, _ = sent[k]
        pl.when(exists)(copy.start)
    tell = pltpu.make_async_remote_copy(
        src_ref=code_out,
        dst_ref=code_in,
        send_sem=code_send,
        recv_sem=code_recv,
        device_id=(i, above),
        device_id_type=MESH,
    )
    tell.start()

    def clear(ref, k):
        ref[k] = jnp.zeros(ref.shape[1:], BF16)

    for k in range(4):
        pl.when(jnp.logical_not(there[k]))(functools.partial(clear, side_in, k))
        pl.when(jnp.logical_not(corner_there[k]))(functools.partial(clear, corner_in, k))

    ox2, oy2 = (jnp.concatenate([o, o], axis=0).astype(BF16) for o in (oxf, oyf))
    not_ox2, not_oy2 = (
        jnp.concatenate([1.0 - o, 1.0 - o], axis=0).astype(BF16) for o in (oxf, oyf)
    )
    field[2:10, 2:10] = jnp.concatenate([s8[...] * (1.0 - ozf), s8[...] * ozf], axis=2).astype(BF16)
    full[1:9, 1:9] = jnp.concatenate([m8[...] * (1.0 - ozf), m8[...] * ozf], axis=2).astype(BF16)
    tiles[:, 0] = jnp.zeros((6, DEEP, C), BF16)
    tiles[:, 9] = jnp.zeros((6, DEEP, C), BF16)
    pack(tiles, s8[...])

    def edge_weights(weight, along_x, along_y):
        for k in range(3):
            for r in range(3):
                rows, columns = slice(k * C, (k + 1) * C), slice(r * C, (r + 1) * C)
                for target, a, b, side, other in (
                    (along_x, k, 6 + k, not_ox2, ox2),
                    (along_y, 3 * k, 3 * k + 2, not_oy2, oy2),
                ):
                    first = weight[a, :, columns].reshape(8, DEEP, C) * side
                    second = weight[b, :, columns].reshape(8, DEEP, C) * other
                    target[rows, columns] = (first + second).reshape(C, C)

    for copy in small[2:]:
        copy.wait()
    bias1 = first_bias[...]
    bias2 = second_bias[...]
    for copy in copies[1:4]:
        copy.wait()
    total8[...] = own_conv(tiles, w1) + bias1
    edge_weights(w1, w1x, w1y)
    for copy in copies[4:]:
        copy.wait()
    edge_weights(w2, w2x, w2y)
    for k in range(3):
        w2x[k * C : (k + 1) * C, 3 * C :] = w2[3 + k]
        w2y[k * C : (k + 1) * C, 3 * C :] = w2[3 * k + 1]

    x = lax.broadcasted_iota(jnp.int32, (8, 8, 8, C), 0)
    y = lax.broadcasted_iota(jnp.int32, (8, 8, 8, C), 1)
    inner_x = jnp.where(x == 0, oxf, jnp.where(x == 7, 1.0 - oxf, 1.0))
    inner_y = jnp.where(y == 0, oyf, jnp.where(y == 7, 1.0 - oyf, 1.0))
    pack(tiles, m8[...] * inner_x * inner_y * silu(total8[...]))
    block8[...] = own_conv(tiles, w2) + bias2 + s8[...]

    groups = [(a, b, k) for a in range(2) for b in range(2) for k in range(2)]
    split_rows(halves, m8[...])
    count = sum(corner_rows(halves, *group) for group in groups)
    count = jnp.concatenate([count, count], axis=1)
    flags_faces = faces(m8, oxf, oyf)
    split_faces(faced, flags_faces)
    face_count = sum(face_rows(faced, *group) for group in groups)
    face_count = jnp.concatenate([face_count, face_count], axis=1)

    def reduced(rows, counted):
        stacked = jnp.concatenate([rows(*group) for group in groups], axis=1).astype(BF16)
        total = dot(stacked, w3[...].reshape(8 * C, 2 * C)) + last_bias[...]
        return jnp.where(counted > 0.5, total, 0.0).astype(BF16)

    split_rows(halves, m8[...] * silu(block8[...]))
    mine[...] = reduced(functools.partial(corner_rows, halves), count)

    for copy, _, exists in sent[4:]:
        pl.when(exists)(copy.wait_recv)

    def decode(tag):
        nx = number(tag >= 4.0)
        rest = tag - 4.0 * nx
        ny = number(rest >= 2.0)
        nz = rest - 2.0 * ny
        return nx, ny, nz

    def placed(value, gate, nz):
        return jnp.concatenate([value * (gate * (1.0 - nz)), value * (gate * nz)], axis=-2)

    facing = (1.0 - oxf, oxf, 1.0 - oyf, oyf)
    lower = [None] * 4
    upper = [None] * 4
    for k in range(4):
        tail = side_in[k, 128:144].astype(F32)
        got = tail[8:16]
        got = got - 8.0 * number(got >= 8.0)
        nx, ny, nz = decode(got)
        across, beside, own = (nx, ny, oyf) if k < 2 else (ny, nx, oxf)
        meets = across if k % 2 == 0 else 1.0 - across
        gate = meets * (inside[k] * facing[k])
        same = gate * (beside * own + (1.0 - beside) * (1.0 - own))
        minus = gate * ((1.0 - beside) * own)
        plus = gate * (beside * (1.0 - own))
        flag = jnp.stack([jnp.broadcast_to(tail[0:8, c : c + 1], (8, C)) for c in range(8)])
        if k < 2:
            value = side_in[k, 0:128].astype(F32).reshape(2, 8, 8, C)
            x = 0 if k == 0 else 10
            field[x : x + 2, 2:10] = placed(value, same, nz).astype(BF16)
            full[0 if k == 0 else 9, 1:9] = placed(flag, same, nz).astype(BF16)
            lower[k] = (placed(value[:, 6:8], minus, nz), placed(flag[7], minus, nz))
            upper[k] = (placed(value[:, 0:2], plus, nz), placed(flag[0], plus, nz))
        else:
            value = side_in[k, 0:128].astype(F32).reshape(8, 2, 8, C)
            y = 0 if k == 2 else 10
            field[2:10, y : y + 2] = placed(value, same, nz).astype(BF16)
            full[1:9, 0 if k == 2 else 9] = placed(flag, same, nz).astype(BF16)
            lower[k] = (placed(value[6:8], minus, nz), placed(flag[7], minus, nz))
            upper[k] = (placed(value[0:2], plus, nz), placed(flag[0], plus, nz))
    def to_owner(source, target, send_sem, recv_sem):
        copy = pltpu.make_async_remote_copy(
            src_ref=source,
            dst_ref=target,
            send_sem=send_sem,
            recv_sem=recv_sem,
            device_id=(i, above),
            device_id_type=MESH,
        )
        copy.start()
        return copy

    for copy, _, exists in sent[:4]:
        pl.when(exists)(copy.wait_recv)
    ahead = to_owner(mine, arrived, ahead_send, ahead_recv)
    for a in range(2):
        for b in range(2):
            k = 2 * a + b
            tail = corner_in[k, 32:48].astype(F32)
            got = tail[8:16]
            got = got - 8.0 * number(got >= 8.0)
            nx, ny, nz = decode(got)
            gate = (nx if a == 0 else 1.0 - nx) * (ny if b == 0 else 1.0 - ny)
            gate = gate * (inside[a] * inside[2 + b] * facing[a] * facing[2 + b])
            value = corner_in[k, 0:32].astype(F32).reshape(2, 2, 8, C)
            from_x = (lower if b == 0 else upper)[a]
            from_y = (lower if a == 0 else upper)[2 + b]
            x, y = 10 * a, 10 * b
            field[x : x + 2, y : y + 2] = (
                placed(value, gate, nz) + from_x[0] + from_y[0]
            ).astype(BF16)
            full[9 * a, 9 * b] = (placed(tail[0:8], gate, nz) + from_x[1] + from_y[1]).astype(BF16)

    beside_x = field[0:3] * not_ox2 + field[9:12] * ox2
    beside_y = field[:, 0:3] * not_oy2 + field[:, 9:12] * oy2
    def without_corner(line):
        return jnp.concatenate([line[0:1] * ox2, line[1:9], line[9:10] * not_ox2], axis=0)

    def add(target, from_x, from_y, near):
        target[near] = target[near] + from_x * (1.0 - oxf)
        target[7 - near] = target[7 - near] + from_x * oxf
        target[:, near] = target[:, near] + from_y * (1.0 - oyf)
        target[:, 7 - near] = target[:, 7 - near] + from_y * oyf

    from_x = own_half(dot(line_taps(beside_x[1, 1:11]), w1x[...]), ozf)
    from_y = own_half(dot(line_taps(without_corner(beside_y[1:11, 1])), w1y[...]), ozf)
    add(total8, from_x, from_y, 0)

    def edge_plane(total, flag):
        zero = jnp.zeros((1, 8, C), F32)
        return jnp.concatenate([zero, flag * silu(total), zero], axis=0)

    plane_x = edge_plane(
        total8[0] * (1.0 - oxf) + total8[7] * oxf, m8[0] * (1.0 - oxf) + m8[7] * oxf
    )
    plane_y = edge_plane(
        total8[:, 0] * (1.0 - oyf) + total8[:, 7] * oyf, m8[:, 0] * (1.0 - oyf) + m8[:, 7] * oyf
    )
    plane_y = jnp.concatenate(
        [
            plane_y[0:1],
            plane_y[1:2] * oxf,
            plane_y[2:8],
            plane_y[8:9] * (1.0 - oxf),
            plane_y[9:10],
        ],
        axis=0,
    )

    stacked = jnp.concatenate(
        [
            jnp.concatenate(
                [
                    beside_x[p, q : q + 10].reshape(10 * DEEP, C),
                    beside_y[p : p + 10, q].reshape(10 * DEEP, C),
                ],
                axis=0,
            )
            for p in range(3)
            for q in range(3)
        ],
        axis=1,
    )
    products = jnp.dot(stacked, w1[...].reshape(9 * C, 3 * C), preferred_element_type=F32)
    flag = jnp.concatenate(
        [full[0] * not_ox2 + full[9] * ox2, full[:, 0] * not_oy2 + full[:, 9] * oy2], axis=0
    ).astype(F32)
    line = (flag * silu(along_z(products, DEEP) + bias1[None])).astype(BF16)

    def edges(outside, plane, weight):
        inward = jnp.concatenate(
            [plane[k : k + 8].reshape(8 * 8, C).astype(BF16) for k in range(3)], axis=1
        )
        inward = dot(inward, weight[...])
        near = own_half(dot(line_taps(outside), weight[:, 0 : 3 * C]), ozf)
        return near + along_z(inward[:, 3 * C :], 8), along_z(inward[:, 0 : 3 * C], 8)

    near_x, next_x = edges(line[0:10], plane_x, w2x)
    near_y, next_y = edges(without_corner(line[10:20]), plane_y, w2y)
    add(block8, near_x, near_y, 0)
    add(block8, next_x, next_y, 1)
    blocks = faces(block8, oxf, oyf)
    split_faces(faced, [flag * silu(block) for flag, block in zip(flags_faces, blocks)])
    mine_faces[...] = reduced(functools.partial(face_rows, faced), face_count)
    last = to_owner(mine_faces, arrived_faces, last_send, last_recv)

    def inner_blocks(held):
        return [held[16 * u : 16 * u + 16].astype(F32) for u in range(4)]

    def put(inner, outer, masks, first):
        blocks = merged(inner, outer, masks)
        for row in range(first, first + 8):
            here = masks[2] == float(row)
            for u in range(4):
                coarse[row, 16 * u : 16 * u + 16] = jnp.where(here, blocks[u], 0.0).astype(BF16)

    put(inner_blocks(mine), mine_faces, own_masks(code_out[...]), 0)
    for copy, exists, _ in sent:
        pl.when(exists)(copy.wait_send)
    tell.wait()
    ahead.wait()
    last.wait_send()
    masks = own_masks(code_in[...])
    inner = inner_blocks(arrived)
    last.wait_recv()
    put(inner, arrived_faces, masks, 8)


def per_device(
    n_gx,
    n_gy,
    channel_activations,
    filled_flags,
    cube_locations,
    holder_flag,
    first_kernel_matrices,
    first_offset_vector,
    second_kernel_matrices,
    second_offset_vector,
    reduction_kernel_matrices,
    reduction_offset_vector,
):
    vmem = pl.BlockSpec(memory_space=pltpu.VMEM)
    hbm = pl.BlockSpec(memory_space=pltpu.HBM)
    dma = pltpu.SemaphoreType.DMA
    limit = 56 * 1024 * 1024
    (coarse,) = pl.pallas_call(
        functools.partial(kernel, n_gx, n_gy),
        out_shape=(
            pltpu.VMEM((16, 64, 256), BF16),
        ),
        in_specs=[hbm, pl.BlockSpec(memory_space=pltpu.SMEM)] + [hbm] * 8,
        out_specs=(vmem,),
        scratch_shapes=[
            pltpu.VMEM((64, 2 * C), BF16),
            pltpu.VMEM((64, 2 * C), BF16),
            pltpu.VMEM((32, 2 * C), BF16),
            pltpu.VMEM((32, 2 * C), BF16),
            pltpu.VMEM((DEEP, C), BF16),
            pltpu.VMEM((DEEP, C), BF16),
            pltpu.VMEM((1, 3), jnp.int32),
            pltpu.VMEM((1, 512), jnp.int32),
            pltpu.VMEM((1, C), F32),
            pltpu.VMEM((1, C), F32),
            pltpu.VMEM((1, 2 * C), F32),
            pltpu.VMEM((512, C), BF16),
            pltpu.VMEM((9, C, 3 * C), BF16),
            pltpu.VMEM((9, C, 3 * C), BF16),
            pltpu.VMEM((8, C, 2 * C), BF16),
            pltpu.VMEM((8, 8, 8, C), F32),
            pltpu.VMEM((8, 8, 8, C), F32),
            pltpu.VMEM((8, 8, 8, C), F32),
            pltpu.VMEM((8, 8, 8, C), F32),
            pltpu.VMEM((8, 2, 32, C), F32),
            pltpu.VMEM((4, 2, 32, C), F32),
            pltpu.VMEM((6, 10, DEEP, C), BF16),
            pltpu.VMEM((12, 12, DEEP, C), BF16),
            pltpu.VMEM((10, 10, DEEP, C), BF16),
            pltpu.VMEM((3 * C, 3 * C), BF16),
            pltpu.VMEM((3 * C, 3 * C), BF16),
            pltpu.VMEM((3 * C, 6 * C), BF16),
            pltpu.VMEM((3 * C, 6 * C), BF16),
            pltpu.VMEM((4, SIDE_ROWS, C), BF16),
            pltpu.VMEM((4, SIDE_ROWS, C), BF16),
            pltpu.VMEM((4, CORNER_ROWS, C), BF16),
            pltpu.VMEM((4, CORNER_ROWS, C), BF16),
            dma((5,)),
            dma((8,)),
            dma((4,)),
            dma((4,)),
            dma((4,)),
            dma((4,)),
            dma,
            dma,
            dma,
            dma,
            dma,
            dma,
        ],
        compiler_params=pltpu.CompilerParams(
            collective_id=0, has_side_effects=True, vmem_limit_bytes=limit
        ),
    )(
        cube_locations.reshape(1, 3),
        holder_flag,
        filled_flags,
        first_offset_vector.reshape(1, C),
        second_offset_vector.reshape(1, C),
        reduction_offset_vector.reshape(1, 2 * C),
        channel_activations,
        first_kernel_matrices.reshape(9, 3, C, C),
        second_kernel_matrices.reshape(9, 3, C, C),
        reduction_kernel_matrices,
    )
    return coarse


def solution(mesh):
    return jax.shard_map(
        functools.partial(per_device, mesh.shape["gx"], mesh.shape["gy"]),
        mesh=mesh,
        in_specs=(
            P(("gx", "gy"), None, None),
            P(("gx", "gy"), None),
            P(None, ("gx", "gy")),
            P("gx", "gy"),
            P(),
            P(),
            P(),
            P(),
            P(),
            P(),
        ),
        out_specs=P(("gx", "gy"), None, None),
        check_vma=False,
    )
```

```python
import functools

import jax
import jax.numpy as jnp
from jax import lax
from jax.experimental import pallas as pl
from jax.experimental.pallas import tpu as pltpu
from jax.sharding import PartitionSpec as P

MESH = pl.DeviceIdType.MESH
F32 = jnp.float32
BF16 = jnp.bfloat16
C = 128
DEEP = 16
SIDE_ROWS = 144
CORNER_ROWS = 48


def silu(s):
    return 0.5 * s * (1.0 + jnp.tanh(0.5 * s))


def number(condition):
    return jnp.where(condition, 1.0, 0.0).astype(F32)


def along_z(products, deep):
    count = products.shape[0] // deep
    low, mid, high = (products[:, k * C : (k + 1) * C].reshape(count, deep, C) for k in range(3))
    z = lax.broadcasted_iota(jnp.int32, (count, deep, C), 1)
    low = jnp.where(z == 0, 0.0, pltpu.roll(low, 1, 1))
    high = jnp.where(z == deep - 1, 0.0, pltpu.roll(high, deep - 1, 1))
    return mid + low + high


def pack(target, value):
    zero = jnp.zeros((1, 8, 8, C), F32)
    upper = jnp.concatenate([zero, value[0:5]], axis=0)
    lower = jnp.concatenate([value[3:8], zero], axis=0)
    target[:, 1:9] = jnp.concatenate([upper, lower], axis=2).astype(BF16)


def own_conv(tiles, weight):
    taps = [tiles[p : p + 4, q : q + 8].reshape(512, C) for p in range(3) for q in range(3)]
    products = jnp.dot(
        jnp.concatenate(taps, axis=1),
        weight[...].reshape(9 * C, 3 * C),
        preferred_element_type=F32,
    )
    total = along_z(products, 8).reshape(4, 8, 2, 8, C)
    return jnp.concatenate([total[:, :, 0], total[:, :, 1]], axis=0)


def line_taps(line):
    return jnp.concatenate([line[k : k + 8].reshape(8 * DEEP, C) for k in range(3)], axis=1)


def own_half(products, ozf):
    total = along_z(products, DEEP)
    return total[:, 0:8] * (1.0 - ozf) + total[:, 8:16] * ozf


def dot(a, b):
    return jnp.dot(a, b, preferred_element_type=F32)


def split_rows(target, value):
    value = value.reshape(8, 4, 2, 8, C)
    for b in range(2):
        target[:, b] = value[:, :, b].reshape(8, 32, C)


def corner_rows(source, a, b, k):
    return jnp.concatenate(
        [source[2 * u + a, b, pl.ds(k, 16, stride=2), :] for u in range(4)], axis=0
    )


def faces(cells, oxf, oyf):
    return [cells[a] * (1.0 - oxf) + cells[6 + a] * oxf for a in range(2)] + [
        cells[:, b] * (1.0 - oyf) + cells[:, 6 + b] * oyf for b in range(2)
    ]


def split_faces(target, planes):
    for k, plane in enumerate(planes):
        plane = plane.reshape(4, 2, 8, C)
        for b in range(2):
            target[k, b] = plane[:, b].reshape(32, C)


def face_rows(source, a, b, k):
    return jnp.concatenate(
        [
            source[a, b, pl.ds(k, 16, stride=2), :],
            source[2 + b, a, pl.ds(k, 16, stride=2), :],
        ],
        axis=0,
    )


def merged(inner, outer, code):
    code = code.astype(F32)
    code = code - 8.0 * number(code >= 8.0)
    ox = number(code >= 4.0)
    oy = number(code - 4.0 * ox >= 2.0)
    ox, oy = (jnp.concatenate([o, o], axis=1) for o in (ox, oy))
    v = (lax.broadcasted_iota(jnp.int32, (16, 2 * C), 0) // 4).astype(F32)
    face_x = outer[0:16].astype(F32)
    face_y = outer[16:32].astype(F32)
    blocks = []
    for u in range(4):
        across = jnp.concatenate([face_y[4 * u : 4 * u + 4]] * 4, axis=0)
        block = jnp.where(v == 3.0 * oy, across, inner[16 * u : 16 * u + 16].astype(F32))
        if u in (0, 3):
            block = jnp.where(ox == float(u == 3), face_x, block)
        blocks.append(block)
    return jnp.concatenate(blocks, axis=0)


def kernel(
    n_gx,
    n_gy,
    location_at,
    holder,
    flags_at,
    first_bias_at,
    second_bias_at,
    last_bias_at,
    features,
    first_weight,
    second_weight,
    last_weight,
    coarse,
    mine,
    arrived,
    mine_faces,
    arrived_faces,
    code_out,
    code_in,
    location,
    flags,
    first_bias,
    second_bias,
    last_bias,
    cells,
    w1,
    w2,
    w3,
    s8,
    m8,
    total8,
    block8,
    halves,
    faced,
    tiles,
    field,
    full,
    w1x,
    w1y,
    w2x,
    w2y,
    side_out,
    side_in,
    corner_out,
    corner_in,
    small_sem,
    local_sem,
    side_send,
    side_recv,
    corner_send,
    corner_recv,
    code_send,
    code_recv,
    ahead_send,
    ahead_recv,
    last_send,
    last_recv,
):
    i = lax.axis_index("gx")
    j = lax.axis_index("gy")
    above = lax.rem(j + 1, n_gy)
    sides = ((i - 1, j), (i + 1, j), (i, j - 1), (i, j + 1))
    corners = ((i - 1, j - 1), (i - 1, j + 1), (i + 1, j - 1), (i + 1, j + 1))
    there = (i > 0, i < n_gx - 1, j > 0, j < n_gy - 1)
    inside = tuple(number(t) for t in there)
    corner_there = tuple(there[a] & there[2 + b] for a in range(2) for b in range(2))

    barrier = pltpu.get_barrier_semaphore()

    def greet(device):
        pl.semaphore_signal(barrier, inc=1, device_id=device, device_id_type=MESH)

    for device, exists in zip(corners + sides, corner_there + there):
        pl.when(exists)(functools.partial(greet, device))
    pl.when(j == 0)(functools.partial(greet, (i, n_gy - 1)))

    copies = [pltpu.make_async_copy(features.at[0], cells, local_sem.at[0])]
    for k in range(3):
        copies.append(
            pltpu.make_async_copy(
                first_weight.at[:, k], w1.at[:, :, pl.ds(k * C, C)], local_sem.at[1 + k]
            )
        )
    for k in range(3):
        copies.append(
            pltpu.make_async_copy(
                second_weight.at[:, k], w2.at[:, :, pl.ds(k * C, C)], local_sem.at[4 + k]
            )
        )
    copies.append(pltpu.make_async_copy(last_weight, w3, local_sem.at[7]))
    small = [
        pltpu.make_async_copy(source, target, small_sem.at[k])
        for k, (source, target) in enumerate(
            (
                (location_at, location),
                (flags_at, flags),
                (first_bias_at, first_bias),
                (second_bias_at, second_bias),
                (last_bias_at, last_bias),
            )
        )
    ]
    for copy in small + copies:
        copy.start()
    for copy in small[0:2]:
        copy.wait()

    octant = (location[...] & 1).astype(F32)
    oxf, oyf, ozf = (jnp.broadcast_to(octant[:, k : k + 1], (8, C)) for k in range(3))
    code = oxf * 4.0 + oyf * 2.0 + ozf + 8.0 * holder[0, 0].astype(F32)

    r = lax.broadcasted_iota(jnp.int32, (C, C), 0)
    c = lax.broadcasted_iota(jnp.int32, (C, C), 1)
    ones = jnp.ones((C, C), BF16)
    for k in range(4):
        line = jnp.broadcast_to(flags[:, k * C : (k + 1) * C].astype(F32), (C, C))
        diagonal = jnp.where(r == c, line, 0.0).astype(BF16)
        m8[pl.ds(2 * k, 2)] = jnp.dot(diagonal, ones, preferred_element_type=F32).reshape(
            2, 8, 8, C
        )

    copies[0].wait()
    s8[...] = cells[...].astype(F32).reshape(8, 8, 8, C) * m8[...]

    lane = lax.broadcasted_iota(jnp.int32, (8, C), 1)

    def in_lanes(columns):
        return sum(jnp.where(lane == c, columns[c], 0.0) for c in range(8))

    code_out[...] = jnp.concatenate([code, code], axis=0).astype(BF16)
    for k in range(4):
        n, f = (0, 0) if k % 2 == 0 else (7, 6)
        value = s8[f : f + 2] if k < 2 else s8[:, f : f + 2]
        near = m8[n] if k < 2 else m8[:, n]
        side_out[k, 0:128] = value.reshape(128, C).astype(BF16)
        side_out[k, 128:144] = jnp.concatenate([in_lanes(near), code], axis=0).astype(BF16)
    for a in range(2):
        for b in range(2):
            near = m8[7 * a, 7 * b]
            corner_out[2 * a + b, 0:32] = (
                s8[6 * a : 6 * a + 2, 6 * b : 6 * b + 2].reshape(32, C).astype(BF16)
            )
            corner_out[2 * a + b, 32:48] = jnp.concatenate(
                [near, code], axis=0
            ).astype(BF16)

    ways = [there[k].astype(jnp.int32) for k in range(4)]
    greeted = (1 + ways[0] + ways[1]) * (1 + ways[2] + ways[3]) - 1
    pl.semaphore_wait(barrier, greeted + (j == n_gy - 1).astype(jnp.int32))
    sent = []
    for k, device in enumerate(corners):
        copy = pltpu.make_async_remote_copy(
            src_ref=corner_out.at[k],
            dst_ref=corner_in.at[3 - k],
            send_sem=corner_send.at[k],
            recv_sem=corner_recv.at[3 - k],
            device_id=device,
            device_id_type=MESH,
        )
        sent.append((copy, corner_there[k], corner_there[3 - k]))
    for k, device in enumerate(sides):
        copy = pltpu.make_async_remote_copy(
            src_ref=side_out.at[k],
            dst_ref=side_in.at[k ^ 1],
            send_sem=side_send.at[k],
            recv_sem=side_recv.at[k ^ 1],
            device_id=device,
            device_id_type=MESH,
        )
        sent.append((copy, there[k], there[k ^ 1]))
    for k in (3, 1, 5, 4, 7, 2, 0, 6):
        copy, exists, _ = sent[k]
        pl.when(exists)(copy.start)
    tell = pltpu.make_async_remote_copy(
        src_ref=code_out,
        dst_ref=code_in,
        send_sem=code_send,
        recv_sem=code_recv,
        device_id=(i, above),
        device_id_type=MESH,
    )
    tell.start()

    def clear(ref, k):
        ref[k] = jnp.zeros(ref.shape[1:], BF16)

    for k in range(4):
        pl.when(jnp.logical_not(there[k]))(functools.partial(clear, side_in, k))
        pl.when(jnp.logical_not(corner_there[k]))(functools.partial(clear, corner_in, k))

    ox2, oy2 = (jnp.concatenate([o, o], axis=0).astype(BF16) for o in (oxf, oyf))
    not_ox2, not_oy2 = (
        jnp.concatenate([1.0 - o, 1.0 - o], axis=0).astype(BF16) for o in (oxf, oyf)
    )
    field[2:10, 2:10] = jnp.concatenate([s8[...] * (1.0 - ozf), s8[...] * ozf], axis=2).astype(BF16)
    full[1:9, 1:9] = jnp.concatenate([m8[...] * (1.0 - ozf), m8[...] * ozf], axis=2).astype(BF16)
    tiles[:, 0] = jnp.zeros((6, DEEP, C), BF16)
    tiles[:, 9] = jnp.zeros((6, DEEP, C), BF16)
    pack(tiles, s8[...])

    def edge_weights(weight, along_x, along_y):
        for k in range(3):
            for r in range(3):
                rows, columns = slice(k * C, (k + 1) * C), slice(r * C, (r + 1) * C)
                for target, a, b, side, other in (
                    (along_x, k, 6 + k, not_ox2, ox2),
                    (along_y, 3 * k, 3 * k + 2, not_oy2, oy2),
                ):
                    first = weight[a, :, columns].reshape(8, DEEP, C) * side
                    second = weight[b, :, columns].reshape(8, DEEP, C) * other
                    target[rows, columns] = (first + second).reshape(C, C)

    for copy in small[2:]:
        copy.wait()
    bias1 = first_bias[...]
    bias2 = second_bias[...]
    for copy in copies[1:4]:
        copy.wait()
    total8[...] = own_conv(tiles, w1) + bias1
    edge_weights(w1, w1x, w1y)
    for copy in copies[4:]:
        copy.wait()
    edge_weights(w2, w2x, w2y)
    for k in range(3):
        w2x[k * C : (k + 1) * C, 3 * C :] = w2[3 + k]
        w2y[k * C : (k + 1) * C, 3 * C :] = w2[3 * k + 1]

    x = lax.broadcasted_iota(jnp.int32, (8, 8, 8, C), 0)
    y = lax.broadcasted_iota(jnp.int32, (8, 8, 8, C), 1)
    inner_x = jnp.where(x == 0, oxf, jnp.where(x == 7, 1.0 - oxf, 1.0))
    inner_y = jnp.where(y == 0, oyf, jnp.where(y == 7, 1.0 - oyf, 1.0))
    pack(tiles, m8[...] * inner_x * inner_y * silu(total8[...]))
    block8[...] = own_conv(tiles, w2) + bias2 + s8[...]

    groups = [(a, b, k) for a in range(2) for b in range(2) for k in range(2)]
    split_rows(halves, m8[...])
    count = sum(corner_rows(halves, *group) for group in groups)
    count = jnp.concatenate([count, count], axis=1)
    flags_faces = faces(m8, oxf, oyf)
    split_faces(faced, flags_faces)
    face_count = sum(face_rows(faced, *group) for group in groups)
    face_count = jnp.concatenate([face_count, face_count], axis=1)

    def reduced(rows, counted):
        stacked = jnp.concatenate([rows(*group) for group in groups], axis=1).astype(BF16)
        total = dot(stacked, w3[...].reshape(8 * C, 2 * C)) + last_bias[...]
        return jnp.where(counted > 0.5, total, 0.0).astype(BF16)

    split_rows(halves, m8[...] * silu(block8[...]))
    mine[...] = reduced(functools.partial(corner_rows, halves), count)

    for copy, _, exists in sent[4:]:
        pl.when(exists)(copy.wait_recv)

    def decode(tag):
        nx = number(tag >= 4.0)
        rest = tag - 4.0 * nx
        ny = number(rest >= 2.0)
        nz = rest - 2.0 * ny
        return nx, ny, nz

    def placed(value, gate, nz):
        return jnp.concatenate([value * (gate * (1.0 - nz)), value * (gate * nz)], axis=-2)

    facing = (1.0 - oxf, oxf, 1.0 - oyf, oyf)
    lower = [None] * 4
    upper = [None] * 4
    for k in range(4):
        tail = side_in[k, 128:144].astype(F32)
        got = tail[8:16]
        got = got - 8.0 * number(got >= 8.0)
        nx, ny, nz = decode(got)
        across, beside, own = (nx, ny, oyf) if k < 2 else (ny, nx, oxf)
        meets = across if k % 2 == 0 else 1.0 - across
        gate = meets * (inside[k] * facing[k])
        same = gate * (beside * own + (1.0 - beside) * (1.0 - own))
        minus = gate * ((1.0 - beside) * own)
        plus = gate * (beside * (1.0 - own))
        flag = jnp.stack([jnp.broadcast_to(tail[0:8, c : c + 1], (8, C)) for c in range(8)])
        if k < 2:
            value = side_in[k, 0:128].astype(F32).reshape(2, 8, 8, C)
            x = 0 if k == 0 else 10
            field[x : x + 2, 2:10] = placed(value, same, nz).astype(BF16)
            full[0 if k == 0 else 9, 1:9] = placed(flag, same, nz).astype(BF16)
            lower[k] = (placed(value[:, 6:8], minus, nz), placed(flag[7], minus, nz))
            upper[k] = (placed(value[:, 0:2], plus, nz), placed(flag[0], plus, nz))
        else:
            value = side_in[k, 0:128].astype(F32).reshape(8, 2, 8, C)
            y = 0 if k == 2 else 10
            field[2:10, y : y + 2] = placed(value, same, nz).astype(BF16)
            full[1:9, 0 if k == 2 else 9] = placed(flag, same, nz).astype(BF16)
            lower[k] = (placed(value[6:8], minus, nz), placed(flag[7], minus, nz))
            upper[k] = (placed(value[0:2], plus, nz), placed(flag[0], plus, nz))
    def to_owner(source, target, send_sem, recv_sem):
        copy = pltpu.make_async_remote_copy(
            src_ref=source,
            dst_ref=target,
            send_sem=send_sem,
            recv_sem=recv_sem,
            device_id=(i, above),
            device_id_type=MESH,
        )
        copy.start()
        return copy

    ahead = to_owner(mine, arrived, ahead_send, ahead_recv)
    for copy, _, exists in sent[:4]:
        pl.when(exists)(copy.wait_recv)
    for a in range(2):
        for b in range(2):
            k = 2 * a + b
            tail = corner_in[k, 32:48].astype(F32)
            got = tail[8:16]
            got = got - 8.0 * number(got >= 8.0)
            nx, ny, nz = decode(got)
            gate = (nx if a == 0 else 1.0 - nx) * (ny if b == 0 else 1.0 - ny)
            gate = gate * (inside[a] * inside[2 + b] * facing[a] * facing[2 + b])
            value = corner_in[k, 0:32].astype(F32).reshape(2, 2, 8, C)
            from_x = (lower if b == 0 else upper)[a]
            from_y = (lower if a == 0 else upper)[2 + b]
            x, y = 10 * a, 10 * b
            field[x : x + 2, y : y + 2] = (
                placed(value, gate, nz) + from_x[0] + from_y[0]
            ).astype(BF16)
            full[9 * a, 9 * b] = (placed(tail[0:8], gate, nz) + from_x[1] + from_y[1]).astype(BF16)

    beside_x = field[0:3] * not_ox2 + field[9:12] * ox2
    beside_y = field[:, 0:3] * not_oy2 + field[:, 9:12] * oy2
    def without_corner(line):
        return jnp.concatenate([line[0:1] * ox2, line[1:9], line[9:10] * not_ox2], axis=0)

    def add(target, from_x, from_y, near):
        target[near] = target[near] + from_x * (1.0 - oxf)
        target[7 - near] = target[7 - near] + from_x * oxf
        target[:, near] = target[:, near] + from_y * (1.0 - oyf)
        target[:, 7 - near] = target[:, 7 - near] + from_y * oyf

    from_x = own_half(dot(line_taps(beside_x[1, 1:11]), w1x[...]), ozf)
    from_y = own_half(dot(line_taps(without_corner(beside_y[1:11, 1])), w1y[...]), ozf)
    add(total8, from_x, from_y, 0)

    def edge_plane(total, flag):
        zero = jnp.zeros((1, 8, C), F32)
        return jnp.concatenate([zero, flag * silu(total), zero], axis=0)

    plane_x = edge_plane(
        total8[0] * (1.0 - oxf) + total8[7] * oxf, m8[0] * (1.0 - oxf) + m8[7] * oxf
    )
    plane_y = edge_plane(
        total8[:, 0] * (1.0 - oyf) + total8[:, 7] * oyf, m8[:, 0] * (1.0 - oyf) + m8[:, 7] * oyf
    )
    plane_y = jnp.concatenate(
        [
            plane_y[0:1],
            plane_y[1:2] * oxf,
            plane_y[2:8],
            plane_y[8:9] * (1.0 - oxf),
            plane_y[9:10],
        ],
        axis=0,
    )

    def hidden_line(taps, flag):
        products = dot(jnp.concatenate(taps, axis=1), w1[...].reshape(9 * C, 3 * C))
        return (flag.astype(F32) * silu(along_z(products, DEEP) + bias1[None])).astype(BF16)

    steps = [(p, q) for p in range(3) for q in range(3)]
    line_x = hidden_line(
        [beside_x[p, q : q + 10].reshape(10 * DEEP, C) for p, q in steps],
        full[0] * not_ox2 + full[9] * ox2,
    )
    line_y = hidden_line(
        [beside_y[p : p + 10, q].reshape(10 * DEEP, C) for p, q in steps],
        full[:, 0] * not_oy2 + full[:, 9] * oy2,
    )

    def edges(outside, plane, weight):
        inward = jnp.concatenate(
            [plane[k : k + 8].reshape(8 * 8, C).astype(BF16) for k in range(3)], axis=1
        )
        inward = dot(inward, weight[...])
        near = own_half(dot(line_taps(outside), weight[:, 0 : 3 * C]), ozf)
        return near + along_z(inward[:, 3 * C :], 8), along_z(inward[:, 0 : 3 * C], 8)

    near_x, next_x = edges(line_x, plane_x, w2x)
    near_y, next_y = edges(without_corner(line_y), plane_y, w2y)
    add(block8, near_x, near_y, 0)
    add(block8, next_x, next_y, 1)
    blocks = faces(block8, oxf, oyf)
    split_faces(faced, [flag * silu(block) for flag, block in zip(flags_faces, blocks)])
    mine_faces[...] = reduced(functools.partial(face_rows, faced), face_count)
    last = to_owner(mine_faces, arrived_faces, last_send, last_recv)

    def put(inner, outer, code, first):
        piece = merged(inner, outer, code)
        here = jnp.concatenate([jnp.concatenate([code] * 4, axis=0)] * 2, axis=1).astype(F32)
        for row in range(first, first + 8):
            coarse[row] = jnp.where(here == float(row), piece, 0.0).astype(BF16)

    put(mine, mine_faces, code_out[...], 0)
    for copy, exists, _ in sent:
        pl.when(exists)(copy.wait_send)
    tell.wait()
    ahead.wait()
    last.wait()
    put(arrived, arrived_faces, code_in[...], 8)


def per_device(
    n_gx,
    n_gy,
    channel_activations,
    filled_flags,
    cube_locations,
    holder_flag,
    first_kernel_matrices,
    first_offset_vector,
    second_kernel_matrices,
    second_offset_vector,
    reduction_kernel_matrices,
    reduction_offset_vector,
):
    vmem = pl.BlockSpec(memory_space=pltpu.VMEM)
    hbm = pl.BlockSpec(memory_space=pltpu.HBM)
    dma = pltpu.SemaphoreType.DMA
    limit = 56 * 1024 * 1024
    (coarse,) = pl.pallas_call(
        functools.partial(kernel, n_gx, n_gy),
        out_shape=(
            pltpu.VMEM((16, 64, 256), BF16),
        ),
        in_specs=[hbm, pl.BlockSpec(memory_space=pltpu.SMEM)] + [hbm] * 8,
        out_specs=(vmem,),
        scratch_shapes=[
            pltpu.VMEM((64, 2 * C), BF16),
            pltpu.VMEM((64, 2 * C), BF16),
            pltpu.VMEM((32, 2 * C), BF16),
            pltpu.VMEM((32, 2 * C), BF16),
            pltpu.VMEM((DEEP, C), BF16),
            pltpu.VMEM((DEEP, C), BF16),
            pltpu.VMEM((1, 3), jnp.int32),
            pltpu.VMEM((1, 512), jnp.int32),
            pltpu.VMEM((1, C), F32),
            pltpu.VMEM((1, C), F32),
            pltpu.VMEM((1, 2 * C), F32),
            pltpu.VMEM((512, C), BF16),
            pltpu.VMEM((9, C, 3 * C), BF16),
            pltpu.VMEM((9, C, 3 * C), BF16),
            pltpu.VMEM((8, C, 2 * C), BF16),
            pltpu.VMEM((8, 8, 8, C), F32),
            pltpu.VMEM((8, 8, 8, C), F32),
            pltpu.VMEM((8, 8, 8, C), F32),
            pltpu.VMEM((8, 8, 8, C), F32),
            pltpu.VMEM((8, 2, 32, C), F32),
            pltpu.VMEM((4, 2, 32, C), F32),
            pltpu.VMEM((6, 10, DEEP, C), BF16),
            pltpu.VMEM((12, 12, DEEP, C), BF16),
            pltpu.VMEM((10, 10, DEEP, C), BF16),
            pltpu.VMEM((3 * C, 3 * C), BF16),
            pltpu.VMEM((3 * C, 3 * C), BF16),
            pltpu.VMEM((3 * C, 6 * C), BF16),
            pltpu.VMEM((3 * C, 6 * C), BF16),
            pltpu.VMEM((4, SIDE_ROWS, C), BF16),
            pltpu.VMEM((4, SIDE_ROWS, C), BF16),
            pltpu.VMEM((4, CORNER_ROWS, C), BF16),
            pltpu.VMEM((4, CORNER_ROWS, C), BF16),
            dma((5,)),
            dma((8,)),
            dma((4,)),
            dma((4,)),
            dma((4,)),
            dma((4,)),
            dma,
            dma,
            dma,
            dma,
            dma,
            dma,
        ],
        compiler_params=pltpu.CompilerParams(
            collective_id=0, has_side_effects=True, vmem_limit_bytes=limit
        ),
    )(
        cube_locations.reshape(1, 3),
        holder_flag,
        filled_flags,
        first_offset_vector.reshape(1, C),
        second_offset_vector.reshape(1, C),
        reduction_offset_vector.reshape(1, 2 * C),
        channel_activations,
        first_kernel_matrices.reshape(9, 3, C, C),
        second_kernel_matrices.reshape(9, 3, C, C),
        reduction_kernel_matrices,
    )
    return coarse


def solution(mesh):
    return jax.shard_map(
        functools.partial(per_device, mesh.shape["gx"], mesh.shape["gy"]),
        mesh=mesh,
        in_specs=(
            P(("gx", "gy"), None, None),
            P(("gx", "gy"), None),
            P(None, ("gx", "gy")),
            P("gx", "gy"),
            P(),
            P(),
            P(),
            P(),
            P(),
            P(),
        ),
        out_specs=P(("gx", "gy"), None, None),
        check_vma=False,
    )
```
